128 devices in a mesh: frame: 64 (over x_hi, y, z, core), chan: 2 (over x_lo).
Axes of the slice: x: 4 (x_hi: 2, x_lo: 2; x = x_hi * 2 + x_lo), y: 4, z: 4, core: 2. Of those that a mesh axis runs over, the one named last changes fastest.
Arguments:
- clip: bfloat16 [128, 256, 1408], P('frame'), may hold values from -6 to 6
- gain: bfloat16 [1408], replicated, may hold values from 0.25 to 1.75
- w_qkv: bfloat16 [3, 1408, 1408], P(None, None, 'chan'), may hold values from -0.15625 to 0.15625
- w_out: bfloat16 [1408, 1408], P('chan'), may hold values from -0.15625 to 0.15625
- old_table: bfloat16 [1024, 1408], replicated, may hold values from -6 to 6
- target_ids: int32 [128, 256], P('frame'), may hold values from 0 to 1023
Outputs:
- d_clip: bfloat16 [128, 256, 1408], P('frame')
- d_qkv: float32 [3, 1408, 1408], P(None, 'frame', 'chan')
- d_out: float32 [1408, 1408], P('chan', 'frame')
The draws below stay inside these ranges and needn't reach their ends.
All inputs are finite; a program needn't handle non-finite values.
Results may differ from the reference program's by a relative error of at most 0.018.
Values may be sent and summed in bfloat16 or wider, within the bound.
A program may use at most 128 MiB of HBM per device.

```python
import jax
import jax.numpy as jnp
from jax import lax

D = 1408
HEADS = 16
HEAD_DIM = 88
PATCHES = 256
OLD = 1024
FRAMES = 128


def with_ends(values, key, smallest, largest):
    longest = values.shape.index(max(values.shape))
    spots = []
    for shift in (0, 1):
        where = [jax.random.randint(jax.random.fold_in(key, axis), (), 0, length) for axis, length in enumerate(values.shape)]
        where[longest] = (where[longest] + shift) % values.shape[longest]
        spots.append(tuple(where))
    return values.at[spots[0]].set(smallest).at[spots[1]].set(largest)


def block_levels(stream_key, shape, cuts, low, high):
    level = 1.0
    for dim, shards_of in cuts:
        heights = jax.random.uniform(jax.random.fold_in(jax.random.fold_in(stream_key, 6), dim), (shards_of,), jnp.float32, low / len(cuts), high / len(cuts))
        level = level * jnp.repeat(jnp.exp(heights), shape[dim] // shards_of).reshape((-1,) + (1,) * (len(shape) - 1 - dim))
    return level


def centred(stream_key, extent, deviation, limit, split=(), kind=jnp.bfloat16):
    result = deviation * jax.random.normal(stream_key, extent, jnp.float32)
    if split:
        result = result * block_levels(stream_key, extent, split, -0.22, 0.18)
    return jnp.clip(result, -limit, limit).astype(kind)


def setup_inputs(seed: int = 0) -> dict:
    splits = jax.random.split(jax.random.key(seed), 7)
    return {
        "clip": centred(splits[0], (FRAMES, PATCHES, D), 1.0, 6.0, ((0, 64),)),
        "gain": jnp.clip(1.0 + 0.15 * jax.random.normal(splits[1], (D,), jnp.float32), 0.25, 1.75).astype(jnp.bfloat16),
        "w_qkv": centred(splits[2], (3, D, D), D ** -0.5, 0.15625, ((2, 2),)),
        "w_out": centred(splits[3], (D, D), D ** -0.5, 0.15625, ((0, 2),)),
        "old_table": centred(splits[4], (OLD, D), 1.0, 6.0),
        "target_ids": with_ends(jax.random.randint(splits[5], (FRAMES, PATCHES), 0, OLD), jax.random.fold_in(splits[5], 1), 0, OLD - 1).astype(jnp.int32),
    }


EPS = 1e-05

def norm_pieces(clip, gain):
    xf = clip.astype(jnp.float32)
    row_average = lax.optimization_barrier(jnp.mean(xf, axis=-1, keepdims=True))
    centered_input = xf - row_average
    var = lax.optimization_barrier(jnp.mean(centered_input * centered_input, axis=-1, keepdims=True))
    inverse_deviation = lax.rsqrt(var + EPS)
    standardized_input = centered_input * inverse_deviation
    normalized_rows = (standardized_input * gain.astype(jnp.float32)).astype(jnp.bfloat16)
    return (standardized_input, inverse_deviation, normalized_rows)

def attend_probs(query, keys):
    scale = HEAD_DIM ** (-0.5)
    scores = jnp.einsum('fphe,gphe->phfg', query.astype(jnp.float32), keys.astype(jnp.float32)) * scale
    top = lax.optimization_barrier(jnp.max(scores, axis=-1, keepdims=True))
    expo = jnp.exp(scores - top)
    return expo / lax.optimization_barrier(jnp.sum(expo, axis=-1, keepdims=True))

def attend(blocks):
    query, keys, values = blocks
    probs = attend_probs(query, keys)
    weights = probs.astype(jnp.bfloat16)
    return jnp.einsum('phfg,gphe->fphe', weights.astype(jnp.float32), values.astype(jnp.float32)).astype(jnp.bfloat16)

def attend_back(blocks):
    query, keys, values, d_attn = blocks
    scale = HEAD_DIM ** (-0.5)
    probs = attend_probs(query, keys)
    weights = probs.astype(jnp.bfloat16)
    dprobs = jnp.einsum('fphe,gphe->phfg', d_attn.astype(jnp.float32), values.astype(jnp.float32))
    rowsum = lax.optimization_barrier(jnp.sum(dprobs * probs, axis=-1, keepdims=True))
    dscore = (probs * (dprobs - rowsum) * scale).astype(jnp.bfloat16).astype(jnp.float32)
    dquery = jnp.einsum('phfg,gphe->fphe', dscore, keys.astype(jnp.float32)).astype(jnp.bfloat16)
    dkeys = jnp.einsum('phfg,fphe->gphe', dscore, query.astype(jnp.float32)).astype(jnp.bfloat16)
    dvalues = jnp.einsum('phfg,fphe->gphe', weights.astype(jnp.float32), d_attn.astype(jnp.float32)).astype(jnp.bfloat16)
    return (dquery, dkeys, dvalues)

def to_blocks(flat):
    return flat.reshape(FRAMES, PATCHES // 16, 16, HEADS, HEAD_DIM).transpose(1, 0, 2, 3, 4)

def from_blocks(blocks):
    return blocks.transpose(1, 0, 2, 3, 4).reshape(FRAMES * PATCHES, D)

def reference(clip, gain, w_qkv, w_out, old_table, target_ids):
    standardized_input, inverse_deviation, normalized_rows = norm_pieces(clip, gain)
    flat = normalized_rows.reshape(-1, D)
    query = jnp.dot(flat, w_qkv[0], preferred_element_type=jnp.float32).astype(jnp.bfloat16)
    keys = jnp.dot(flat, w_qkv[1], preferred_element_type=jnp.float32).astype(jnp.bfloat16)
    values = jnp.dot(flat, w_qkv[2], preferred_element_type=jnp.float32).astype(jnp.bfloat16)
    qblk, kblk, vblk = (to_blocks(query), to_blocks(keys), to_blocks(values))
    attn = from_blocks(lax.map(attend, (qblk, kblk, vblk)))
    y_full = clip.reshape(-1, D).astype(jnp.float32) + jnp.dot(attn, w_out, preferred_element_type=jnp.float32)
    target = old_table[target_ids.reshape(-1)].astype(jnp.float32)
    d_y = (y_full - target).astype(jnp.bfloat16)
    d_out = jnp.dot(attn.T, d_y, preferred_element_type=jnp.float32)
    d_attn = jnp.dot(d_y, w_out.T, preferred_element_type=jnp.float32).astype(jnp.bfloat16)
    dqb, dkb, dvb = lax.map(attend_back, (qblk, kblk, vblk, to_blocks(d_attn)))
    grads = (from_blocks(dqb), from_blocks(dkb), from_blocks(dvb))
    d_qkv = jnp.stack([jnp.dot(flat.T, grads[index], preferred_element_type=jnp.float32) for index in range(3)])
    d_norm = jnp.dot(grads[0], w_qkv[0].T, preferred_element_type=jnp.float32)
    d_norm = d_norm + jnp.dot(grads[1], w_qkv[1].T, preferred_element_type=jnp.float32)
    d_norm = d_norm + jnp.dot(grads[2], w_qkv[2].T, preferred_element_type=jnp.float32)
    gain_scaled = d_norm.reshape(FRAMES, PATCHES, D) * gain.astype(jnp.float32)
    norm_backward_pass = inverse_deviation * (gain_scaled - lax.optimization_barrier(jnp.mean(gain_scaled, axis=-1, keepdims=True)) - standardized_input * lax.optimization_barrier(jnp.mean(gain_scaled * standardized_input, axis=-1, keepdims=True)))
    d_clip = (d_y.reshape(FRAMES, PATCHES, D).astype(jnp.float32) + norm_backward_pass).astype(jnp.bfloat16)
    return (d_clip, d_qkv, d_out)
```

```python
import functools

import jax
import jax.numpy as jnp
from jax import lax
from jax.experimental import pallas as pl
from jax.experimental.pallas import tpu as pltpu
from jax.sharding import PartitionSpec as P

HEAD_DIM = 88
EPS = 1e-05
XH, Y, Z, CORE = 2, 4, 4, 2
ROWS = 22
PAD = 24

f32 = jnp.float32
bf16 = jnp.bfloat16


def frame_index(xh, y, z, core):
    return ((xh * Y + y) * Z + z) * CORE + core


def coordinates():
    f = lax.axis_index("frame")
    return f // (Y * Z * CORE), (f // (Z * CORE)) % Y, (f // CORE) % Z, f % CORE


def source_row(p):
    r = p % PAD
    b = (p // PAD) % 4
    xh = (p // (PAD * 4)) % 2
    a = (p // (PAD * 8)) % 4
    core = p // (PAD * 32)
    y = a + core * (b - a)
    z = b + core * (a - b)
    return jnp.where(r < ROWS, frame_index(xh, y, z, core) * ROWS + r, -1)


def add_blocks(out, terms, count):
    def step(j, _):
        total = terms[0][j].astype(f32)
        for t in terms[1:]:
            total = total + t[j].astype(f32)
        out[j] = total.astype(out.dtype)
        return 0

    lax.fori_loop(0, count, step, 0)


def reduce_scatter_kernel(
    g, out, own, sib, summed, r1, l1, r2, l2, r3, l3, t, mr, ml,
    br1, bl1, br2, bl2, br3, bl3, u, bmr, bml, xr,
    local_sem, core_send, core_recv, a_send, a_recv, b_send, b_recv, x_send, x_recv,
):
    xh, y, z, core = coordinates()
    here = y * (1 - core) + z * core
    there = z * (1 - core) + y * core

    def ring(first, step):
        dy = step if first else 0
        dz = 0 if first else step
        ny = (y + (1 - core) * dy + core * dz + Y) % Y
        nz = (z + core * dy + (1 - core) * dz + Z) % Z
        return {"frame": frame_index(xh, ny, nz, core)}

    sibling = {"frame": frame_index(xh, y, z, 1 - core)}
    across = {"frame": frame_index(1 - xh, y, z, core)}
    barrier = pltpu.get_barrier_semaphore()
    for peer in (sibling, across, ring(True, 1), ring(True, -1), ring(False, 1), ring(False, -1)):
        pl.semaphore_signal(barrier, inc=1, device_id=peer, device_id_type=pl.DeviceIdType.MESH)
    pl.semaphore_wait(barrier, 6)

    def remote(src, dst, send, recv, peer):
        return pltpu.make_async_remote_copy(
            src_ref=src, dst_ref=dst, send_sem=send, recv_sem=recv,
            device_id=peer, device_id_type=pl.DeviceIdType.MESH,
        )

    order = ((2, 0), (2, 1), (1, 1), (3, 0), (1, 0), (3, 1), (0, 0), (0, 1))
    mine = [((here + da) % 4, h) for da, h in order]
    theirs = [((there + da) % 4, h) for da, h in order]
    swaps, loads = [], []
    for i in range(8):
        a, h = theirs[i]
        c = remote(g.at[1 - core, a, h], sib.at[i], core_send.at[i], core_recv.at[i], sibling)
        c.start()
        swaps.append(c)
        a, h = mine[i]
        c = pltpu.make_async_copy(g.at[core, a, h], own.at[i], local_sem.at[i])
        c.start()
        loads.append(c)

    def fold(i):
        loads[i].wait()
        swaps[i].wait_recv()
        add_blocks(summed.at[i], (own.at[i], sib.at[i]), 4)

    right, left = ring(True, 1), ring(True, -1)
    copies = []

    def send(src, dst, k, peer, sends, recvs):
        c = remote(src, dst, sends.at[k], recvs.at[k], peer)
        c.start()
        copies.append(c)
        return c

    fold(0)
    c1r = send(summed.at[0], r1, 0, right, a_send, a_recv)
    fold(1)
    c1l = send(summed.at[1], l1, 1, left, a_send, a_recv)
    fold(2)
    c2r = send(summed.at[2], r2, 2, right, a_send, a_recv)
    fold(3)
    c2l = send(summed.at[3], l2, 3, left, a_send, a_recv)
    fold(4)
    c1r.wait_recv()
    add_blocks(mr, (summed.at[4], r1), 4)
    c3r = send(mr, r3, 4, right, a_send, a_recv)
    fold(5)
    c1l.wait_recv()
    add_blocks(ml, (summed.at[5], l1), 4)
    c3l = send(ml, l3, 5, left, a_send, a_recv)
    fold(6)
    fold(7)
    c2l.wait_recv()
    c3r.wait_recv()
    add_blocks(t.at[0], (summed.at[6], r3, l2), 4)
    c2r.wait_recv()
    c3l.wait_recv()
    add_blocks(t.at[1], (summed.at[7], r2, l3), 4)

    right, left = ring(False, 1), ring(False, -1)
    at = lambda h, d: t.at[h, (there + d) % 4]
    d1r = send(at(0, 2), br1, 0, right, b_send, b_recv)
    d1l = send(at(1, 2), bl1, 1, left, b_send, b_recv)
    d2r = send(at(1, 1), br2, 2, right, b_send, b_recv)
    d2l = send(at(0, 3), bl2, 3, left, b_send, b_recv)
    d1r.wait_recv()
    bmr[...] = (at(0, 1)[...].astype(f32) + br1[...].astype(f32)).astype(bf16)
    d3r = send(bmr, br3, 4, right, b_send, b_recv)
    d1l.wait_recv()
    bml[...] = (at(1, 3)[...].astype(f32) + bl1[...].astype(f32)).astype(bf16)
    d3l = send(bml, bl3, 5, left, b_send, b_recv)
    d2l.wait_recv()
    d3r.wait_recv()
    u[0] = at(0, 0)[...].astype(f32) + br3[...].astype(f32) + bl2[...].astype(f32)
    d2r.wait_recv()
    d3l.wait_recv()
    u[1] = at(1, 0)[...].astype(f32) + br2[...].astype(f32) + bl3[...].astype(f32)

    e = remote(u.at[1 - xh], xr, x_send, x_recv, across)
    e.start()
    e.wait_recv()
    out[...] = u[xh] + xr[...]
    e.wait_send()
    for c in swaps:
        c.wait_send()
    for c in copies:
        c.wait_send()


def reduce_scatter(g, collective_id):
    width = g.shape[-1]
    piece = (4, PAD, width)
    block = (PAD, width)
    return pl.pallas_call(
        reduce_scatter_kernel,
        out_shape=jax.ShapeDtypeStruct(block, f32),
        in_specs=[pl.BlockSpec(memory_space=pl.ANY)],
        out_specs=pl.BlockSpec(memory_space=pltpu.VMEM),
        scratch_shapes=[
            pltpu.VMEM((8,) + piece, bf16),
            pltpu.VMEM((8,) + piece, bf16),
            pltpu.VMEM((8,) + piece, bf16),
        ]
        + [pltpu.VMEM(piece, bf16)] * 6
        + [pltpu.VMEM((2,) + piece, bf16)]
        + [pltpu.VMEM(piece, bf16)] * 2
        + [pltpu.VMEM(block, bf16)] * 6
        + [pltpu.VMEM((2,) + block, f32)]
        + [pltpu.VMEM(block, bf16)] * 2
        + [pltpu.VMEM(block, f32)]
        + [
            pltpu.SemaphoreType.DMA((8,)),
            pltpu.SemaphoreType.DMA((8,)),
            pltpu.SemaphoreType.DMA((8,)),
            pltpu.SemaphoreType.DMA((6,)),
            pltpu.SemaphoreType.DMA((6,)),
            pltpu.SemaphoreType.DMA((6,)),
            pltpu.SemaphoreType.DMA((6,)),
            pltpu.SemaphoreType.DMA,
            pltpu.SemaphoreType.DMA,
        ],
        compiler_params=pltpu.CompilerParams(
            collective_id=collective_id, has_side_effects=True, vmem_limit_bytes=48 * 2**20
        ),
        name="grad_reduce_scatter",
    )(g)


def body(clip, gain, w_qkv, w_out, old_table, target_ids):
    frames_here, patches, width = clip.shape
    cols = w_qkv.shape[2]
    heads_here = cols // HEAD_DIM
    groups = lax.axis_size("frame")
    patch_here = patches // groups
    total = frames_here * groups
    tokens = total * patch_here
    scale = HEAD_DIM ** (-0.5)
    gain_float = gain.astype(f32)
    me = lax.axis_index("frame")

    all_ids = lax.all_gather(target_ids, "frame", axis=0, tiled=True)
    ids = lax.dynamic_slice_in_dim(all_ids, me * patch_here, patch_here, axis=1)
    ids = ids.T.reshape(-1)

    moved = lax.all_to_all(
        clip.reshape(frames_here, groups, patch_here, width),
        "frame", split_axis=1, concat_axis=0, tiled=True,
    )
    x = moved.reshape(total, patch_here, width).transpose(1, 0, 2).reshape(tokens, width)

    xf = x.astype(f32)
    centered = xf - jnp.mean(xf, axis=-1, keepdims=True)
    var = jnp.mean(centered * centered, axis=-1, keepdims=True)
    rstd = lax.rsqrt(var + EPS)
    xhat = centered * rstd
    normed = (xhat * gain_float).astype(bf16)
    qkv = jnp.einsum("td,idh->ith", normed, w_qkv, preferred_element_type=f32).astype(bf16)
    heads = qkv.reshape(3, patch_here, total, heads_here, HEAD_DIM).transpose(0, 1, 3, 2, 4)
    query, keys, values = heads[0], heads[1], heads[2]
    scores = jnp.einsum("phfe,phge->phfg", query, keys, preferred_element_type=f32) * scale
    top = jnp.max(scores, axis=-1, keepdims=True)
    expo = jnp.exp(scores - top)
    probs = expo / jnp.sum(expo, axis=-1, keepdims=True)
    weights = probs.astype(bf16)
    attn = jnp.einsum("phfg,phge->phfe", weights, values, preferred_element_type=f32).astype(bf16)
    attn = attn.transpose(0, 2, 1, 3).reshape(tokens, cols)
    part = jnp.dot(attn, w_out, preferred_element_type=f32)
    branch = lax.psum(part.astype(bf16), "chan").astype(f32)
    target = jnp.take(old_table, ids, axis=0).astype(f32)
    d_y = (xf + branch - target).astype(bf16)
    d_attn = jnp.einsum("td,hd->th", d_y, w_out, preferred_element_type=f32).astype(bf16)
    d_attn = d_attn.reshape(patch_here, total, heads_here, HEAD_DIM).transpose(0, 2, 1, 3)
    dprobs = jnp.einsum("phfe,phge->phfg", d_attn, values, preferred_element_type=f32)
    rowsum = jnp.sum(dprobs * probs, axis=-1, keepdims=True)
    dscore = (probs * (dprobs - rowsum) * scale).astype(bf16)
    dq = jnp.einsum("phfg,phge->phfe", dscore, keys, preferred_element_type=f32).astype(bf16)
    dk = jnp.einsum("phfg,phfe->phge", dscore, query, preferred_element_type=f32).astype(bf16)
    dv = jnp.einsum("phfg,phfe->phge", weights, d_attn, preferred_element_type=f32).astype(bf16)
    grads = jnp.stack([dq, dk, dv]).transpose(0, 1, 3, 2, 4).reshape(3, tokens, cols)

    padded = PAD * 64
    rows = source_row(lax.broadcasted_iota(jnp.int32, (width, padded), 1))
    pick = (rows == lax.broadcasted_iota(jnp.int32, (width, padded), 0)).astype(bf16)
    normed_padded = jnp.dot(normed, pick, preferred_element_type=f32).astype(bf16)
    d_y_padded = jnp.dot(d_y, pick, preferred_element_type=f32).astype(bf16)
    g_qkv = jnp.einsum("td,ith->dih", normed_padded, grads, preferred_element_type=f32)
    g_out = jnp.einsum("td,th->dh", d_y_padded, attn, preferred_element_type=f32)
    g = jnp.concatenate([g_qkv.astype(bf16), g_out.astype(bf16)[:, None]], axis=1)
    g = g.reshape(CORE, 4, XH, 4, PAD, 4 * cols)
    reduced = reduce_scatter(g, 0)[:ROWS].reshape(ROWS, 4, cols)
    d_qkv_shard = reduced[:, :3].transpose(1, 0, 2)
    d_out_shard = reduced[:, 3].T

    d_part = jnp.einsum("ith,idh->td", grads, w_qkv, preferred_element_type=f32)
    d_norm = lax.psum(d_part.astype(bf16), "chan").astype(f32)
    gs = d_norm * gain_float
    back = rstd * (
        gs
        - jnp.mean(gs, axis=-1, keepdims=True)
        - xhat * jnp.mean(gs * xhat, axis=-1, keepdims=True)
    )
    d_clip = (d_y.astype(f32) + back).astype(bf16)
    d_clip = d_clip.reshape(patch_here, total, width).transpose(1, 0, 2)
    home = lax.all_to_all(
        d_clip.reshape(groups, frames_here, patch_here, width),
        "frame", split_axis=0, concat_axis=2, tiled=True,
    )
    return (home.reshape(frames_here, patches, width), d_qkv_shard, d_out_shard)


def solution(mesh):
    return jax.shard_map(
        body,
        mesh=mesh,
        in_specs=(
            P("frame", None, None),
            P(),
            P(None, None, "chan"),
            P("chan", None),
            P(),
            P("frame", None),
        ),
        out_specs=(P("frame", None, None), P(None, "frame", "chan"), P("chan", "frame")),
        check_vma=False,
    )
```

```python
import functools

import jax
import jax.numpy as jnp
from jax import lax
from jax.experimental import pallas as pl
from jax.experimental.pallas import tpu as pltpu
from jax.sharding import PartitionSpec as P

HEAD_DIM = 88
EPS = 1e-05
XH, Y, Z, CORE = 2, 4, 4, 2
FRAME = XH * Y * Z * CORE
ROWS = 22
PAD = 24

f32 = jnp.float32
bf16 = jnp.bfloat16


def frame_index(xh, y, z, core):
    return ((xh * Y + y) * Z + z) * CORE + core


def coordinates():
    f = lax.axis_index("frame")
    return f // (Y * Z * CORE), (f // (Z * CORE)) % Y, (f // CORE) % Z, f % CORE


def all_peer(k):
    f = lax.axis_index("frame")
    chan = lax.axis_index("chan")
    p = (f + k) % FRAME
    far = (p // (FRAME // 2) + f // (FRAME // 2)) % 2
    return p, {"frame": p, "chan": (chan + far) % 2}


def greet_all(extra):
    barrier = pltpu.get_barrier_semaphore()

    def greet(k, _):
        pl.semaphore_signal(
            barrier, inc=1, device_id=all_peer(k)[1], device_id_type=pl.DeviceIdType.MESH
        )
        return 0

    lax.fori_loop(1, FRAME, greet, 0)
    pl.semaphore_signal(barrier, inc=1, device_id=extra, device_id_type=pl.DeviceIdType.MESH)
    pl.semaphore_wait(barrier, FRAME)


def all_copy(src, dst, sends, recvs, k):
    p, peer = all_peer(k)
    return pltpu.make_async_remote_copy(
        src_ref=src.at[p], dst_ref=dst.at[lax.axis_index("frame")],
        send_sem=sends.at[k], recv_sem=recvs.at[k],
        device_id=peer, device_id_type=pl.DeviceIdType.MESH,
    )


def start_all(src, dst, sends, recvs, own_sem):
    def start(k, _):
        all_copy(src, dst, sends, recvs, k).start()
        return 0

    lax.fori_loop(1, FRAME, start, 0)
    f = lax.axis_index("frame")
    pltpu.make_async_copy(src.at[f], dst.at[f], own_sem).start()


def wait_all(src, dst, sends, recvs, own_sem):
    f = lax.axis_index("frame")
    pltpu.make_async_copy(src.at[f], dst.at[f], own_sem).wait()

    def wait(k, _):
        all_copy(src, dst, sends, recvs, k).wait_recv()
        return 0

    lax.fori_loop(1, FRAME, wait, 0)

    def drain(k, _):
        all_copy(src, dst, sends, recvs, k).wait_send()
        return 0

    lax.fori_loop(1, FRAME, drain, 0)


def gather_kernel(src, w, dst, w_other, sends, recvs, own_sem, w_send, w_recv):
    xh, y, z, core = coordinates()
    chan = lax.axis_index("chan")
    partner = {"chan": 1 - chan}
    sibling = {"frame": frame_index(xh, y, z, 1 - core)}
    greet_all(partner)

    def remote(s, d, k, peer):
        return pltpu.make_async_remote_copy(
            src_ref=s, dst_ref=d, send_sem=w_send.at[k], recv_sem=w_recv.at[k],
            device_id=peer, device_id_type=pl.DeviceIdType.MESH,
        )

    first = remote(w.at[core], w_other.at[core], 0, partner)
    first.start()
    start_all(src, dst, sends, recvs, own_sem)
    first.wait_recv()
    second = remote(w_other.at[core], w_other.at[core], 1, sibling)
    second.start()
    second.wait_recv()
    first.wait_send()
    second.wait_send()
    wait_all(src, dst, sends, recvs, own_sem)


def gather_clip(src, w):
    any_spec = pl.BlockSpec(memory_space=pl.ANY)
    return pl.pallas_call(
        gather_kernel,
        out_shape=[
            jax.ShapeDtypeStruct(src.shape, src.dtype),
            jax.ShapeDtypeStruct(w.shape, w.dtype),
        ],
        in_specs=[pl.BlockSpec(memory_space=pltpu.VMEM), any_spec],
        out_specs=[pl.BlockSpec(memory_space=pltpu.VMEM), any_spec],
        scratch_shapes=[
            pltpu.SemaphoreType.DMA((FRAME,)),
            pltpu.SemaphoreType.DMA((FRAME,)),
            pltpu.SemaphoreType.DMA,
            pltpu.SemaphoreType.DMA((2,)),
            pltpu.SemaphoreType.DMA((2,)),
        ],
        compiler_params=pltpu.CompilerParams(
            collective_id=1, has_side_effects=True, vmem_limit_bytes=32 * 2**20
        ),
        name="gather_clip",
    )(src, w)


def dot(a, b):
    return jnp.dot(a, b, preferred_element_type=f32)


def dot_nt(a, b):
    return lax.dot_general(a, b, (((1,), (1,)), ((), ())), preferred_element_type=f32)


def dot_tn(a, b):
    return lax.dot_general(a, b, (((0,), (0,)), ((), ())), preferred_element_type=f32)


def iota(shape, dim):
    return lax.broadcasted_iota(jnp.int32, shape, dim)


def norm_terms(x):
    centered = x - jnp.mean(x, axis=-1, keepdims=True)
    rstd = lax.rsqrt(jnp.mean(centered * centered, axis=-1, keepdims=True) + EPS)
    return centered * rstd, rstd


def sublayer_kernel(
    r, gain, w_qkv, w_out, w_other, table, home, g,
    x_s, ids_s, n_s, q_s, k_s, v_s, o_s, oo_s, p_s, dy_s, do_s, dq_s, dk_s, dv_s, dn_s, dno_s, d_s,
    o_send, o_recv, dn_send, dn_recv,
):
    width = x_s.shape[1]
    cols = q_s.shape[1]
    n_heads = cols // HEAD_DIM
    frames = 128
    tokens = x_s.shape[0]
    patches = tokens // frames
    scale = HEAD_DIM ** (-0.5)
    partner = {"chan": 1 - lax.axis_index("chan")}
    barrier = pltpu.get_barrier_semaphore()
    pl.semaphore_signal(barrier, inc=1, device_id=partner, device_id_type=pl.DeviceIdType.MESH)
    pl.semaphore_wait(barrier, 1)

    def rows(p):
        return pl.ds(pl.multiple_of(p * frames, frames), frames)

    def swap(src, dst, sends, recvs, p):
        return pltpu.make_async_remote_copy(
            src_ref=src.at[rows(p)], dst_ref=dst.at[rows(p)],
            send_sem=sends.at[p], recv_sem=recvs.at[p],
            device_id=partner, device_id_type=pl.DeviceIdType.MESH,
        )

    def head(ref, p, h):
        return ref[rows(p), h * HEAD_DIM : (h + 1) * HEAD_DIM]

    def forward(p, _):
        t = iota((frames, tokens), 0)
        pick = (iota((frames, tokens), 1) == (t // 2) * 8 + 2 * p + t % 2).astype(bf16)
        moved = dot(pick, r[...])
        x = moved[:, :width]
        x_s[rows(p), :] = x.astype(bf16)
        ids_s[rows(p), :] = moved[:, width:]
        xhat, _ = norm_terms(x)
        normed = (xhat * gain[...].astype(f32)).astype(bf16)
        n_s[rows(p), :] = normed
        q_s[rows(p), :] = dot(normed, w_qkv[0]).astype(bf16)
        k_s[rows(p), :] = dot(normed, w_qkv[1]).astype(bf16)
        v_s[rows(p), :] = dot(normed, w_qkv[2]).astype(bf16)
        for h in range(n_heads):
            scores = dot_nt(head(q_s, p, h), head(k_s, p, h)) * scale
            expo = jnp.exp(scores - jnp.max(scores, axis=-1, keepdims=True))
            probs = expo / jnp.sum(expo, axis=-1, keepdims=True)
            p_s[p * n_heads + h] = probs
            o_s[rows(p), h * HEAD_DIM : (h + 1) * HEAD_DIM] = dot(
                probs.astype(bf16), head(v_s, p, h)
            ).astype(bf16)
        swap(o_s, oo_s, o_send, o_recv, p).start()
        return 0

    lax.fori_loop(0, patches, forward, 0)

    def backward(p, _):
        hi_lo = ids_s[rows(p), :]
        ids = hi_lo[:, 0:1] * 32.0 + hi_lo[:, 1:2]
        n_old = table.shape[0]
        pick = (iota((frames, n_old), 1).astype(f32) == ids).astype(bf16)
        target = dot(pick, table[...])
        swap(o_s, oo_s, o_send, o_recv, p).wait_recv()
        branch = dot(o_s[rows(p), :], w_out[...]) + dot(oo_s[rows(p), :], w_other[...])
        d_y = (x_s[rows(p), :].astype(f32) + branch - target).astype(bf16)
        dy_s[rows(p), :] = d_y
        do_s[rows(p), :] = dot_nt(d_y, w_out[...]).astype(bf16)
        for h in range(n_heads):
            here = slice(h * HEAD_DIM, (h + 1) * HEAD_DIM)
            probs = p_s[p * n_heads + h]
            d_o = head(do_s, p, h)
            dprobs = dot_nt(d_o, head(v_s, p, h))
            rowsum = jnp.sum(dprobs * probs, axis=-1, keepdims=True)
            ds = (probs * (dprobs - rowsum) * scale).astype(bf16)
            dq_s[rows(p), here] = dot(ds, head(k_s, p, h)).astype(bf16)
            dk_s[rows(p), here] = dot_tn(ds, head(q_s, p, h)).astype(bf16)
            dv_s[rows(p), here] = dot_tn(probs.astype(bf16), d_o).astype(bf16)
        dn = dot_nt(dq_s[rows(p), :], w_qkv[0])
        dn = dn + dot_nt(dk_s[rows(p), :], w_qkv[1])
        dn = dn + dot_nt(dv_s[rows(p), :], w_qkv[2])
        dn_s[rows(p), :] = dn.astype(bf16)
        swap(dn_s, dno_s, dn_send, dn_recv, p).start()
        return 0

    lax.fori_loop(0, patches, backward, 0)

    block = 8 * ROWS
    window = 384

    def weight_grads(k, _):
        start = jnp.minimum(k * block // 128, (width - window) // 128) * 128
        lanes = pl.ds(pl.multiple_of(start, 128), window)
        shape = (8 * PAD, window)
        at = iota(shape, 0)
        wanted = jnp.where(at % PAD < ROWS, k * block + (at // PAD) * ROWS + at % PAD - start, -1)
        pick = (iota(shape, 1) == wanted).astype(bf16)
        normed_t = dot_nt(pick, n_s[:, lanes]).astype(bf16)
        d_y_t = dot_nt(pick, dy_s[:, lanes]).astype(bf16)
        xh, y = k // Y, k % Y
        for i, (left, right) in enumerate(
            ((normed_t, dq_s), (normed_t, dk_s), (normed_t, dv_s), (d_y_t, o_s))
        ):
            part = dot(left, right[...]).astype(bf16)
            for j in range(8):
                z, core = j // 2, j % 2
                a, b = (y, z) if core == 0 else (z, y)
                g[core, a, xh, b, :, i * cols : (i + 1) * cols] = part[j * PAD : (j + 1) * PAD]
        return 0

    lax.fori_loop(0, width // block, weight_grads, 0)

    def finish(p, _):
        swap(dn_s, dno_s, dn_send, dn_recv, p).wait_recv()
        dn = dn_s[rows(p), :].astype(f32) + dno_s[rows(p), :].astype(f32)
        xhat, rstd = norm_terms(x_s[rows(p), :].astype(f32))
        gs = dn * gain[...].astype(f32)
        back = rstd * (
            gs
            - jnp.mean(gs, axis=-1, keepdims=True)
            - xhat * jnp.mean(gs * xhat, axis=-1, keepdims=True)
        )
        d_s[rows(p), :] = (dy_s[rows(p), :].astype(f32) + back).astype(bf16)
        return 0

    lax.fori_loop(0, patches, finish, 0)

    def to_home(j, _):
        t = iota((frames, tokens), 0) + j * frames
        source = (t % 8 // 2) * frames + 2 * (t // 8) + t % 2
        pick = (iota((frames, tokens), 1) == source).astype(bf16)
        moved = dot(pick, d_s[...])
        home[pl.ds(j * (frames // 8), frames // 8)] = moved.reshape(
            frames // 8, 8, width
        ).astype(bf16)
        return 0

    lax.fori_loop(0, patches, to_home, 0)

    def drain(p, _):
        swap(o_s, oo_s, o_send, o_recv, p).wait_send()
        swap(dn_s, dno_s, dn_send, dn_recv, p).wait_send()
        return 0

    lax.fori_loop(0, patches, drain, 0)


def sublayer(r, gain, w_qkv, w_out, w_other, table):
    tokens = r.shape[0]
    width, cols = w_qkv.shape[1:]
    patches = tokens // 128
    vmem = pl.BlockSpec(memory_space=pltpu.VMEM)
    wide = pltpu.VMEM((tokens, width), bf16)
    narrow = pltpu.VMEM((tokens, cols), bf16)
    return pl.pallas_call(
        sublayer_kernel,
        out_shape=[
            jax.ShapeDtypeStruct((FRAME, 8, width), bf16),
            jax.ShapeDtypeStruct((CORE, 4, XH, 4, PAD, 4 * cols), bf16),
        ],
        in_specs=[vmem] * 6,
        out_specs=[vmem] * 2,
        scratch_shapes=[
            wide,
            pltpu.VMEM((tokens, r.shape[1] - width), f32),
            wide,
            narrow, narrow, narrow, narrow, narrow,
            pltpu.VMEM((patches * cols // HEAD_DIM, 128, 128), f32),
            wide,
            narrow, narrow, narrow, narrow,
            wide, wide, wide,
        ]
        + [pltpu.SemaphoreType.DMA((patches,))] * 4,
        compiler_params=pltpu.CompilerParams(
            collective_id=2, has_side_effects=True, vmem_limit_bytes=60 * 2**20
        ),
        name="sublayer",
    )(r, gain, w_qkv, w_out, w_other, table)


def add_blocks(out, terms, count):
    def step(j, _):
        total = terms[0][j].astype(f32)
        for t in terms[1:]:
            total = total + t[j].astype(f32)
        out[j] = total.astype(out.dtype)
        return 0

    lax.fori_loop(0, count, step, 0)


def reduce_scatter_kernel(
    g, d_send, out, d_recv, own, sib, summed, r1, l1, r2, l2, r3, l3, t, mr, ml,
    br1, bl1, br2, bl2, br3, bl3, u, bmr, bml, xr,
    local_sem, core_send, core_recv, a_send, a_recv, b_send, b_recv, x_send, x_recv, d_sems, e_sems, f_sem,
):
    xh, y, z, core = coordinates()
    chan = lax.axis_index("chan")
    here = y * (1 - core) + z * core
    there = z * (1 - core) + y * core

    def ring(first, step):
        dy = step if first else 0
        dz = 0 if first else step
        ny = (y + (1 - core) * dy + core * dz + Y) % Y
        nz = (z + core * dy + (1 - core) * dz + Z) % Z
        return {"frame": frame_index(xh, ny, nz, core)}

    sibling = {"frame": frame_index(xh, y, z, 1 - core)}
    across = {"frame": frame_index(1 - xh, y, z, core)}
    greet_all(across)

    def remote(src, dst, send, recv, peer):
        return pltpu.make_async_remote_copy(
            src_ref=src, dst_ref=dst, send_sem=send, recv_sem=recv,
            device_id=peer, device_id_type=pl.DeviceIdType.MESH,
        )

    start_all(d_send, d_recv, d_sems, e_sems, f_sem)

    order = ((2, 0), (2, 1), (1, 1), (3, 0), (1, 0), (3, 1), (0, 0), (0, 1))
    mine = [((here + da) % 4, h) for da, h in order]
    theirs = [((there + da) % 4, h) for da, h in order]
    swaps, loads = [], []
    for i in range(8):
        a, h = theirs[i]
        c = remote(g.at[1 - core, a, h], sib.at[i], core_send.at[i], core_recv.at[i], sibling)
        c.start()
        swaps.append(c)
        a, h = mine[i]
        c = pltpu.make_async_copy(g.at[core, a, h], own.at[i], local_sem.at[i])
        c.start()
        loads.append(c)

    def fold(i):
        loads[i].wait()
        swaps[i].wait_recv()
        add_blocks(summed.at[i], (own.at[i], sib.at[i]), 4)

    right, left = ring(True, 1), ring(True, -1)
    copies = []

    def send(src, dst, k, peer, sends, recvs):
        c = remote(src, dst, sends.at[k], recvs.at[k], peer)
        c.start()
        copies.append(c)
        return c

    fold(0)
    c1r = send(summed.at[0], r1, 0, right, a_send, a_recv)
    fold(1)
    c1l = send(summed.at[1], l1, 1, left, a_send, a_recv)
    fold(2)
    c2r = send(summed.at[2], r2, 2, right, a_send, a_recv)
    fold(3)
    c2l = send(summed.at[3], l2, 3, left, a_send, a_recv)
    fold(4)
    c1r.wait_recv()
    add_blocks(mr, (summed.at[4], r1), 4)
    c3r = send(mr, r3, 4, right, a_send, a_recv)
    fold(5)
    c1l.wait_recv()
    add_blocks(ml, (summed.at[5], l1), 4)
    c3l = send(ml, l3, 5, left, a_send, a_recv)
    fold(6)
    fold(7)
    c2l.wait_recv()
    c3r.wait_recv()
    add_blocks(t.at[0], (summed.at[6], r3, l2), 4)
    c2r.wait_recv()
    c3l.wait_recv()
    add_blocks(t.at[1], (summed.at[7], r2, l3), 4)

    right, left = ring(False, 1), ring(False, -1)
    at = lambda h, d: t.at[h, (there + d) % 4]
    d1r = send(at(0, 2), br1, 0, right, b_send, b_recv)
    d1l = send(at(1, 2), bl1, 1, left, b_send, b_recv)
    d2r = send(at(1, 1), br2, 2, right, b_send, b_recv)
    d2l = send(at(0, 3), bl2, 3, left, b_send, b_recv)
    d1r.wait_recv()
    bmr[...] = (at(0, 1)[...].astype(f32) + br1[...].astype(f32)).astype(bf16)
    d3r = send(bmr, br3, 4, right, b_send, b_recv)
    d1l.wait_recv()
    bml[...] = (at(1, 3)[...].astype(f32) + bl1[...].astype(f32)).astype(bf16)
    d3l = send(bml, bl3, 5, left, b_send, b_recv)
    d2l.wait_recv()
    d3r.wait_recv()
    u[0] = at(0, 0)[...].astype(f32) + br3[...].astype(f32) + bl2[...].astype(f32)
    d2r.wait_recv()
    d3l.wait_recv()
    u[1] = at(1, 0)[...].astype(f32) + br2[...].astype(f32) + bl3[...].astype(f32)

    e = remote(u.at[1 - xh], xr, x_send, x_recv, across)
    e.start()
    e.wait_recv()
    out[...] = u[xh] + xr[...]
    e.wait_send()
    for c in swaps:
        c.wait_send()
    for c in copies:
        c.wait_send()
    wait_all(d_send, d_recv, d_sems, e_sems, f_sem)


def reduce_scatter(g, home):
    width = g.shape[-1]
    piece = (4, PAD, width)
    block = (PAD, width)
    return pl.pallas_call(
        reduce_scatter_kernel,
        out_shape=[
            jax.ShapeDtypeStruct(block, f32),
            jax.ShapeDtypeStruct(home.shape, home.dtype),
        ],
        in_specs=[pl.BlockSpec(memory_space=pl.ANY), pl.BlockSpec(memory_space=pltpu.VMEM)],
        out_specs=[pl.BlockSpec(memory_space=pltpu.VMEM)] * 2,
        scratch_shapes=[
            pltpu.VMEM((8,) + piece, bf16),
            pltpu.VMEM((8,) + piece, bf16),
            pltpu.VMEM((8,) + piece, bf16),
        ]
        + [pltpu.VMEM(piece, bf16)] * 6
        + [pltpu.VMEM((2,) + piece, bf16)]
        + [pltpu.VMEM(piece, bf16)] * 2
        + [pltpu.VMEM(block, bf16)] * 6
        + [pltpu.VMEM((2,) + block, f32)]
        + [pltpu.VMEM(block, bf16)] * 2
        + [pltpu.VMEM(block, f32)]
        + [
            pltpu.SemaphoreType.DMA((8,)),
            pltpu.SemaphoreType.DMA((8,)),
            pltpu.SemaphoreType.DMA((8,)),
            pltpu.SemaphoreType.DMA((6,)),
            pltpu.SemaphoreType.DMA((6,)),
            pltpu.SemaphoreType.DMA((6,)),
            pltpu.SemaphoreType.DMA((6,)),
            pltpu.SemaphoreType.DMA,
            pltpu.SemaphoreType.DMA,
            pltpu.SemaphoreType.DMA((FRAME,)),
            pltpu.SemaphoreType.DMA((FRAME,)),
            pltpu.SemaphoreType.DMA,
        ],
        compiler_params=pltpu.CompilerParams(
            collective_id=0, has_side_effects=True, vmem_limit_bytes=48 * 2**20
        ),
        name="grad_reduce_scatter",
    )(g, home)


def body(clip, gain, w_qkv, w_out, old_table, target_ids):
    frames_here, patches, width = clip.shape
    cols = w_qkv.shape[2]
    tokens = frames_here * patches
    each = tokens // FRAME

    ids = target_ids.reshape(tokens, 1)
    extra = jnp.concatenate([ids // 32, ids % 32, jnp.zeros((tokens, 126), jnp.int32)], axis=1)
    flat = jnp.concatenate([clip.reshape(tokens, width), extra.astype(bf16)], axis=1)
    t = iota((tokens, tokens), 0)
    pick = iota((tokens, tokens), 1) == (t % 2) * patches + (t // 8) * 4 + t % 8 // 2
    leaving = dot(pick.astype(bf16), flat).astype(bf16).reshape(FRAME, each, width + 128)
    arrived, w_other = gather_clip(leaving, w_out.reshape(2, cols // 2, width))

    home, g = sublayer(
        arrived.reshape(tokens, width + 128),
        gain.reshape(1, width),
        w_qkv,
        w_out,
        w_other.reshape(cols, width),
        old_table,
    )
    reduced, returned = reduce_scatter(g, home)

    t = iota((tokens, tokens), 0)
    source = (t % patches // 4) * 8 + (t % 4) * 2 + t // patches
    pick = iota((tokens, tokens), 1) == source
    d_clip = dot(pick.astype(bf16), returned.reshape(tokens, width)).astype(bf16)
    reduced = reduced[:ROWS].reshape(ROWS, 4, cols)
    return (
        d_clip.reshape(frames_here, patches, width),
        reduced[:, :3].transpose(1, 0, 2),
        reduced[:, 3].T,
    )


def solution(mesh):
    return jax.shard_map(
        body,
        mesh=mesh,
        in_specs=(
            P("frame", None, None),
            P(),
            P(None, None, "chan"),
            P("chan", None),
            P(),
            P("frame", None),
        ),
        out_specs=(P("frame", None, None), P(None, "frame", "chan"), P("chan", "frame")),
        check_vma=False,
    )
```

```python
import jax
import jax.numpy as jnp
from jax import lax
from jax.experimental import pallas as pl
from jax.experimental.pallas import tpu as pltpu
from jax.sharding import PartitionSpec as P

HEAD_DIM = 88
EPS = 1e-05
VMEM_LIMIT = 63 * 2**20
XH, Y, Z, CORE = 2, 4, 4, 2
FRAME = XH * Y * Z * CORE
ROWS = 22
PAD = 24

f32 = jnp.float32
bf16 = jnp.bfloat16


def frame_index(xh, y, z, core):
    return ((xh * Y + y) * Z + z) * CORE + core


def coordinates():
    f = lax.axis_index("frame")
    return f // (Y * Z * CORE), (f // (Z * CORE)) % Y, (f // CORE) % Z, f % CORE


def all_peer(k):
    f = lax.axis_index("frame")
    chan = lax.axis_index("chan")
    p = (f + k) % FRAME
    far = (p // (FRAME // 2) + f // (FRAME // 2)) % 2
    return p, {"frame": p, "chan": (chan + far) % 2}


def greet_all(extras):
    barrier = pltpu.get_barrier_semaphore()

    def greet(k, _):
        pl.semaphore_signal(
            barrier, inc=1, device_id=all_peer(k)[1], device_id_type=pl.DeviceIdType.MESH
        )
        return 0

    lax.fori_loop(1, FRAME, greet, 0)
    for extra in extras:
        pl.semaphore_signal(barrier, inc=1, device_id=extra, device_id_type=pl.DeviceIdType.MESH)


def part(ref, i, width):
    return ref.at[i, :, pl.ds(0, width)]


def all_copy(src, dst, sends, recvs, k, width):
    p, peer = all_peer(k)
    return pltpu.make_async_remote_copy(
        src_ref=part(src, p, width), dst_ref=part(dst, lax.axis_index("frame"), width),
        send_sem=sends.at[k], recv_sem=recvs.at[k],
        device_id=peer, device_id_type=pl.DeviceIdType.MESH,
    )


def start_all(src, dst, sends, recvs, own_sem, width):
    def start(k, _):
        all_copy(src, dst, sends, recvs, k, width).start()
        return 0

    lax.fori_loop(1, FRAME, start, 0)
    f = lax.axis_index("frame")
    pltpu.make_async_copy(part(src, f, width), part(dst, f, width), own_sem).start()


def wait_all(src, dst, sends, recvs, own_sem, width):
    f = lax.axis_index("frame")
    pltpu.make_async_copy(part(src, f, width), part(dst, f, width), own_sem).wait()

    def wait(k, _):
        all_copy(src, dst, sends, recvs, k, width).wait_recv()
        return 0

    lax.fori_loop(1, FRAME, wait, 0)


def drain_all(src, dst, sends, recvs, width):
    def drain(k, _):
        all_copy(src, dst, sends, recvs, k, width).wait_send()
        return 0

    lax.fori_loop(1, FRAME, drain, 0)


def dot(a, b):
    return jnp.dot(a, b, preferred_element_type=f32)


def dot_nt(a, b):
    return lax.dot_general(a, b, (((1,), (1,)), ((), ())), preferred_element_type=f32)


def dot_tn(a, b):
    return lax.dot_general(a, b, (((0,), (0,)), ((), ())), preferred_element_type=f32)


def iota(shape, dim):
    return lax.broadcasted_iota(jnp.int32, shape, dim)


def norm_terms(x):
    centered = x - jnp.mean(x, axis=-1, keepdims=True)
    rstd = lax.rsqrt(jnp.mean(centered * centered, axis=-1, keepdims=True) + EPS)
    return centered * rstd, rstd


def add_blocks(out, terms, count):
    def step(j, _):
        total = terms[0][j].astype(f32)
        for t in terms[1:]:
            total = total + t[j].astype(f32)
        out[j] = total.astype(out.dtype)
        return 0

    lax.fori_loop(0, count, step, 0)


def layer_kernel(
    clip, ids, gain, w_qkv_hbm, w_out_hbm, table_hbm, out, d_recv,
    x_v, ids_v, leave, r, w_qkv, w_out, w_other, table,
    x_s, ids_s, n_s, qkv_s, o_s, oo_s, p_s, dy_s, do_s, d_s, dn_s, dno_s, n_t, dy_t,
    g, sib, r1, l1, r2, l2, r3, l3, br1, bl1, br2, bl2, br3, bl3, bmr, bml, u, xr,
    load_sem, w_sem, w_send, w_recv, own_sem, all_send, all_recv, home_own, home_send, home_recv,
    o_send, o_recv, dn_send, dn_recv,
    core_send, core_recv, a_send, a_recv, b_send, b_recv, x_send, x_recv,
):
    xh, y, z, core = coordinates()
    chan = lax.axis_index("chan")
    tokens, width = x_v.shape
    cols = o_s.shape[0]
    n_heads = cols // HEAD_DIM
    half = tokens // 2
    scale = HEAD_DIM ** (-0.5)
    here = y * (1 - core) + z * core
    there = z * (1 - core) + y * core

    def ring(first, step):
        dy = step if first else 0
        dz = 0 if first else step
        ny = (y + (1 - core) * dy + core * dz + Y) % Y
        nz = (z + core * dy + (1 - core) * dz + Z) % Z
        return {"frame": frame_index(xh, ny, nz, core)}

    sibling = {"frame": frame_index(xh, y, z, 1 - core)}
    across = {"frame": frame_index(1 - xh, y, z, core)}
    partner = {"chan": 1 - chan}

    def remote(src, dst, send, recv, peer):
        return pltpu.make_async_remote_copy(
            src_ref=src, dst_ref=dst, send_sem=send, recv_sem=recv,
            device_id=peer, device_id_type=pl.DeviceIdType.MESH,
        )

    loads = [
        pltpu.make_async_copy(clip, x_v, load_sem.at[0]),
        pltpu.make_async_copy(ids, ids_v, load_sem.at[1]),
        pltpu.make_async_copy(w_out_hbm, w_out, load_sem.at[2]),
        pltpu.make_async_copy(w_qkv_hbm, w_qkv, load_sem.at[3]),
        pltpu.make_async_copy(table_hbm, table, load_sem.at[4]),
    ]
    for c in loads:
        c.start()
    greet_all((partner, across))

    loads[0].wait()
    loads[1].wait()

    def leaving(j, _):
        t = iota((128, tokens), 0) + j * 128
        source = (t % 2) * half + (t // 8) * 4 + t % 8 // 2
        pick = (iota((128, tokens), 1) == source).astype(bf16)
        to = pl.ds(j * 16, 16)
        leave[to, :, :width] = dot(pick, x_v[...]).reshape(16, 8, width).astype(bf16)
        leave[to, :, width:] = dot(pick, ids_v[...]).reshape(16, 8, 128).astype(bf16)
        return 0

    lax.fori_loop(0, 4, leaving, 0)
    loads[2].wait()
    pl.semaphore_wait(pltpu.get_barrier_semaphore(), FRAME + 1)

    rows_half = cols // 2
    own_rows = pl.ds(pl.multiple_of(core * rows_half, 16), rows_half)
    w_first = remote(w_out.at[own_rows], w_other.at[own_rows], w_send.at[0], w_recv.at[0], partner)
    w_first.start()
    start_all(leave, r, all_send, all_recv, own_sem, width + 128)
    w_first.wait_recv()
    w_second = remote(
        w_other.at[own_rows], w_other.at[own_rows], w_send.at[1], w_recv.at[1], sibling
    )
    w_second.start()
    w_second.wait_recv()
    wait_all(leave, r, all_send, all_recv, own_sem, width + 128)
    loads[3].wait()
    loads[4].wait()

    def rows(c):
        return pl.ds(pl.multiple_of(c * half, half), half)

    def swap_o(c):
        return remote(o_s.at[:, rows(c)], oo_s.at[:, rows(c)], o_send.at[c], o_recv.at[c], partner)

    def swap_dn(c):
        return remote(dn_s.at[rows(c)], dno_s.at[rows(c)], dn_send.at[c], dn_recv.at[c], partner)

    def patch(c, pp):
        return pl.ds(pl.multiple_of(c * half + pp * 128, 128), 128)

    def forward(c, _):
        t = iota((half, tokens), 0)
        source = (t % 128 // 2) * 8 + 2 * (2 * c + t // 128) + t % 2
        pick = (iota((half, tokens), 1) == source).astype(bf16)
        moved = dot(pick, r[...].reshape(tokens, width + 128))
        x = moved[:, :width]
        x_s[rows(c), :] = x.astype(bf16)
        ids_s[rows(c), :] = moved[:, width:]
        xhat, _ = norm_terms(x)
        normed = (xhat * gain[...].astype(f32)).astype(bf16)
        n_s[rows(c), :] = normed
        for i in range(3):
            qkv = dot_nt(w_qkv[i * cols : (i + 1) * cols, :], normed)
            for h in range(n_heads):
                qkv_s[i * n_heads + h, :, rows(c)] = qkv[
                    h * HEAD_DIM : (h + 1) * HEAD_DIM
                ].astype(bf16)
        for pp in range(2):
            at = patch(c, pp)
            for h in range(n_heads):
                scores = dot_tn(qkv_s[n_heads + h, :, at], qkv_s[h, :, at]) * scale
                expo = jnp.exp(scores - jnp.max(scores, axis=0, keepdims=True))
                probs = expo * (1.0 / jnp.sum(expo, axis=0, keepdims=True))
                p_s[(2 * c + pp) * n_heads + h] = probs
                o_s[h * HEAD_DIM : (h + 1) * HEAD_DIM, at] = dot(
                    qkv_s[2 * n_heads + h, :, at], probs.astype(bf16)
                ).astype(bf16)
        swap_o(c).start()
        return 0

    lax.fori_loop(0, 2, forward, 0)

    block = 8 * ROWS
    window = 384

    def columns(source, target):
        for k in range(width // block):
            start = min(k * block // 128, (width - window) // 128) * 128
            shape = (8 * PAD, window)
            at = iota(shape, 0)
            wanted = jnp.where(
                at % PAD < ROWS, k * block + (at // PAD) * ROWS + at % PAD - start, -1
            )
            pick = (iota(shape, 1) == wanted).astype(bf16)
            picked = dot_nt(pick, source[:, start : start + window])
            for j in range(8):
                cj, zj = j % 2, j // 2
                a, b = (k % Y, zj) if cj == 0 else (zj, k % Y)
                to = (((cj * 4 + a) * 2 + k // Y) * 4 + b) * PAD
                target[to : to + PAD, :] = picked[j * PAD : (j + 1) * PAD].astype(bf16)

    def targets(c, _):
        hi_lo = ids_s[rows(c), :]
        wanted = hi_lo[:, 0:1] * 32.0 + hi_lo[:, 1:2]
        n_old = table.shape[0]
        pick = (iota((half, n_old), 1).astype(f32) == wanted).astype(bf16)
        x_v[rows(c), :] = dot(pick, table[...]).astype(bf16)
        return 0

    lax.fori_loop(0, 2, targets, 0)
    columns(n_s, n_t)

    def backward(c, _):
        swap_o(c).wait_recv()
        branch = dot_tn(o_s[:, rows(c)], w_out[...]) + dot_tn(oo_s[:, rows(c)], w_other[...])
        d_y = (x_s[rows(c), :].astype(f32) + branch - x_v[rows(c), :].astype(f32)).astype(bf16)
        dy_s[rows(c), :] = d_y
        d_o = dot_nt(w_out[...], d_y)
        for h in range(n_heads):
            do_s[h] = d_o[h * HEAD_DIM : (h + 1) * HEAD_DIM].astype(bf16)
        for pp in range(2):
            at = patch(c, pp)
            for h in range(n_heads):
                probs = p_s[(2 * c + pp) * n_heads + h]
                d_oh = do_s[h, :, pp * 128 : (pp + 1) * 128]
                dprobs = dot_tn(qkv_s[2 * n_heads + h, :, at], d_oh)
                rowsum = jnp.sum(dprobs * probs, axis=0, keepdims=True)
                ds = (probs * (dprobs - rowsum) * scale).astype(bf16)
                lo, hi = h * HEAD_DIM, (h + 1) * HEAD_DIM
                d_s[lo:hi, at] = dot(qkv_s[n_heads + h, :, at], ds).astype(bf16)
                d_s[cols + lo : cols + hi, at] = dot_nt(qkv_s[h, :, at], ds).astype(bf16)
                d_s[2 * cols + lo : 2 * cols + hi, at] = dot_nt(d_oh, probs.astype(bf16)).astype(
                    bf16
                )
        dn_s[rows(c), :] = dot_tn(d_s[:, rows(c)], w_qkv[...]).astype(bf16)
        swap_dn(c).start()
        return 0

    lax.fori_loop(0, 2, backward, 0)
    columns(dy_s, dy_t)

    def weight_grads(m):
        m = (m + 2 * (1 - core)) % 4
        at = pl.ds(pl.multiple_of(m * 16 * PAD, 16 * PAD), 16 * PAD)
        to = pl.ds(m * 16, 16)
        g[to, :, : 3 * cols] = (
            dot_nt(n_t[at, :], d_s[...]).reshape(16, PAD, 3 * cols).astype(bf16)
        )
        g[to, :, 3 * cols :] = dot_nt(dy_t[at, :], o_s[...]).reshape(16, PAD, cols).astype(bf16)

    def piece(c, a, h):
        return g.at[pl.ds(((c * 4 + a) * 2 + h) * 4, 4)]

    order = ((2, 0), (2, 1), (1, 1), (3, 0), (1, 0), (3, 1), (0, 0), (0, 1))
    mine = [piece(core, (here + da) % 4, h) for da, h in order]
    theirs = [piece(1 - core, (there + da) % 4, h) for da, h in order]
    lax.fori_loop(0, 2, lambda m, _: (weight_grads(m), 0)[1], 0)
    swaps = []
    for i in range(8):
        c = remote(theirs[i], sib.at[i], core_send.at[i], core_recv.at[i], sibling)
        c.start()
        swaps.append(c)
    lax.fori_loop(2, 4, lambda m, _: (weight_grads(m), 0)[1], 0)

    def fold(i):
        swaps[i].wait_recv()
        add_blocks(mine[i], (mine[i], sib.at[i]), 4)

    copies = []

    def send(src, dst, k, peer, sends, recvs):
        c = remote(src, dst, sends.at[k], recvs.at[k], peer)
        c.start()
        copies.append(c)
        return c

    right, left = ring(True, 1), ring(True, -1)
    fold(0)
    c1r = send(mine[0], r1, 0, right, a_send, a_recv)
    fold(1)
    c1l = send(mine[1], l1, 1, left, a_send, a_recv)
    fold(2)
    c2r = send(mine[2], r2, 2, right, a_send, a_recv)
    fold(3)
    c2l = send(mine[3], l2, 3, left, a_send, a_recv)
    fold(4)
    fold(5)
    fold(6)
    fold(7)

    drain_all(leave, r, all_send, all_recv, width + 128)

    def finish(c, _):
        swap_dn(c).wait_recv()
        dn = dn_s[rows(c), :].astype(f32) + dno_s[rows(c), :].astype(f32)
        xhat, rstd = norm_terms(x_s[rows(c), :].astype(f32))
        gs = dn * gain[...].astype(f32)
        back = rstd * (
            gs
            - jnp.mean(gs, axis=-1, keepdims=True)
            - xhat * jnp.mean(gs * xhat, axis=-1, keepdims=True)
        )
        x_v[rows(c), :] = (dy_s[rows(c), :].astype(f32) + back).astype(bf16)
        return 0

    lax.fori_loop(0, 2, finish, 0)

    def to_home(j, _):
        t = iota((128, tokens), 0) + j * 128
        source = (t % 8 // 2) * 128 + 2 * (t // 8) + t % 2
        pick = (iota((128, tokens), 1) == source).astype(bf16)
        leave[pl.ds(j * 16, 16), :, :width] = (
            dot(pick, x_v[...]).reshape(16, 8, width).astype(bf16)
        )
        return 0

    lax.fori_loop(0, 4, to_home, 0)
    start_all(leave, d_recv, home_send, home_recv, home_own, width)

    c1r.wait_recv()
    add_blocks(mine[4], (mine[4], r1), 4)
    c3r = send(mine[4], r3, 4, right, a_send, a_recv)
    c1l.wait_recv()
    add_blocks(mine[5], (mine[5], l1), 4)
    c3l = send(mine[5], l3, 5, left, a_send, a_recv)
    c2l.wait_recv()
    c3r.wait_recv()
    add_blocks(mine[6], (mine[6], r3, l2), 4)
    c2r.wait_recv()
    c3l.wait_recv()
    add_blocks(mine[7], (mine[7], r2, l3), 4)

    right, left = ring(False, 1), ring(False, -1)
    at = lambda h, d: g.at[((core * 4 + here) * 2 + h) * 4 + (there + d) % 4]
    d1r = send(at(0, 2), br1, 0, right, b_send, b_recv)
    d1l = send(at(1, 2), bl1, 1, left, b_send, b_recv)
    d2r = send(at(1, 1), br2, 2, right, b_send, b_recv)
    d2l = send(at(0, 3), bl2, 3, left, b_send, b_recv)
    d1r.wait_recv()
    bmr[...] = (at(0, 1)[...].astype(f32) + br1[...].astype(f32)).astype(bf16)
    d3r = send(bmr, br3, 4, right, b_send, b_recv)
    d1l.wait_recv()
    bml[...] = (at(1, 3)[...].astype(f32) + bl1[...].astype(f32)).astype(bf16)
    d3l = send(bml, bl3, 5, left, b_send, b_recv)
    d2l.wait_recv()
    d3r.wait_recv()
    u[0] = (at(0, 0)[...].astype(f32) + br3[...].astype(f32) + bl2[...].astype(f32)).astype(bf16)
    d2r.wait_recv()
    d3l.wait_recv()
    u[1] = (at(1, 0)[...].astype(f32) + br2[...].astype(f32) + bl3[...].astype(f32)).astype(bf16)

    e = remote(u.at[1 - xh], xr, x_send, x_recv, across)
    e.start()
    e.wait_recv()
    out[...] = u[xh].astype(f32) + xr[...].astype(f32)
    wait_all(leave, d_recv, home_send, home_recv, home_own, width)

    e.wait_send()
    w_first.wait_send()
    w_second.wait_send()
    for c in swaps:
        c.wait_send()
    for c in copies:
        c.wait_send()
    for c in range(2):
        swap_o(c).wait_send()
        swap_dn(c).wait_send()
    drain_all(leave, d_recv, home_send, home_recv, width)


def layer(clip, ids, gain, w_qkv, w_out, table):
    tokens, width = clip.shape
    cols = w_out.shape[0]
    n_heads = cols // HEAD_DIM
    each = tokens // FRAME
    vmem = pl.BlockSpec(memory_space=pltpu.VMEM)
    anywhere = pl.BlockSpec(memory_space=pl.ANY)
    wide = pltpu.VMEM((tokens, width), bf16)
    narrow = pltpu.VMEM((cols, tokens), bf16)
    piece = pltpu.VMEM((4, PAD, 4 * cols), bf16)
    block = pltpu.VMEM((PAD, 4 * cols), bf16)
    carry = pltpu.VMEM((FRAME, each, width + 128), bf16)
    dma = pltpu.SemaphoreType.DMA
    return pl.pallas_call(
        layer_kernel,
        out_shape=[
            jax.ShapeDtypeStruct((PAD, 4 * cols), f32),
            jax.ShapeDtypeStruct((FRAME, each, width), bf16),
        ],
        in_specs=[anywhere, anywhere, vmem, anywhere, anywhere, anywhere],
        out_specs=[vmem, vmem],
        scratch_shapes=[
            wide,
            pltpu.VMEM((tokens, 128), bf16),
            carry,
            carry,
            pltpu.VMEM((3 * cols, width), bf16),
            pltpu.VMEM((cols, width), bf16),
            pltpu.VMEM((cols, width), bf16),
            pltpu.VMEM(table.shape, bf16),
            wide,
            pltpu.VMEM((tokens, 128), f32),
            wide,
            pltpu.VMEM((3 * n_heads, HEAD_DIM, tokens), bf16),
            narrow,
            narrow,
            pltpu.VMEM((tokens // 128 * n_heads, 128, 128), f32),
            wide,
            pltpu.VMEM((n_heads, HEAD_DIM, tokens // 2), bf16),
            pltpu.VMEM((3 * cols, tokens), bf16),
            wide,
            wide,
            pltpu.VMEM((FRAME * PAD, tokens), bf16),
            pltpu.VMEM((FRAME * PAD, tokens), bf16),
            pltpu.VMEM((FRAME, PAD, 4 * cols), bf16),
            pltpu.VMEM((8, 4, PAD, 4 * cols), bf16),
        ]
        + [piece] * 6
        + [block] * 8
        + [pltpu.VMEM((2, PAD, 4 * cols), bf16), block]
        + [
            dma((5,)), dma, dma((2,)), dma((2,)),
            dma, dma((FRAME,)), dma((FRAME,)), dma, dma((FRAME,)), dma((FRAME,)),
            dma((2,)), dma((2,)), dma((2,)), dma((2,)),
            dma((8,)), dma((8,)), dma((6,)), dma((6,)), dma((6,)), dma((6,)), dma, dma,
        ],
        compiler_params=pltpu.CompilerParams(
            collective_id=0, has_side_effects=True, vmem_limit_bytes=VMEM_LIMIT
        ),
        name="layer",
    )(clip, ids, gain, w_qkv, w_out, table)


def body(clip, gain, w_qkv, w_out, old_table, target_ids):
    frames_here, patches, width = clip.shape
    cols = w_qkv.shape[2]
    tokens = frames_here * patches

    ids = target_ids.reshape(tokens, 1)
    lane = iota((tokens, 128), 1)
    ids = jnp.where(lane == 0, ids // 32, jnp.where(lane == 1, ids % 32, 0)).astype(bf16)
    reduced, returned = layer(
        clip.reshape(tokens, width),
        ids,
        gain.reshape(1, width),
        w_qkv.transpose(0, 2, 1).reshape(3 * cols, width),
        w_out,
        old_table,
    )

    t = iota((tokens, tokens), 0)
    source = (t % patches // 4) * 8 + (t % 4) * 2 + t // patches
    pick = iota((tokens, tokens), 1) == source
    d_clip = dot(pick.astype(bf16), returned.reshape(tokens, width)).astype(bf16)
    reduced = reduced[:ROWS].reshape(ROWS, 4, cols)
    return (
        d_clip.reshape(frames_here, patches, width),
        reduced[:, :3].transpose(1, 0, 2),
        reduced[:, 3].T,
    )


def solution(mesh):
    return jax.shard_map(
        body,
        mesh=mesh,
        in_specs=(
            P("frame", None, None),
            P(),
            P(None, None, "chan"),
            P("chan", None),
            P(),
            P("frame", None),
        ),
        out_specs=(P("frame", None, None), P(None, "frame", "chan"), P("chan", "frame")),
        check_vma=False,
    )
```

```python
import functools

import jax
import jax.numpy as jnp
from jax import lax
from jax.experimental import pallas as pl
from jax.experimental.pallas import tpu as pltpu
from jax.sharding import PartitionSpec as P

HEAD_DIM = 88
EPS = 1e-05
VMEM_LIMIT = 63 * 2**20
XH, Y, Z, CORE = 2, 4, 4, 2
FRAME = XH * Y * Z * CORE
CHAN = 2
ROWS = 22
PAD = 24

f32 = jnp.float32
bf16 = jnp.bfloat16


def frame_index(xh, y, z, core):
    return ((xh * Y + y) * Z + z) * CORE + core


def coordinates():
    f = lax.axis_index("frame")
    return f // (Y * Z * CORE), (f // (Z * CORE)) % Y, (f // CORE) % Z, f % CORE


def all_peer(k):
    f = lax.axis_index("frame")
    chan = lax.axis_index("chan")
    p = (f + k) % FRAME
    far = (p // (FRAME // 2) + f // (FRAME // 2)) % 2
    return p, {"frame": p, "chan": (chan + far) % 2}


def greet_all():
    barrier = pltpu.get_barrier_semaphore()
    me = lax.axis_index("frame") * CHAN + lax.axis_index("chan")

    def greet(k, _):
        other = (me + k) % (FRAME * CHAN)
        pl.semaphore_signal(
            barrier, inc=1, device_id={"frame": other // CHAN, "chan": other % CHAN},
            device_id_type=pl.DeviceIdType.MESH,
        )
        return 0

    lax.fori_loop(1, FRAME * CHAN, greet, 0)


def part(ref, i, width):
    return ref.at[i, :, pl.ds(0, width)]


def all_copy(src, dst, sends, recvs, k, width):
    p, peer = all_peer(k)
    return pltpu.make_async_remote_copy(
        src_ref=part(src, p, width), dst_ref=part(dst, lax.axis_index("frame"), width),
        send_sem=sends.at[k], recv_sem=recvs.at[k],
        device_id=peer, device_id_type=pl.DeviceIdType.MESH,
    )


def start_all(src, dst, sends, recvs, own_sem, width):
    def start(k, _):
        all_copy(src, dst, sends, recvs, k, width).start()
        return 0

    lax.fori_loop(1, FRAME, start, 0)
    f = lax.axis_index("frame")
    pltpu.make_async_copy(part(src, f, width), part(dst, f, width), own_sem).start()


def wait_all(src, dst, sends, recvs, own_sem, width):
    f = lax.axis_index("frame")
    pltpu.make_async_copy(part(src, f, width), part(dst, f, width), own_sem).wait()

    def wait(k, _):
        all_copy(src, dst, sends, recvs, k, width).wait_recv()
        return 0

    lax.fori_loop(1, FRAME, wait, 0)


def drain_all(src, dst, sends, recvs, width):
    def drain(k, _):
        all_copy(src, dst, sends, recvs, k, width).wait_send()
        return 0

    lax.fori_loop(1, FRAME, drain, 0)


def dot(a, b):
    return jnp.dot(a, b, preferred_element_type=f32)


def dot_nt(a, b):
    return lax.dot_general(a, b, (((1,), (1,)), ((), ())), preferred_element_type=f32)


def dot_tn(a, b):
    return lax.dot_general(a, b, (((0,), (0,)), ((), ())), preferred_element_type=f32)


def alone(run):
    def once(i, _):
        run()
        return 0

    lax.fori_loop(0, lax.axis_index("chan") // 2 + 1, once, 0)


def iota(shape, dim):
    return lax.broadcasted_iota(jnp.int32, shape, dim)


def norm_terms(x):
    centered = x - jnp.mean(x, axis=-1, keepdims=True)
    rstd = lax.rsqrt(jnp.mean(centered * centered, axis=-1, keepdims=True) + EPS)
    return centered * rstd, rstd


def add_blocks(out, terms, count):
    def step(j, _):
        total = terms[0][j].astype(f32)
        for t in terms[1:]:
            total = total + t[j].astype(f32)
        out[j] = total.astype(out.dtype)
        return 0

    lax.fori_loop(0, count, step, 0)


def layer_kernel(
    clip, ids, gain, w_qkv_hbm, w_out_hbm, table_hbm, out, d_recv,
    x_v, ids_v, leave, r, w_qkv, w_out, w_other, table,
    x_s, ids_s, n_s, qkv_s, o_s, oo_s, p_s, dy_s, do_s, ds_s, d_s, dn_s, dno_s, n_t, dy_t,
    g, sib, r1, l1, r2, l2, r3, l3, br1, bl1, br2, bl2, br3, bl3, bmr, bml, u, xr,
    load_sem, w_sem, w_send, w_recv, own_sem, all_send, all_recv, home_own, home_send, home_recv,
    o_send, o_recv, dn_send, dn_recv,
    core_send, core_recv, a_send, a_recv, b_send, b_recv, x_send, x_recv,
):
    xh, y, z, core = coordinates()
    chan = lax.axis_index("chan")
    tokens, width = x_v.shape
    cols = o_s.shape[0]
    n_heads = cols // HEAD_DIM
    half = tokens // 2
    scale = HEAD_DIM ** (-0.5)
    kept = (xh + chan + core) % 2
    here = y * (1 - core) + z * core
    there = z * (1 - core) + y * core

    def ring(first, step):
        dy = step if first else 0
        dz = 0 if first else step
        ny = (y + (1 - core) * dy + core * dz + Y) % Y
        nz = (z + core * dy + (1 - core) * dz + Z) % Z
        return {"frame": frame_index(xh, ny, nz, core)}

    sibling = {"frame": frame_index(xh, y, z, 1 - core)}
    across = {"frame": frame_index(1 - xh, y, z, core)}
    partner = {"chan": 1 - chan}

    def remote(src, dst, send, recv, peer):
        return pltpu.make_async_remote_copy(
            src_ref=src, dst_ref=dst, send_sem=send, recv_sem=recv,
            device_id=peer, device_id_type=pl.DeviceIdType.MESH,
        )

    loads = [
        pltpu.make_async_copy(clip, x_v, load_sem.at[0]),
        pltpu.make_async_copy(ids, ids_v, load_sem.at[1]),
        pltpu.make_async_copy(w_out_hbm, w_out, load_sem.at[2]),
        pltpu.make_async_copy(w_qkv_hbm, w_qkv, load_sem.at[3]),
        pltpu.make_async_copy(table_hbm, table, load_sem.at[4]),
    ]
    for c in loads:
        c.start()
    greet_all()

    loads[0].wait()
    loads[1].wait()

    def leaving(j, _):
        t = iota((128, tokens), 0) + j * 128
        source = (t % 2) * half + (t // 8) * 4 + t % 8 // 2
        pick = (iota((128, tokens), 1) == source).astype(bf16)
        to = pl.ds(j * 16, 16)
        leave[to, :, :width] = dot(pick, x_v[...]).reshape(16, 8, width).astype(bf16)
        leave[to, :, width:] = dot(pick, ids_v[...]).reshape(16, 8, 128).astype(bf16)
        return 0

    lax.fori_loop(0, 4, leaving, 0)
    loads[2].wait()
    pl.semaphore_wait(pltpu.get_barrier_semaphore(), FRAME * CHAN - 1)

    rows_half = cols // 2
    own_rows = pl.ds(pl.multiple_of(core * rows_half, 16), rows_half)
    w_first = remote(w_out.at[own_rows], w_other.at[own_rows], w_send.at[0], w_recv.at[0], partner)
    w_first.start()
    start_all(leave, r, all_send, all_recv, own_sem, width + 128)
    wait_all(leave, r, all_send, all_recv, own_sem, width + 128)
    loads[3].wait()
    loads[4].wait()

    def rows(c):
        return pl.ds(pl.multiple_of(c * half, half), half)

    def swap_o(c):
        return remote(o_s.at[:, rows(c)], oo_s.at[:, rows(c)], o_send.at[c], o_recv.at[c], partner)

    def swap_dn(c):
        two = pl.ds(2 * c, 2)
        return remote(
            dn_s.at[two, 1 - kept], dno_s.at[two], dn_send.at[c], dn_recv.at[c], partner
        )

    def patch(c, pp):
        return pl.ds(pl.multiple_of(c * half + pp * 128, 128), 128)

    def forward(c, _):
        t = iota((half, tokens), 0)
        source = (t % 128 // 2) * 8 + 2 * (2 * c + t // 128) + t % 2
        pick = (iota((half, tokens), 1) == source).astype(bf16)
        moved = dot(pick, r[...].reshape(tokens, width + 128))
        x = moved[:, :width]
        x_s[rows(c), :] = x.astype(bf16)
        ids_s[rows(c), :] = moved[:, width:]
        xhat, _ = norm_terms(x)
        normed = (xhat * gain[...].astype(f32)).astype(bf16)
        n_s[rows(c), :] = normed
        for i in range(3):
            qkv = dot_nt(w_qkv[i * cols : (i + 1) * cols, :], normed)
            for h in range(n_heads):
                qkv_s[i * n_heads + h, :, rows(c)] = qkv[
                    h * HEAD_DIM : (h + 1) * HEAD_DIM
                ].astype(bf16)
        alone(functools.partial(forward_heads, c))
        swap_o(c).start()
        return 0

    def forward_heads(c):
        for pp in range(2):
            at = patch(c, pp)
            for h in range(n_heads):
                scores = dot_tn(qkv_s[n_heads + h, :, at], qkv_s[h, :, at]) * scale
                expo = jnp.exp(scores - jnp.max(scores, axis=0, keepdims=True))
                probs = expo * (1.0 / jnp.sum(expo, axis=0, keepdims=True))
                p_s[(2 * c + pp) * n_heads + h] = probs
                o_s[h * HEAD_DIM : (h + 1) * HEAD_DIM, at] = dot(
                    qkv_s[2 * n_heads + h, :, at], probs.astype(bf16)
                ).astype(bf16)

    lax.fori_loop(0, 2, forward, 0)

    block = 8 * ROWS
    window = 384

    def columns(source, target):
        for k in range(width // block):
            start = min(k * block // 128, (width - window) // 128) * 128
            shape = (8 * PAD, window)
            at = iota(shape, 0)
            wanted = jnp.where(
                at % PAD < ROWS, k * block + (at // PAD) * ROWS + at % PAD - start, -1
            )
            pick = (iota(shape, 1) == wanted).astype(bf16)
            picked = dot_nt(pick, source[:, start : start + window])
            for j in range(8):
                cj, zj = j % 2, j // 2
                a, b = (k % Y, zj) if cj == 0 else (zj, k % Y)
                to = (((cj * 4 + a) * 2 + k // Y) * 4 + b) * PAD
                target[to : to + PAD, :] = picked[j * PAD : (j + 1) * PAD].astype(bf16)

    def targets(c, _):
        hi_lo = ids_s[rows(c), :]
        wanted = hi_lo[:, 0:1] * 32.0 + hi_lo[:, 1:2]
        n_old = table.shape[0]
        pick = (iota((half, n_old), 1).astype(f32) == wanted).astype(bf16)
        x_v[rows(c), :] = dot(pick, table[...]).astype(bf16)
        return 0

    w_first.wait_recv()
    w_second = remote(
        w_other.at[own_rows], w_other.at[own_rows], w_send.at[1], w_recv.at[1], sibling
    )
    w_second.start()
    lax.fori_loop(0, 2, targets, 0)
    columns(n_s, n_t)
    w_second.wait_recv()

    def backward(c, _):
        swap_o(c).wait_recv()
        branch = dot_tn(o_s[:, rows(c)], w_out[...]) + dot_tn(oo_s[:, rows(c)], w_other[...])
        d_y = (x_s[rows(c), :].astype(f32) + branch - x_v[rows(c), :].astype(f32)).astype(bf16)
        dy_s[rows(c), :] = d_y
        d_o = dot_nt(w_out[...], d_y)
        for h in range(n_heads):
            do_s[h] = d_o[h * HEAD_DIM : (h + 1) * HEAD_DIM].astype(bf16)
        alone(functools.partial(score_heads, c))
        alone(functools.partial(value_heads, c))
        dn = dot_tn(d_s[:, rows(c)], w_qkv[...])
        dn_s[pl.ds(2 * c, 2)] = dn.reshape(2, 2, 64, width).astype(bf16)
        swap_dn(c).start()
        return 0

    def score_heads(c):
        for pp in range(2):
            at = patch(c, pp)
            for h in range(n_heads):
                probs = p_s[(2 * c + pp) * n_heads + h]
                d_oh = do_s[h, :, pp * 128 : (pp + 1) * 128]
                dprobs = dot_tn(qkv_s[2 * n_heads + h, :, at], d_oh)
                rowsum = jnp.sum(dprobs * probs, axis=0, keepdims=True)
                ds = (probs * (dprobs - rowsum) * scale).astype(bf16)
                ds_s[pp * n_heads + h] = ds
                d_s[h * HEAD_DIM : (h + 1) * HEAD_DIM, at] = dot(
                    qkv_s[n_heads + h, :, at], ds
                ).astype(bf16)

    def value_heads(c):
        for pp in range(2):
            at = patch(c, pp)
            for h in range(n_heads):
                lo, hi = h * HEAD_DIM, (h + 1) * HEAD_DIM
                probs = p_s[(2 * c + pp) * n_heads + h].astype(bf16)
                d_oh = do_s[h, :, pp * 128 : (pp + 1) * 128]
                d_s[cols + lo : cols + hi, at] = dot_nt(
                    qkv_s[h, :, at], ds_s[pp * n_heads + h]
                ).astype(bf16)
                d_s[2 * cols + lo : 2 * cols + hi, at] = dot_nt(d_oh, probs).astype(bf16)

    lax.fori_loop(0, 2, backward, 0)
    columns(dy_s, dy_t)

    def weight_grads(m):
        m = (m + 2 * (1 - core)) % 4
        at = pl.ds(pl.multiple_of(m * 16 * PAD, 16 * PAD), 16 * PAD)
        to = pl.ds(m * 16, 16)
        g[to, :, : 3 * cols] = (
            dot_nt(n_t[at, :], d_s[...]).reshape(16, PAD, 3 * cols).astype(bf16)
        )
        g[to, :, 3 * cols :] = dot_nt(dy_t[at, :], o_s[...]).reshape(16, PAD, cols).astype(bf16)

    def piece(c, a, h):
        return g.at[pl.ds(((c * 4 + a) * 2 + h) * 4, 4)]

    order = ((2, 0), (2, 1), (1, 1), (3, 0), (1, 0), (3, 1), (0, 0), (0, 1))
    mine = [piece(core, (here + da) % 4, h) for da, h in order]
    theirs = [piece(1 - core, (there + da) % 4, h) for da, h in order]
    lax.fori_loop(0, 2, lambda m, _: (weight_grads(m), 0)[1], 0)
    swaps = []
    for i in range(8):
        c = remote(theirs[i], sib.at[i], core_send.at[i], core_recv.at[i], sibling)
        c.start()
        swaps.append(c)
    lax.fori_loop(2, 4, lambda m, _: (weight_grads(m), 0)[1], 0)

    def fold(i):
        swaps[i].wait_recv()
        add_blocks(mine[i], (mine[i], sib.at[i]), 4)

    copies = []

    def send(src, dst, k, peer, sends, recvs):
        c = remote(src, dst, sends.at[k], recvs.at[k], peer)
        c.start()
        copies.append(c)
        return c

    right, left = ring(True, 1), ring(True, -1)
    fold(0)
    c1r = send(mine[0], r1, 0, right, a_send, a_recv)
    fold(1)
    c1l = send(mine[1], l1, 1, left, a_send, a_recv)
    fold(2)
    c2r = send(mine[2], r2, 2, right, a_send, a_recv)
    fold(3)
    c2l = send(mine[3], l2, 3, left, a_send, a_recv)
    fold(4)
    fold(5)
    fold(6)
    fold(7)

    drain_all(leave, r, all_send, all_recv, width + 128)

    def finish(p, _):
        @pl.when(p % 2 == 0)
        def _():
            swap_dn(p // 2).wait_recv()

        at = pl.ds(pl.multiple_of(p * 128 + kept * 64, 64), 64)
        dn = dn_s[p, kept].astype(f32) + dno_s[p].astype(f32)
        xhat, rstd = norm_terms(x_s[at, :].astype(f32))
        gs = dn * gain[...].astype(f32)
        back = rstd * (
            gs
            - jnp.mean(gs, axis=-1, keepdims=True)
            - xhat * jnp.mean(gs * xhat, axis=-1, keepdims=True)
        )
        x_v[pl.ds(pl.multiple_of(p * 64, 64), 64), :] = (
            dy_s[at, :].astype(f32) + back
        ).astype(bf16)
        return 0

    lax.fori_loop(0, 4, finish, 0)

    def to_home(j, _):
        t = iota((128, half), 0) + j * 128
        source = (t % 8 // 2) * 64 + 2 * (t // 8) + t % 2
        pick = (iota((128, half), 1) == source).astype(bf16)
        leave[pl.ds(j * 16, 16), :, :width] = (
            dot(pick, x_v[pl.ds(0, half), :]).reshape(16, 8, width).astype(bf16)
        )
        return 0

    lax.fori_loop(0, 2, to_home, 0)

    f = lax.axis_index("frame")
    own = (kept + xh) % 2 == 0

    def home_copy(k, c):
        q = (f + k) % (FRAME // 2)
        return pltpu.make_async_remote_copy(
            src_ref=part(leave, q, width), dst_ref=d_recv.at[f],
            send_sem=home_send.at[2 * k + c], recv_sem=home_recv.at[2 * k + c],
            device_id={"frame": kept * (FRAME // 2) + q, "chan": (chan + c) % 2},
            device_id_type=pl.DeviceIdType.MESH,
        )

    home_local = pltpu.make_async_copy(part(leave, f % (FRAME // 2), width), d_recv.at[f], home_own)

    def home_each(run, run_own):
        @pl.when(own)
        def _():
            run_own()

        @pl.when(jnp.logical_not(own))
        def _():
            run(home_copy(0, 0))

        run(home_copy(0, 1))

        def step(k, _):
            run(home_copy(k, 0))
            run(home_copy(k, 1))
            return 0

        lax.fori_loop(1, FRAME // 2, step, 0)

    home_each(lambda c: c.start(), home_local.start)

    c1r.wait_recv()
    add_blocks(mine[4], (mine[4], r1), 4)
    c3r = send(mine[4], r3, 4, right, a_send, a_recv)
    c1l.wait_recv()
    add_blocks(mine[5], (mine[5], l1), 4)
    c3l = send(mine[5], l3, 5, left, a_send, a_recv)
    c2l.wait_recv()
    c3r.wait_recv()
    add_blocks(mine[6], (mine[6], r3, l2), 4)
    c2r.wait_recv()
    c3l.wait_recv()
    add_blocks(mine[7], (mine[7], r2, l3), 4)

    right, left = ring(False, 1), ring(False, -1)
    at = lambda h, d: g.at[((core * 4 + here) * 2 + h) * 4 + (there + d) % 4]
    d1r = send(at(0, 2), br1, 0, right, b_send, b_recv)
    d1l = send(at(1, 2), bl1, 1, left, b_send, b_recv)
    d2r = send(at(1, 1), br2, 2, right, b_send, b_recv)
    d2l = send(at(0, 3), bl2, 3, left, b_send, b_recv)
    d1r.wait_recv()
    bmr[...] = (at(0, 1)[...].astype(f32) + br1[...].astype(f32)).astype(bf16)
    d3r = send(bmr, br3, 4, right, b_send, b_recv)
    d1l.wait_recv()
    bml[...] = (at(1, 3)[...].astype(f32) + bl1[...].astype(f32)).astype(bf16)
    d3l = send(bml, bl3, 5, left, b_send, b_recv)
    d2l.wait_recv()
    d3r.wait_recv()
    u[0] = (at(0, 0)[...].astype(f32) + br3[...].astype(f32) + bl2[...].astype(f32)).astype(bf16)
    d2r.wait_recv()
    d3l.wait_recv()
    u[1] = (at(1, 0)[...].astype(f32) + br2[...].astype(f32) + bl3[...].astype(f32)).astype(bf16)

    e = remote(u.at[1 - xh], xr, x_send, x_recv, across)
    e.start()
    e.wait_recv()
    out[...] = u[xh].astype(f32) + xr[...].astype(f32)
    home_each(lambda c: c.wait_recv(), home_local.wait)

    e.wait_send()
    w_first.wait_send()
    w_second.wait_send()
    for c in swaps:
        c.wait_send()
    for c in copies:
        c.wait_send()
    for c in range(2):
        swap_o(c).wait_send()
        swap_dn(c).wait_send()
    home_each(lambda c: c.wait_send(), lambda: None)


def layer(clip, ids, gain, w_qkv, w_out, table):
    tokens, width = clip.shape
    cols = w_out.shape[0]
    n_heads = cols // HEAD_DIM
    each = tokens // FRAME
    vmem = pl.BlockSpec(memory_space=pltpu.VMEM)
    anywhere = pl.BlockSpec(memory_space=pl.ANY)
    wide = pltpu.VMEM((tokens, width), bf16)
    narrow = pltpu.VMEM((cols, tokens), bf16)
    piece = pltpu.VMEM((4, PAD, 4 * cols), bf16)
    block = pltpu.VMEM((PAD, 4 * cols), bf16)
    carry = pltpu.VMEM((FRAME, each, width + 128), bf16)
    dma = pltpu.SemaphoreType.DMA
    return pl.pallas_call(
        layer_kernel,
        out_shape=[
            jax.ShapeDtypeStruct((PAD, 4 * cols), f32),
            jax.ShapeDtypeStruct((FRAME, each, width), bf16),
        ],
        in_specs=[anywhere, anywhere, vmem, anywhere, anywhere, anywhere],
        out_specs=[vmem, vmem],
        scratch_shapes=[
            wide,
            pltpu.VMEM((tokens, 128), bf16),
            carry,
            carry,
            pltpu.VMEM((3 * cols, width), bf16),
            pltpu.VMEM((cols, width), bf16),
            pltpu.VMEM((cols, width), bf16),
            pltpu.VMEM(table.shape, bf16),
            wide,
            pltpu.VMEM((tokens, 128), f32),
            wide,
            pltpu.VMEM((3 * n_heads, HEAD_DIM, tokens), bf16),
            narrow,
            narrow,
            pltpu.VMEM((tokens // 128 * n_heads, 128, 128), f32),
            wide,
            pltpu.VMEM((n_heads, HEAD_DIM, tokens // 2), bf16),
            pltpu.VMEM((2 * n_heads, 128, 128), bf16),
            pltpu.VMEM((3 * cols, tokens), bf16),
            pltpu.VMEM((4, 2, 64, width), bf16),
            pltpu.VMEM((4, 64, width), bf16),
            pltpu.VMEM((FRAME * PAD, tokens), bf16),
            pltpu.VMEM((FRAME * PAD, tokens), bf16),
            pltpu.VMEM((FRAME, PAD, 4 * cols), bf16),
            pltpu.VMEM((8, 4, PAD, 4 * cols), bf16),
        ]
        + [piece] * 6
        + [block] * 8
        + [pltpu.VMEM((2, PAD, 4 * cols), bf16), block]
        + [
            dma((5,)), dma, dma((2,)), dma((2,)),
            dma, dma((FRAME,)), dma((FRAME,)), dma, dma((FRAME,)), dma((FRAME,)),
            dma((2,)), dma((2,)), dma((2,)), dma((2,)),
            dma((8,)), dma((8,)), dma((6,)), dma((6,)), dma((6,)), dma((6,)), dma, dma,
        ],
        compiler_params=pltpu.CompilerParams(
            collective_id=0, has_side_effects=True, vmem_limit_bytes=VMEM_LIMIT
        ),
        name="layer",
    )(clip, ids, gain, w_qkv, w_out, table)


def body(clip, gain, w_qkv, w_out, old_table, target_ids):
    frames_here, patches, width = clip.shape
    cols = w_qkv.shape[2]
    tokens = frames_here * patches

    ids = target_ids.reshape(tokens, 1)
    lane = iota((tokens, 128), 1)
    ids = jnp.where(lane == 0, ids // 32, jnp.where(lane == 1, ids % 32, 0)).astype(bf16)
    reduced, returned = layer(
        clip.reshape(tokens, width),
        ids,
        gain.reshape(1, width),
        w_qkv.transpose(0, 2, 1).reshape(3 * cols, width),
        w_out,
        old_table,
    )

    t = iota((tokens, tokens), 0)
    source = (t % patches // 4) * 8 + (t % 4) * 2 + t // patches
    pick = iota((tokens, tokens), 1) == source
    d_clip = dot(pick.astype(bf16), returned.reshape(tokens, width)).astype(bf16)
    reduced = reduced[:ROWS].reshape(ROWS, 4, cols)
    return (
        d_clip.reshape(frames_here, patches, width),
        reduced[:, :3].transpose(1, 0, 2),
        reduced[:, 3].T,
    )


def solution(mesh):
    return jax.shard_map(
        body,
        mesh=mesh,
        in_specs=(
            P("frame", None, None),
            P(),
            P(None, None, "chan"),
            P("chan", None),
            P(),
            P("frame", None),
        ),
        out_specs=(P("frame", None, None), P(None, "frame", "chan"), P("chan", "frame")),
        check_vma=False,
    )
```

```python
import functools

import jax
import jax.numpy as jnp
from jax import lax
from jax.experimental import pallas as pl
from jax.experimental.pallas import tpu as pltpu
from jax.sharding import PartitionSpec as P

HEAD_DIM = 88
EPS = 1e-05
VMEM_LIMIT = 63 * 2**20
XH, Y, Z, CORE = 2, 4, 4, 2
FRAME = XH * Y * Z * CORE
CHAN = 2
ROWS = 22
PAD = 24

f32 = jnp.float32
bf16 = jnp.bfloat16


def frame_index(xh, y, z, core):
    return ((xh * Y + y) * Z + z) * CORE + core


def coordinates():
    f = lax.axis_index("frame")
    return f // (Y * Z * CORE), (f // (Z * CORE)) % Y, (f // CORE) % Z, f % CORE


def all_peer(k):
    f = lax.axis_index("frame")
    chan = lax.axis_index("chan")
    p = (f + k) % FRAME
    far = (p // (FRAME // 2) + f // (FRAME // 2)) % 2
    return p, {"frame": p, "chan": (chan + far) % 2}


def greet(k):
    me = lax.axis_index("frame") * CHAN + lax.axis_index("chan")
    other = (me + k) % (FRAME * CHAN)
    pl.semaphore_signal(
        pltpu.get_barrier_semaphore(),
        inc=1,
        device_id={"frame": other // CHAN, "chan": other % CHAN},
        device_id_type=pl.DeviceIdType.MESH,
    )


def part(ref, i, width):
    return ref.at[i, :, pl.ds(0, width)]


def all_copy(src, dst, sends, recvs, k, width):
    p, peer = all_peer(k)
    return pltpu.make_async_remote_copy(
        src_ref=part(src, p, width), dst_ref=part(dst, lax.axis_index("frame"), width),
        send_sem=sends.at[k], recv_sem=recvs.at[k],
        device_id=peer, device_id_type=pl.DeviceIdType.MESH,
    )


def start_all(src, dst, sends, recvs, own_sem, width):
    def start(k, _):
        all_copy(src, dst, sends, recvs, k, width).start()
        return 0

    lax.fori_loop(1, FRAME, start, 0)
    f = lax.axis_index("frame")
    pltpu.make_async_copy(part(src, f, width), part(dst, f, width), own_sem).start()


def wait_all(src, dst, sends, recvs, own_sem, width):
    f = lax.axis_index("frame")
    pltpu.make_async_copy(part(src, f, width), part(dst, f, width), own_sem).wait()

    def wait(k, _):
        all_copy(src, dst, sends, recvs, k, width).wait_recv()
        return 0

    lax.fori_loop(1, FRAME, wait, 0)


def drain_all(src, dst, sends, recvs, width):
    def drain(k, _):
        all_copy(src, dst, sends, recvs, k, width).wait_send()
        return 0

    lax.fori_loop(1, FRAME, drain, 0)


def dot(a, b):
    return jnp.dot(a, b, preferred_element_type=f32)


def dot_nt(a, b):
    return lax.dot_general(a, b, (((1,), (1,)), ((), ())), preferred_element_type=f32)


def dot_tn(a, b):
    return lax.dot_general(a, b, (((0,), (0,)), ((), ())), preferred_element_type=f32)


def alone(run):
    def once(i, _):
        run()
        return 0

    lax.fori_loop(0, lax.axis_index("chan") // 2 + 1, once, 0)


def iota(shape, dim):
    return lax.broadcasted_iota(jnp.int32, shape, dim)


def norm_terms(x):
    centered = x - jnp.mean(x, axis=-1, keepdims=True)
    rstd = lax.rsqrt(jnp.mean(centered * centered, axis=-1, keepdims=True) + EPS)
    return centered * rstd, rstd


def add_blocks(out, terms, count):
    def step(j, _):
        total = terms[0][j].astype(f32)
        for t in terms[1:]:
            total = total + t[j].astype(f32)
        out[j] = total.astype(out.dtype)
        return 0

    lax.fori_loop(0, count, step, 0)


def layer_kernel(
    clip, ids, gain, w_qkv_hbm, w_out_hbm, table_hbm, out, d_clip,
    d_recv, x_v, ids_v, leave, r, w_qkv, w_out, w_other, table,
    x_s, ids_s, n_s, qkv_s, o_s, oo_s, p_s, dy_s, do_s, ds_s, d_s, dn_s, dno_s, n_t, dy_t,
    nt_x, dyt_x, d_x, o_x, g, r1, l1, r2, l2, r3, l3, br1, bl1, br2, bl2, br3, bl3, bmr, bml, u, xr,
    load_sem, w_sem, w_send, w_recv, own_sem, all_send, all_recv, home_own, home_send, home_recv,
    o_send, o_recv, dn_send, dn_recv,
    ox_sems, ntx_sems, dyx_sems, dx_sems, a_send, a_recv, b_send, b_recv, x_send, x_recv,
):
    xh, y, z, core = coordinates()
    chan = lax.axis_index("chan")
    tokens, width = x_v.shape
    cols = o_s.shape[0]
    n_heads = cols // HEAD_DIM
    half = tokens // 2
    scale = HEAD_DIM ** (-0.5)
    kept = (xh + chan + core) % 2
    here = y * (1 - core) + z * core
    there = z * (1 - core) + y * core

    def ring(first, step):
        dy = step if first else 0
        dz = 0 if first else step
        ny = (y + (1 - core) * dy + core * dz + Y) % Y
        nz = (z + core * dy + (1 - core) * dz + Z) % Z
        return {"frame": frame_index(xh, ny, nz, core)}

    sibling = {"frame": frame_index(xh, y, z, 1 - core)}
    across = {"frame": frame_index(1 - xh, y, z, core)}
    partner = {"chan": 1 - chan}

    def remote(src, dst, send, recv, peer):
        return pltpu.make_async_remote_copy(
            src_ref=src, dst_ref=dst, send_sem=send, recv_sem=recv,
            device_id=peer, device_id_type=pl.DeviceIdType.MESH,
        )

    loads = [
        pltpu.make_async_copy(clip, x_v, load_sem.at[0]),
        pltpu.make_async_copy(ids, ids_v, load_sem.at[1]),
        pltpu.make_async_copy(w_out_hbm, w_out, load_sem.at[2]),
        pltpu.make_async_copy(w_qkv_hbm, w_qkv, load_sem.at[3]),
        pltpu.make_async_copy(table_hbm, table, load_sem.at[4]),
    ]
    for c in loads:
        c.start()
    def greet_some(k, _):
        greet(k)
        return 0

    lax.fori_loop(1, FRAME * CHAN, greet_some, 0)

    loads[0].wait()
    loads[1].wait()

    def leaving(j, _):
        t = iota((128, tokens), 0) + j * 128
        source = (t % 2) * half + (t // 8) * 4 + t % 8 // 2
        pick = (iota((128, tokens), 1) == source).astype(bf16)
        to = pl.ds(j * 16, 16)
        leave[to, :, :width] = dot(pick, x_v[...]).reshape(16, 8, width).astype(bf16)
        leave[to, :, width:] = dot(pick, ids_v[...]).reshape(16, 8, 128).astype(bf16)
        return 0

    lax.fori_loop(0, 4, leaving, 0)
    loads[2].wait()
    pl.semaphore_wait(pltpu.get_barrier_semaphore(), FRAME * CHAN - 1)

    rows_half = cols // 2
    own_rows = pl.ds(pl.multiple_of(core * rows_half, 16), rows_half)
    w_first = remote(w_out.at[own_rows], w_other.at[own_rows], w_send.at[0], w_recv.at[0], partner)
    w_first.start()
    start_all(leave, r, all_send, all_recv, own_sem, width + 128)
    wait_all(leave, r, all_send, all_recv, own_sem, width + 128)
    loads[3].wait()
    loads[4].wait()

    def rows(c):
        return pl.ds(pl.multiple_of(c * half, half), half)

    def swap_o(c):
        return remote(o_s.at[:, rows(c)], oo_s.at[:, rows(c)], o_send.at[c], o_recv.at[c], partner)

    def swap_dn(c):
        two = pl.ds(2 * c, 2)
        return remote(
            dn_s.at[two, 1 - kept], dno_s.at[two], dn_send.at[c], dn_recv.at[c], partner
        )

    half_rows = FRAME * PAD // 2
    theirs = pl.ds(pl.multiple_of((1 - core) * half_rows, half_rows), half_rows)
    ours = pl.ds(pl.multiple_of(core * half_rows, half_rows), half_rows)

    def swap_core(src, dst, sems, c):
        return remote(src, dst, sems.at[0, c], sems.at[1, c], sibling)

    def swap_ox(c):
        return swap_core(o_s.at[:, rows(c)], o_x.at[:, rows(c)], ox_sems, c)

    def swap_ntx(c):
        return swap_core(n_t.at[theirs, rows(c)], nt_x.at[:, rows(c)], ntx_sems, c)

    def swap_dyx(c):
        return swap_core(dy_t.at[theirs, rows(c)], dyt_x.at[:, rows(c)], dyx_sems, c)

    def swap_dx(c):
        return swap_core(d_s.at[:, rows(c)], d_x.at[:, rows(c)], dx_sems, c)

    def patch(c, pp):
        return pl.ds(pl.multiple_of(c * half + pp * 128, 128), 128)

    def forward(c, _):
        t = iota((half, tokens), 0)
        source = (t % 128 // 2) * 8 + 2 * (2 * c + t // 128) + t % 2
        pick = (iota((half, tokens), 1) == source).astype(bf16)
        moved = dot(pick, r[...].reshape(tokens, width + 128))
        x = moved[:, :width]
        x_s[rows(c), :] = x.astype(bf16)
        ids_s[rows(c), :] = moved[:, width:]
        xhat, _ = norm_terms(x)
        normed = (xhat * gain[...].astype(f32)).astype(bf16)
        n_s[rows(c), :] = normed
        for i in range(3):
            qkv = dot_nt(w_qkv[i * cols : (i + 1) * cols, :], normed)
            for h in range(n_heads):
                qkv_s[i * n_heads + h, :, rows(c)] = qkv[
                    h * HEAD_DIM : (h + 1) * HEAD_DIM
                ].astype(bf16)
        alone(functools.partial(forward_heads, c))
        swap_o(c).start()
        swap_ox(c).start()
        return 0

    def forward_heads(c):
        for pp in range(2):
            at = patch(c, pp)
            for h in range(n_heads):
                scores = dot_tn(qkv_s[n_heads + h, :, at], qkv_s[h, :, at]) * scale
                expo = jnp.exp(scores - jnp.max(scores, axis=0, keepdims=True))
                probs = expo * (1.0 / jnp.sum(expo, axis=0, keepdims=True))
                p_s[(2 * c + pp) * n_heads + h] = probs
                o_s[h * HEAD_DIM : (h + 1) * HEAD_DIM, at] = dot(
                    qkv_s[2 * n_heads + h, :, at], probs.astype(bf16)
                ).astype(bf16)

    lax.fori_loop(0, 2, forward, 0)

    block = 8 * ROWS
    window = 384

    def columns(source, target, c):
        for k in range(width // block):
            start = min(k * block // 128, (width - window) // 128) * 128
            shape = (8 * PAD, window)
            at = iota(shape, 0)
            wanted = jnp.where(
                at % PAD < ROWS, k * block + (at // PAD) * ROWS + at % PAD - start, -1
            )
            pick = (iota(shape, 1) == wanted).astype(bf16)
            picked = dot_nt(pick, source[rows(c), start : start + window])
            for j in range(8):
                cj, zj = j % 2, j // 2
                a, b = (k % Y, zj) if cj == 0 else (zj, k % Y)
                to = (((cj * 4 + a) * 2 + k // Y) * 4 + b) * PAD
                target[to : to + PAD, rows(c)] = picked[j * PAD : (j + 1) * PAD].astype(bf16)

    def targets(c, _):
        hi_lo = ids_s[rows(c), :]
        wanted = hi_lo[:, 0:1] * 32.0 + hi_lo[:, 1:2]
        n_old = table.shape[0]
        pick = (iota((half, n_old), 1).astype(f32) == wanted).astype(bf16)
        x_v[rows(c), :] = dot(pick, table[...]).astype(bf16)
        alone(functools.partial(columns, n_s, n_t, c))
        swap_ntx(c).start()
        return 0

    w_first.wait_recv()
    w_second = remote(
        w_other.at[own_rows], w_other.at[own_rows], w_send.at[1], w_recv.at[1], sibling
    )
    w_second.start()
    lax.fori_loop(0, 2, targets, 0)
    w_second.wait_recv()

    def backward(c, _):
        swap_o(c).wait_recv()
        branch = dot_tn(o_s[:, rows(c)], w_out[...]) + dot_tn(oo_s[:, rows(c)], w_other[...])
        d_y = (x_s[rows(c), :].astype(f32) + branch - x_v[rows(c), :].astype(f32)).astype(bf16)
        dy_s[rows(c), :] = d_y
        alone(functools.partial(columns, dy_s, dy_t, c))
        swap_dyx(c).start()
        d_o = dot_nt(w_out[...], d_y)
        for h in range(n_heads):
            do_s[h] = d_o[h * HEAD_DIM : (h + 1) * HEAD_DIM].astype(bf16)
        alone(functools.partial(score_heads, c))
        alone(functools.partial(value_heads, c))
        swap_dx(c).start()
        dn = dot_tn(d_s[:, rows(c)], w_qkv[...])
        dn_s[pl.ds(2 * c, 2)] = dn.reshape(2, 2, 64, width).astype(bf16)
        swap_dn(c).start()
        return 0

    def score_heads(c):
        for pp in range(2):
            at = patch(c, pp)
            for h in range(n_heads):
                probs = p_s[(2 * c + pp) * n_heads + h]
                d_oh = do_s[h, :, pp * 128 : (pp + 1) * 128]
                dprobs = dot_tn(qkv_s[2 * n_heads + h, :, at], d_oh)
                rowsum = jnp.sum(dprobs * probs, axis=0, keepdims=True)
                ds = (probs * (dprobs - rowsum) * scale).astype(bf16)
                ds_s[pp * n_heads + h] = ds
                d_s[h * HEAD_DIM : (h + 1) * HEAD_DIM, at] = dot(
                    qkv_s[n_heads + h, :, at], ds
                ).astype(bf16)

    def value_heads(c):
        for pp in range(2):
            at = patch(c, pp)
            for h in range(n_heads):
                lo, hi = h * HEAD_DIM, (h + 1) * HEAD_DIM
                probs = p_s[(2 * c + pp) * n_heads + h].astype(bf16)
                d_oh = do_s[h, :, pp * 128 : (pp + 1) * 128]
                d_s[cols + lo : cols + hi, at] = dot_nt(
                    qkv_s[h, :, at], ds_s[pp * n_heads + h]
                ).astype(bf16)
                d_s[2 * cols + lo : 2 * cols + hi, at] = dot_nt(d_oh, probs).astype(bf16)

    lax.fori_loop(0, 2, backward, 0)

    def piece(a, h):
        return g.at[pl.ds(((here + a) % 4 * 2 + h) * 4, 4)]

    copies = []

    def plan(src, dst, k, peer, sends, recvs):
        c = remote(src, dst, sends.at[k], recvs.at[k], peer)
        copies.append(c)
        return c

    def send(*what):
        c = plan(*what)
        c.start()
        return c

    right, left = ring(True, 1), ring(True, -1)
    c1r = plan(piece(2, 0), r1, 0, right, a_send, a_recv)
    c1l = plan(piece(2, 1), l1, 1, left, a_send, a_recv)
    c2r = plan(piece(1, 1), r2, 2, right, a_send, a_recv)
    c2l = plan(piece(3, 0), l2, 3, left, a_send, a_recv)
    for c in range(2):
        swap_ntx(c).wait_recv()
        swap_ox(c).wait_recv()
        swap_dyx(c).wait_recv()
        swap_dx(c).wait_recv()

    def weight_grads(i, _):
        a = (here + jnp.where(i < 2, 2 - i, 5 - i - (i // 3) * 2)) % 4
        at = pl.ds(pl.multiple_of((core * 4 + a) * 8 * PAD, 8 * PAD), 8 * PAD)
        at_x = pl.ds(pl.multiple_of(a * 8 * PAD, 8 * PAD), 8 * PAD)
        to = pl.ds(a * 8, 8)
        part = dot_nt(n_t[at, :], d_s[...]) + dot_nt(nt_x[at_x, :], d_x[...])
        g[to, :, : 3 * cols] = part.reshape(8, PAD, 3 * cols).astype(bf16)
        part = dot_nt(dy_t[at, :], o_s[...]) + dot_nt(dyt_x[at_x, :], o_x[...])
        g[to, :, 3 * cols :] = part.reshape(8, PAD, cols).astype(bf16)

        @pl.when(i == 0)
        def _():
            c1r.start()
            c1l.start()

        @pl.when(i == 1)
        def _():
            c2r.start()

        @pl.when(i == 2)
        def _():
            c2l.start()

        return 0

    lax.fori_loop(0, 4, weight_grads, 0)

    drain_all(leave, r, all_send, all_recv, width + 128)

    def finish(p, _):
        @pl.when(p % 2 == 0)
        def _():
            swap_dn(p // 2).wait_recv()

        at = pl.ds(pl.multiple_of(p * 128 + kept * 64, 64), 64)
        dn = dn_s[p, kept].astype(f32) + dno_s[p].astype(f32)
        xhat, rstd = norm_terms(x_s[at, :].astype(f32))
        gs = dn * gain[...].astype(f32)
        back = rstd * (
            gs
            - jnp.mean(gs, axis=-1, keepdims=True)
            - xhat * jnp.mean(gs * xhat, axis=-1, keepdims=True)
        )
        x_v[pl.ds(pl.multiple_of(p * 64, 64), 64), :] = (
            dy_s[at, :].astype(f32) + back
        ).astype(bf16)
        return 0

    lax.fori_loop(0, 4, finish, 0)

    def to_home(j, _):
        t = iota((128, half), 0) + j * 128
        source = (t % 8 // 2) * 64 + 2 * (t // 8) + t % 2
        pick = (iota((128, half), 1) == source).astype(bf16)
        leave[pl.ds(j * 16, 16), :, :width] = (
            dot(pick, x_v[pl.ds(0, half), :]).reshape(16, 8, width).astype(bf16)
        )
        return 0

    lax.fori_loop(0, 2, to_home, 0)

    f = lax.axis_index("frame")
    own = (kept + xh) % 2 == 0

    def home_copy(k, c):
        q = (f + k) % (FRAME // 2)
        return pltpu.make_async_remote_copy(
            src_ref=part(leave, q, width), dst_ref=d_recv.at[f],
            send_sem=home_send.at[2 * k + c], recv_sem=home_recv.at[2 * k + c],
            device_id={"frame": kept * (FRAME // 2) + q, "chan": (chan + c) % 2},
            device_id_type=pl.DeviceIdType.MESH,
        )

    home_local = pltpu.make_async_copy(part(leave, f % (FRAME // 2), width), d_recv.at[f], home_own)

    def home_each(run, run_own):
        @pl.when(own)
        def _():
            run_own()

        @pl.when(jnp.logical_not(own))
        def _():
            run(home_copy(0, 0))

        run(home_copy(0, 1))

        def step(k, _):
            run(home_copy(k, 0))
            run(home_copy(k, 1))
            return 0

        lax.fori_loop(1, FRAME // 2, step, 0)

    c1r.wait_recv()
    add_blocks(piece(1, 0), (piece(1, 0), r1), 4)
    c3r = send(piece(1, 0), r3, 4, right, a_send, a_recv)
    c1l.wait_recv()
    add_blocks(piece(3, 1), (piece(3, 1), l1), 4)
    c3l = send(piece(3, 1), l3, 5, left, a_send, a_recv)
    home_each(lambda c: c.start(), home_local.start)
    c2l.wait_recv()
    c3r.wait_recv()
    add_blocks(piece(0, 0), (piece(0, 0), r3, l2), 4)
    c2r.wait_recv()
    c3l.wait_recv()
    add_blocks(piece(0, 1), (piece(0, 1), r2, l3), 4)

    right, left = ring(False, 1), ring(False, -1)
    at = lambda h, d: g.at[(here * 2 + h) * 4 + (there + d) % 4]
    d1r = send(at(0, 2), br1, 0, right, b_send, b_recv)
    d1l = send(at(1, 2), bl1, 1, left, b_send, b_recv)
    d2r = send(at(1, 1), br2, 2, right, b_send, b_recv)
    d2l = send(at(0, 3), bl2, 3, left, b_send, b_recv)
    d1r.wait_recv()
    bmr[...] = (at(0, 1)[...].astype(f32) + br1[...].astype(f32)).astype(bf16)
    d3r = send(bmr, br3, 4, right, b_send, b_recv)
    d1l.wait_recv()
    bml[...] = (at(1, 3)[...].astype(f32) + bl1[...].astype(f32)).astype(bf16)
    d3l = send(bml, bl3, 5, left, b_send, b_recv)
    d2l.wait_recv()
    d3r.wait_recv()
    u[0] = (at(0, 0)[...].astype(f32) + br3[...].astype(f32) + bl2[...].astype(f32)).astype(bf16)
    d2r.wait_recv()
    d3l.wait_recv()
    u[1] = (at(1, 0)[...].astype(f32) + br2[...].astype(f32) + bl3[...].astype(f32)).astype(bf16)

    e = remote(u.at[1 - xh], xr, x_send, x_recv, across)
    e.start()
    e.wait_recv()
    out[...] = u[xh].astype(f32) + xr[...].astype(f32)
    home_each(lambda c: c.wait_recv(), home_local.wait)
    for h in range(2):
        t = iota((half, half), 0)
        source = (t % 128 // 4) * 8 + (t % 4) * 2 + t // 128
        pick = (iota((half, half), 1) == source).astype(bf16)
        landed = d_recv[h * (FRAME // 2) : (h + 1) * (FRAME // 2)].reshape(half, width)
        moved = dot(pick, landed).astype(bf16)
        d_clip[h * 128 : (h + 1) * 128, :] = moved[:128]
        d_clip[half + h * 128 : half + (h + 1) * 128, :] = moved[128:]

    e.wait_send()
    w_first.wait_send()
    w_second.wait_send()
    for c in copies:
        c.wait_send()
    for c in range(2):
        swap_o(c).wait_send()
        swap_dn(c).wait_send()
        swap_ox(c).wait_send()
        swap_ntx(c).wait_send()
        swap_dyx(c).wait_send()
        swap_dx(c).wait_send()
    home_each(lambda c: c.wait_send(), lambda: None)


def layer(clip, ids, gain, w_qkv, w_out, table):
    tokens, width = clip.shape
    cols = w_out.shape[0]
    n_heads = cols // HEAD_DIM
    each = tokens // FRAME
    vmem = pl.BlockSpec(memory_space=pltpu.VMEM)
    anywhere = pl.BlockSpec(memory_space=pl.ANY)
    wide = pltpu.VMEM((tokens, width), bf16)
    narrow = pltpu.VMEM((cols, tokens), bf16)
    piece = pltpu.VMEM((4, PAD, 4 * cols), bf16)
    block = pltpu.VMEM((PAD, 4 * cols), bf16)
    carry = pltpu.VMEM((FRAME, each, width + 128), bf16)
    dma = pltpu.SemaphoreType.DMA
    return pl.pallas_call(
        layer_kernel,
        out_shape=[
            jax.ShapeDtypeStruct((PAD, 4 * cols), f32),
            jax.ShapeDtypeStruct((tokens, width), bf16),
        ],
        in_specs=[anywhere, anywhere, vmem, anywhere, anywhere, anywhere],
        out_specs=[vmem, vmem],
        scratch_shapes=[
            pltpu.VMEM((FRAME, each, width), bf16),
            wide,
            pltpu.VMEM((tokens, 128), bf16),
            carry,
            carry,
            pltpu.VMEM((3 * cols, width), bf16),
            pltpu.VMEM((cols, width), bf16),
            pltpu.VMEM((cols, width), bf16),
            pltpu.VMEM(table.shape, bf16),
            wide,
            pltpu.VMEM((tokens, 128), f32),
            wide,
            pltpu.VMEM((3 * n_heads, HEAD_DIM, tokens), bf16),
            narrow,
            narrow,
            pltpu.VMEM((tokens // 128 * n_heads, 128, 128), f32),
            wide,
            pltpu.VMEM((n_heads, HEAD_DIM, tokens // 2), bf16),
            pltpu.VMEM((2 * n_heads, 128, 128), bf16),
            pltpu.VMEM((3 * cols, tokens), bf16),
            pltpu.VMEM((4, 2, 64, width), bf16),
            pltpu.VMEM((4, 64, width), bf16),
            pltpu.VMEM((FRAME * PAD, tokens), bf16),
            pltpu.VMEM((FRAME * PAD, tokens), bf16),
            pltpu.VMEM((FRAME * PAD // 2, tokens), bf16),
            pltpu.VMEM((FRAME * PAD // 2, tokens), bf16),
            pltpu.VMEM((3 * cols, tokens), bf16),
            narrow,
            pltpu.VMEM((FRAME // 2, PAD, 4 * cols), bf16),
        ]
        + [piece] * 6
        + [block] * 8
        + [pltpu.VMEM((2, PAD, 4 * cols), bf16), block]
        + [
            dma((5,)), dma, dma((2,)), dma((2,)),
            dma, dma((FRAME,)), dma((FRAME,)), dma, dma((FRAME,)), dma((FRAME,)),
            dma((2,)), dma((2,)), dma((2,)), dma((2,)),
            dma((2, 2)), dma((2, 2)), dma((2, 2)), dma((2, 2)), dma((6,)), dma((6,)), dma((6,)), dma((6,)), dma, dma,
        ],
        compiler_params=pltpu.CompilerParams(
            collective_id=0, has_side_effects=True, vmem_limit_bytes=VMEM_LIMIT
        ),
        name="layer",
    )(clip, ids, gain, w_qkv, w_out, table)


def body(clip, gain, w_qkv, w_out, old_table, target_ids):
    frames_here, patches, width = clip.shape
    cols = w_qkv.shape[2]
    tokens = frames_here * patches

    ids = target_ids.reshape(tokens, 1)
    lane = iota((tokens, 128), 1)
    ids = jnp.where(lane == 0, ids // 32, jnp.where(lane == 1, ids % 32, 0)).astype(bf16)
    reduced, d_clip = layer(
        clip.reshape(tokens, width),
        ids,
        gain.reshape(1, width),
        w_qkv.transpose(0, 2, 1).reshape(3 * cols, width),
        w_out,
        old_table,
    )

    reduced = reduced[:ROWS].reshape(ROWS, 4, cols)
    return (
        d_clip.reshape(frames_here, patches, width),
        reduced[:, :3].transpose(1, 0, 2),
        reduced[:, 3].T,
    )


def solution(mesh):
    return jax.shard_map(
        body,
        mesh=mesh,
        in_specs=(
            P("frame", None, None),
            P(),
            P(None, None, "chan"),
            P("chan", None),
            P(),
            P("frame", None),
        ),
        out_specs=(P("frame", None, None), P(None, "frame", "chan"), P("chan", "frame")),
        check_vma=False,
    )
```

```python
import functools

import jax
import jax.numpy as jnp
from jax import lax
from jax.experimental import pallas as pl
from jax.experimental.pallas import tpu as pltpu
from jax.sharding import PartitionSpec as P

HEAD_DIM = 88
EPS = 1e-05
VMEM_LIMIT = 63 * 2**20
XH, Y, Z, CORE = 2, 4, 4, 2
FRAME = XH * Y * Z * CORE
ROWS = 22
PAD = 24

f32 = jnp.float32
bf16 = jnp.bfloat16


def frame_index(xh, y, z, core):
    return ((xh * Y + y) * Z + z) * CORE + core


def coordinates():
    f = lax.axis_index("frame")
    return f // (Y * Z * CORE), (f // (Z * CORE)) % Y, (f // CORE) % Z, f % CORE


def all_peer(k):
    f = lax.axis_index("frame")
    chan = lax.axis_index("chan")
    p = (f + k) % FRAME
    far = (p // (FRAME // 2) + f // (FRAME // 2)) % 2
    return p, {"frame": p, "chan": (chan + far) % 2}


def greet(peer):
    pl.semaphore_signal(
        pltpu.get_barrier_semaphore(), inc=1, device_id=peer, device_id_type=pl.DeviceIdType.MESH
    )


def part(ref, i, width):
    return ref.at[i, :, pl.ds(0, width)]


def all_copy(src, dst, sends, recvs, k, width):
    p, peer = all_peer(k)
    return pltpu.make_async_remote_copy(
        src_ref=part(src, p, width), dst_ref=part(dst, lax.axis_index("frame"), width),
        send_sem=sends.at[k], recv_sem=recvs.at[k],
        device_id=peer, device_id_type=pl.DeviceIdType.MESH,
    )


def start_all(src, dst, sends, recvs, own_sem, width):
    def start(k, _):
        all_copy(src, dst, sends, recvs, k, width).start()
        return 0

    lax.fori_loop(1, FRAME, start, 0)
    f = lax.axis_index("frame")
    pltpu.make_async_copy(part(src, f, width), part(dst, f, width), own_sem).start()


def wait_all(src, dst, sends, recvs, own_sem, width):
    f = lax.axis_index("frame")
    pltpu.make_async_copy(part(src, f, width), part(dst, f, width), own_sem).wait()

    def wait(k, _):
        all_copy(src, dst, sends, recvs, k, width).wait_recv()
        return 0

    lax.fori_loop(1, FRAME, wait, 0)


def drain_all(src, dst, sends, recvs, width):
    def drain(k, _):
        all_copy(src, dst, sends, recvs, k, width).wait_send()
        return 0

    lax.fori_loop(1, FRAME, drain, 0)


def dot(a, b):
    return jnp.dot(a, b, preferred_element_type=f32)


def dot_nt(a, b):
    return lax.dot_general(a, b, (((1,), (1,)), ((), ())), preferred_element_type=f32)


def dot_tn(a, b):
    return lax.dot_general(a, b, (((0,), (0,)), ((), ())), preferred_element_type=f32)


def alone(run):
    def once(i, _):
        run()
        return 0

    lax.fori_loop(0, lax.axis_index("chan") // 2 + 1, once, 0)


def iota(shape, dim):
    return lax.broadcasted_iota(jnp.int32, shape, dim)


def norm_terms(x):
    centered = x - jnp.mean(x, axis=-1, keepdims=True)
    rstd = lax.rsqrt(jnp.mean(centered * centered, axis=-1, keepdims=True) + EPS)
    return centered * rstd, rstd


def add_blocks(out, terms, count):
    def step(j, _):
        total = terms[0][j].astype(f32)
        for t in terms[1:]:
            total = total + t[j].astype(f32)
        out[j] = total.astype(out.dtype)
        return 0

    lax.fori_loop(0, count, step, 0)


def layer_kernel(
    clip, ids, gain, w_qkv_hbm, w_out_hbm, table_hbm, out_qkv, out_o, d_clip,
    d_recv, x_v, leave, r, w_qkv, w_out, w_other, table,
    x_s, ids_s, n_s, qkv_s, o_s, oo_s, p_s, dy_s, do_s, ds_s, d_s, dn_s, dno_s, n_t, dy_t,
    nt_x, dyt_x, d_x, o_x, g, r1, l1, r2, l2, r3, l3, br1, bl1, br2, bl2, br3, bl3, bmr, bml, u, xr,
    load_sem, w_sem, w_send, w_recv, own_sem, all_send, all_recv, home_own, home_send, home_recv, on_send, on_recv,
    o_send, o_recv, dn_send, dn_recv,
    ox_sems, ntx_sems, dyx_sems, dx_sems, a_send, a_recv, b_send, b_recv, x_send, x_recv,
):
    xh, y, z, core = coordinates()
    chan = lax.axis_index("chan")
    tokens, width = x_v.shape
    cols = o_s.shape[0]
    n_heads = cols // HEAD_DIM
    half = tokens // 2
    scale = HEAD_DIM ** (-0.5)
    kept = (xh + chan + core) % 2
    here = y * (1 - core) + z * core
    there = z * (1 - core) + y * core

    def ring(first, step):
        dy = step if first else 0
        dz = 0 if first else step
        ny = (y + (1 - core) * dy + core * dz + Y) % Y
        nz = (z + core * dy + (1 - core) * dz + Z) % Z
        return {"frame": frame_index(xh, ny, nz, core)}

    sibling = {"frame": frame_index(xh, y, z, 1 - core)}
    across = {"frame": frame_index(1 - xh, y, z, core)}
    partner = {"chan": 1 - chan}

    def remote(src, dst, send, recv, peer):
        return pltpu.make_async_remote_copy(
            src_ref=src, dst_ref=dst, send_sem=send, recv_sem=recv,
            device_id=peer, device_id_type=pl.DeviceIdType.MESH,
        )

    loads = [
        pltpu.make_async_copy(clip, x_v, load_sem.at[0]),
        pltpu.make_async_copy(w_out_hbm, w_out, load_sem.at[1]),
        pltpu.make_async_copy(w_qkv_hbm, w_qkv, load_sem.at[2]),
        pltpu.make_async_copy(table_hbm, table, load_sem.at[3]),
    ]
    for c in loads:
        c.start()
    def greet_some(k, _):
        greet(all_peer(k)[1])
        return 0

    lax.fori_loop(1, FRAME, greet_some, 0)
    greet(partner)
    greet(across)

    loads[0].wait()
    gain_row = gain[...].astype(f32).reshape(1, width)
    id_row = jnp.concatenate([ids[0:1, :], ids[1:2, :]], axis=1).astype(f32)

    def leaving(j, _):
        t = iota((128, tokens), 0) + j * 128
        source = (t % 2) * half + (t // 8) * 4 + t % 8 // 2
        pick = iota((128, tokens), 1) == source
        to = pl.ds(j * 16, 16)
        moved = dot(pick.astype(bf16), x_v[...])
        leave[to, :, :width] = moved.reshape(16, 8, width).astype(bf16)
        id_here = jnp.sum(jnp.where(pick, id_row, 0.0), axis=1, keepdims=True)
        high = jnp.floor(id_here * (1.0 / 32.0))
        lane = iota((128, 128), 1)
        pair = jnp.where(lane == 0, high, jnp.where(lane == 1, id_here - high * 32.0, 0.0))
        leave[to, :, width:] = pair.reshape(16, 8, 128).astype(bf16)
        return 0

    lax.fori_loop(0, 4, leaving, 0)
    loads[1].wait()
    pl.semaphore_wait(pltpu.get_barrier_semaphore(), FRAME + 1)

    rows_half = cols // 2
    own_rows = pl.ds(pl.multiple_of(core * rows_half, 16), rows_half)
    w_first = remote(w_out.at[own_rows], w_other.at[own_rows], w_send.at[0], w_recv.at[0], partner)
    start_all(leave, r, all_send, all_recv, own_sem, width + 128)
    w_first.start()
    wait_all(leave, r, all_send, all_recv, own_sem, width + 128)
    loads[2].wait()
    loads[3].wait()

    def rows(c):
        return pl.ds(pl.multiple_of(c * half, half), half)

    def swap_o(c):
        return remote(o_s.at[:, rows(c)], oo_s.at[:, rows(c)], o_send.at[c], o_recv.at[c], partner)

    def swap_dn(c):
        two = pl.ds(2 * c, 2)
        return remote(
            dn_s.at[two, 1 - kept], dno_s.at[two], dn_send.at[c], dn_recv.at[c], partner
        )

    half_rows = FRAME * PAD // 2
    theirs = pl.ds(pl.multiple_of((1 - core) * half_rows, half_rows), half_rows)
    ours = pl.ds(pl.multiple_of(core * half_rows, half_rows), half_rows)

    def swap_core(src, dst, sems, c):
        return remote(src, dst, sems.at[0, c], sems.at[1, c], sibling)

    def swap_ox(c):
        return swap_core(o_s.at[:, rows(c)], o_x.at[:, rows(c)], ox_sems, c)

    def swap_ntx(c):
        return swap_core(n_t.at[theirs, rows(c)], nt_x.at[:, rows(c)], ntx_sems, c)

    def swap_dyx(c):
        return swap_core(dy_t.at[theirs, rows(c)], dyt_x.at[:, rows(c)], dyx_sems, c)

    def swap_dx(c):
        return swap_core(d_s.at[:, rows(c)], d_x.at[:, rows(c)], dx_sems, c)

    def patch(c, pp):
        return pl.ds(pl.multiple_of(c * half + pp * 128, 128), 128)

    def forward(c, _):
        t = iota((half, tokens), 0)
        source = (t % 128 // 2) * 8 + 2 * (2 * c + t // 128) + t % 2
        pick = (iota((half, tokens), 1) == source).astype(bf16)
        moved = dot(pick, r[...].reshape(tokens, width + 128))
        x = moved[:, :width]
        x_s[rows(c), :] = x.astype(bf16)
        ids_s[rows(c), :] = moved[:, width:]
        xhat, _ = norm_terms(x)
        normed = (xhat * gain_row).astype(bf16)
        n_s[rows(c), :] = normed
        for i in range(3):
            qkv = dot_nt(w_qkv[i * cols : (i + 1) * cols, :], normed)
            for h in range(n_heads):
                qkv_s[i * n_heads + h, :, rows(c)] = qkv[
                    h * HEAD_DIM : (h + 1) * HEAD_DIM
                ].astype(bf16)
        alone(functools.partial(forward_heads, c))
        swap_o(c).start()
        swap_ox(c).start()
        return 0

    def forward_heads(c):
        for pp in range(2):
            at = patch(c, pp)
            for h in range(n_heads):
                scores = dot_tn(qkv_s[n_heads + h, :, at], qkv_s[h, :, at]) * scale
                expo = jnp.exp(scores - jnp.max(scores, axis=0, keepdims=True))
                probs = expo * (1.0 / jnp.sum(expo, axis=0, keepdims=True))
                p_s[(2 * c + pp) * n_heads + h] = probs
                o_s[h * HEAD_DIM : (h + 1) * HEAD_DIM, at] = dot(
                    qkv_s[2 * n_heads + h, :, at], probs.astype(bf16)
                ).astype(bf16)

    lax.fori_loop(0, 2, forward, 0)

    block = 8 * ROWS
    window = 384

    def columns(source, target, c):
        for k in range(width // block):
            start = min(k * block // 128, (width - window) // 128) * 128
            shape = (8 * PAD, window)
            at = iota(shape, 0)
            wanted = jnp.where(
                at % PAD < ROWS, k * block + (at // PAD) * ROWS + at % PAD - start, -1
            )
            pick = (iota(shape, 1) == wanted).astype(bf16)
            picked = dot_nt(pick, source[rows(c), start : start + window])
            for j in range(8):
                cj, zj = j % 2, j // 2
                a, b = (k % Y, zj) if cj == 0 else (zj, k % Y)
                to = (((cj * 4 + a) * 2 + k // Y) * 4 + b) * PAD
                target[to : to + PAD, rows(c)] = picked[j * PAD : (j + 1) * PAD].astype(bf16)

    def targets(c, _):
        hi_lo = ids_s[rows(c), :]
        wanted = hi_lo[:, 0:1] * 32.0 + hi_lo[:, 1:2]
        n_old = table.shape[0]
        pick = (iota((half, n_old), 1).astype(f32) == wanted).astype(bf16)
        x_v[rows(c), :] = dot(pick, table[...]).astype(bf16)
        alone(functools.partial(columns, n_s, n_t, c))
        swap_ntx(c).start()
        return 0

    w_first.wait_recv()
    w_second = remote(
        w_other.at[own_rows], w_other.at[own_rows], w_send.at[1], w_recv.at[1], sibling
    )
    w_second.start()
    lax.fori_loop(0, 2, targets, 0)
    w_second.wait_recv()

    def backward(c, _):
        swap_o(c).wait_recv()
        branch = dot_tn(o_s[:, rows(c)], w_out[...]) + dot_tn(oo_s[:, rows(c)], w_other[...])
        d_y = (x_s[rows(c), :].astype(f32) + branch - x_v[rows(c), :].astype(f32)).astype(bf16)
        dy_s[rows(c), :] = d_y
        alone(functools.partial(columns, dy_s, dy_t, c))
        swap_dyx(c).start()
        d_o = dot_nt(w_out[...], d_y)
        for h in range(n_heads):
            do_s[h] = d_o[h * HEAD_DIM : (h + 1) * HEAD_DIM].astype(bf16)
        alone(functools.partial(score_heads, c))
        alone(functools.partial(value_heads, c))
        swap_dx(c).start()
        dn = dot_tn(d_s[:, rows(c)], w_qkv[...])
        dn_s[pl.ds(2 * c, 2)] = dn.reshape(2, 2, 64, width).astype(bf16)
        swap_dn(c).start()
        return 0

    def score_heads(c):
        for pp in range(2):
            at = patch(c, pp)
            for h in range(n_heads):
                probs = p_s[(2 * c + pp) * n_heads + h]
                d_oh = do_s[h, :, pp * 128 : (pp + 1) * 128]
                dprobs = dot_tn(qkv_s[2 * n_heads + h, :, at], d_oh)
                rowsum = jnp.sum(dprobs * probs, axis=0, keepdims=True)
                ds = (probs * (dprobs - rowsum) * scale).astype(bf16)
                ds_s[pp * n_heads + h] = ds
                d_s[h * HEAD_DIM : (h + 1) * HEAD_DIM, at] = dot(
                    qkv_s[n_heads + h, :, at], ds
                ).astype(bf16)

    def value_heads(c):
        for pp in range(2):
            at = patch(c, pp)
            for h in range(n_heads):
                lo, hi = h * HEAD_DIM, (h + 1) * HEAD_DIM
                probs = p_s[(2 * c + pp) * n_heads + h].astype(bf16)
                d_oh = do_s[h, :, pp * 128 : (pp + 1) * 128]
                d_s[cols + lo : cols + hi, at] = dot_nt(
                    qkv_s[h, :, at], ds_s[pp * n_heads + h]
                ).astype(bf16)
                d_s[2 * cols + lo : 2 * cols + hi, at] = dot_nt(d_oh, probs).astype(bf16)

    lax.fori_loop(0, 2, backward, 0)

    def piece(a, h):
        return g.at[pl.ds(((here + a) % 4 * 2 + h) * 4, 4)]

    copies = []

    def plan(src, dst, k, peer, sends, recvs):
        c = remote(src, dst, sends.at[k], recvs.at[k], peer)
        copies.append(c)
        return c

    def send(*what):
        c = plan(*what)
        c.start()
        return c

    right, left = ring(True, 1), ring(True, -1)
    c1r = plan(piece(2, 0), r1, 0, right, a_send, a_recv)
    c1l = plan(piece(2, 1), l1, 1, left, a_send, a_recv)
    c2r = plan(piece(1, 1), r2, 2, right, a_send, a_recv)
    c2l = plan(piece(3, 0), l2, 3, left, a_send, a_recv)
    for c in range(2):
        swap_ntx(c).wait_recv()
        swap_ox(c).wait_recv()
        swap_dyx(c).wait_recv()
        swap_dx(c).wait_recv()

    def weight_grads(i, _):
        a = (here + jnp.where(i < 2, 2 - i, 5 - i - (i // 3) * 2)) % 4
        at = pl.ds(pl.multiple_of((core * 4 + a) * 8 * PAD, 8 * PAD), 8 * PAD)
        at_x = pl.ds(pl.multiple_of(a * 8 * PAD, 8 * PAD), 8 * PAD)
        to = pl.ds(a * 8, 8)
        part = dot_nt(n_t[at, :], d_s[...]) + dot_nt(nt_x[at_x, :], d_x[...])
        g[to, :, : 3 * cols] = part.reshape(8, PAD, 3 * cols).astype(bf16)
        part = dot_nt(dy_t[at, :], o_s[...]) + dot_nt(dyt_x[at_x, :], o_x[...])
        g[to, :, 3 * cols :] = part.reshape(8, PAD, cols).astype(bf16)

        @pl.when(i == 0)
        def _():
            c1r.start()
            c1l.start()

        @pl.when(i == 1)
        def _():
            c2r.start()

        @pl.when(i == 2)
        def _():
            c2l.start()

        return 0

    lax.fori_loop(0, 4, weight_grads, 0)

    drain_all(leave, r, all_send, all_recv, width + 128)

    def finish(p, _):
        @pl.when(p % 2 == 0)
        def _():
            swap_dn(p // 2).wait_recv()

        at = pl.ds(pl.multiple_of(p * 128 + kept * 64, 64), 64)
        dn = dn_s[p, kept].astype(f32) + dno_s[p].astype(f32)
        xhat, rstd = norm_terms(x_s[at, :].astype(f32))
        gs = dn * gain_row
        back = rstd * (
            gs
            - jnp.mean(gs, axis=-1, keepdims=True)
            - xhat * jnp.mean(gs * xhat, axis=-1, keepdims=True)
        )
        x_v[pl.ds(pl.multiple_of(p * 64, 64), 64), :] = (
            dy_s[at, :].astype(f32) + back
        ).astype(bf16)
        return 0

    lax.fori_loop(0, 4, finish, 0)

    def to_home(j, _):
        t = iota((128, half), 0) + j * 128
        source = (t % 8 // 2) * 64 + 2 * (t // 8) + t % 2
        pick = (iota((128, half), 1) == source).astype(bf16)
        leave[pl.ds(j * 16, 16), :, :width] = (
            dot(pick, x_v[pl.ds(0, half), :]).reshape(16, 8, width).astype(bf16)
        )
        return 0

    lax.fori_loop(0, 2, to_home, 0)

    f = lax.axis_index("frame")
    spots = FRAME // 2
    spot = f % spots
    own = core == chan

    def home_copy(k):
        q = (spot + k) % spots
        return remote(
            part(leave, q, width), d_recv.at[f], home_send.at[k], home_recv.at[f // 2],
            {"frame": kept * spots + q, "chan": core},
        )

    home_local = pltpu.make_async_copy(part(leave, spot, width), d_recv.at[f], home_own)

    def home_each(run, run_own):
        @pl.when(own)
        def _():
            run_own()

        @pl.when(jnp.logical_not(own))
        def _():
            run(home_copy(0))

        def step(k, _):
            run(home_copy(k))
            return 0

        lax.fori_loop(1, spots, step, 0)

    def pass_on(i):
        return remote(d_recv.at[i], d_recv.at[i], on_send.at[i // 2], on_recv.at[i // 2], partner)

    def landed(k, _):
        k = 2 * k + (core + chan) % 2
        for n in range(2):
            source = n * spots + (spot - k + spots) % spots
            local = jnp.logical_and(source == f, own)

            @pl.when(local)
            def _():
                home_local.wait()

            @pl.when(jnp.logical_not(local))
            def _(source=source):
                remote(
                    part(leave, 0, width), d_recv.at[source], home_send.at[0],
                    home_recv.at[source // 2], partner,
                ).wait_recv()

            pass_on(source).start()
        return 0

    def passed_on(run):
        def step(i, _):
            run(i)
            return 0

        lax.fori_loop(0, spots, step, 0)

    home_each(lambda c: c.start(), home_local.start)
    c1r.wait_recv()
    add_blocks(piece(1, 0), (piece(1, 0), r1), 4)
    c3r = send(piece(1, 0), r3, 4, right, a_send, a_recv)
    c1l.wait_recv()
    add_blocks(piece(3, 1), (piece(3, 1), l1), 4)
    c3l = send(piece(3, 1), l3, 5, left, a_send, a_recv)
    lax.fori_loop(0, spots // 2, landed, 0)
    c2l.wait_recv()
    c3r.wait_recv()
    add_blocks(piece(0, 0), (piece(0, 0), r3, l2), 4)
    c2r.wait_recv()
    c3l.wait_recv()
    add_blocks(piece(0, 1), (piece(0, 1), r2, l3), 4)

    right, left = ring(False, 1), ring(False, -1)
    at = lambda h, d: g.at[(here * 2 + h) * 4 + (there + d) % 4]
    d1r = send(at(0, 2), br1, 0, right, b_send, b_recv)
    d1l = send(at(1, 2), bl1, 1, left, b_send, b_recv)
    d2r = send(at(1, 1), br2, 2, right, b_send, b_recv)
    d2l = send(at(0, 3), bl2, 3, left, b_send, b_recv)
    d1r.wait_recv()
    bmr[...] = (at(0, 1)[...].astype(f32) + br1[...].astype(f32)).astype(bf16)
    d3r = send(bmr, br3, 4, right, b_send, b_recv)
    d1l.wait_recv()
    bml[...] = (at(1, 3)[...].astype(f32) + bl1[...].astype(f32)).astype(bf16)
    d3l = send(bml, bl3, 5, left, b_send, b_recv)
    d2l.wait_recv()
    d3r.wait_recv()
    u[0] = (at(0, 0)[...].astype(f32) + br3[...].astype(f32) + bl2[...].astype(f32)).astype(bf16)
    d2r.wait_recv()
    d3l.wait_recv()
    u[1] = (at(1, 0)[...].astype(f32) + br2[...].astype(f32) + bl3[...].astype(f32)).astype(bf16)

    e = remote(u.at[1 - xh], xr, x_send, x_recv, across)
    e.start()
    e.wait_recv()
    total = u[xh].astype(f32) + xr[...].astype(f32)
    for i in range(3):
        out_qkv[i] = total[:ROWS, i * cols : (i + 1) * cols]
    out_o[...] = total[:ROWS, 3 * cols :]
    passed_on(lambda i: pass_on(2 * i + 1 - chan).wait_recv())
    for h in range(2):
        t = iota((half, half), 0)
        source = (t % 128 // 4) * 8 + (t % 4) * 2 + t // 128
        pick = (iota((half, half), 1) == source).astype(bf16)
        landed = d_recv[h * (FRAME // 2) : (h + 1) * (FRAME // 2)].reshape(half, width)
        moved = dot(pick, landed).astype(bf16)
        d_clip[h * 128 : (h + 1) * 128, :] = moved[:128]
        d_clip[half + h * 128 : half + (h + 1) * 128, :] = moved[128:]

    e.wait_send()
    w_first.wait_send()
    w_second.wait_send()
    for c in copies:
        c.wait_send()
    for c in range(2):
        swap_o(c).wait_send()
        swap_dn(c).wait_send()
        swap_ox(c).wait_send()
        swap_ntx(c).wait_send()
        swap_dyx(c).wait_send()
        swap_dx(c).wait_send()
    home_each(lambda c: c.wait_send(), lambda: None)
    passed_on(lambda i: pass_on(2 * i + chan).wait_send())


def layer(clip, ids, gain, w_qkv, w_out, table):
    tokens, width = clip.shape
    cols = w_out.shape[0]
    n_heads = cols // HEAD_DIM
    each = tokens // FRAME
    vmem = pl.BlockSpec(memory_space=pltpu.VMEM)
    anywhere = pl.BlockSpec(memory_space=pl.ANY)
    wide = pltpu.VMEM((tokens, width), bf16)
    narrow = pltpu.VMEM((cols, tokens), bf16)
    piece = pltpu.VMEM((4, PAD, 4 * cols), bf16)
    block = pltpu.VMEM((PAD, 4 * cols), bf16)
    carry = pltpu.VMEM((FRAME, each, width + 128), bf16)
    dma = pltpu.SemaphoreType.DMA
    return pl.pallas_call(
        layer_kernel,
        out_shape=[
            jax.ShapeDtypeStruct((3, ROWS, cols), f32),
            jax.ShapeDtypeStruct((ROWS, cols), f32),
            jax.ShapeDtypeStruct((tokens, width), bf16),
        ],
        in_specs=[anywhere, vmem, vmem, anywhere, anywhere, anywhere],
        out_specs=[vmem, vmem, vmem],
        scratch_shapes=[
            pltpu.VMEM((FRAME, each, width), bf16),
            wide,
            carry,
            carry,
            pltpu.VMEM((3 * cols, width), bf16),
            pltpu.VMEM((cols, width), bf16),
            pltpu.VMEM((cols, width), bf16),
            pltpu.VMEM(table.shape, bf16),
            wide,
            pltpu.VMEM((tokens, 128), f32),
            wide,
            pltpu.VMEM((3 * n_heads, HEAD_DIM, tokens), bf16),
            narrow,
            narrow,
            pltpu.VMEM((tokens // 128 * n_heads, 128, 128), f32),
            wide,
            pltpu.VMEM((n_heads, HEAD_DIM, tokens // 2), bf16),
            pltpu.VMEM((2 * n_heads, 128, 128), bf16),
            pltpu.VMEM((3 * cols, tokens), bf16),
            pltpu.VMEM((4, 2, 64, width), bf16),
            pltpu.VMEM((4, 64, width), bf16),
            pltpu.VMEM((FRAME * PAD, tokens), bf16),
            pltpu.VMEM((FRAME * PAD, tokens), bf16),
            pltpu.VMEM((FRAME * PAD // 2, tokens), bf16),
            pltpu.VMEM((FRAME * PAD // 2, tokens), bf16),
            pltpu.VMEM((3 * cols, tokens), bf16),
            narrow,
            pltpu.VMEM((FRAME // 2, PAD, 4 * cols), bf16),
        ]
        + [piece] * 6
        + [block] * 8
        + [pltpu.VMEM((2, PAD, 4 * cols), bf16), block]
        + [
            dma((4,)), dma, dma((2,)), dma((2,)),
            dma, dma((FRAME,)), dma((FRAME,)),
            dma, dma((FRAME // 2,)), dma((FRAME // 2,)), dma((FRAME // 2,)), dma((FRAME // 2,)),
            dma((2,)), dma((2,)), dma((2,)), dma((2,)),
            dma((2, 2)), dma((2, 2)), dma((2, 2)), dma((2, 2)), dma((6,)), dma((6,)), dma((6,)), dma((6,)), dma, dma,
        ],
        compiler_params=pltpu.CompilerParams(
            collective_id=0, has_side_effects=True, vmem_limit_bytes=VMEM_LIMIT
        ),
        name="layer",
    )(clip, ids, gain, w_qkv, w_out, table)


def body(clip, gain, w_qkv, w_out, old_table, target_ids):
    frames_here, patches, width = clip.shape
    cols = w_qkv.shape[2]
    tokens = frames_here * patches

    d_qkv, d_out, d_clip = layer(
        clip.reshape(tokens, width),
        target_ids,
        gain,
        w_qkv.transpose(0, 2, 1).reshape(3 * cols, width),
        w_out,
        old_table,
    )
    return d_clip.reshape(frames_here, patches, width), d_qkv, d_out.T


def solution(mesh):
    return jax.shard_map(
        body,
        mesh=mesh,
        in_specs=(
            P("frame", None, None),
            P(),
            P(None, None, "chan"),
            P("chan", None),
            P(),
            P("frame", None),
        ),
        out_specs=(P("frame", None, None), P(None, "frame", "chan"), P("chan", "frame")),
        check_vma=False,
    )
```

```python
import functools

import jax
import jax.numpy as jnp
from jax import lax
from jax.experimental import pallas as pl
from jax.experimental.pallas import tpu as pltpu
from jax.sharding import PartitionSpec as P

HEAD_DIM = 88
EPS = 1e-05
VMEM_LIMIT = 63 * 2**20
XH, Y, Z, CORE = 2, 4, 4, 2
FRAME = XH * Y * Z * CORE
ROWS = 22
PAD = 24

f32 = jnp.float32
bf16 = jnp.bfloat16


def frame_index(xh, y, z, core):
    return ((xh * Y + y) * Z + z) * CORE + core


def coordinates():
    f = lax.axis_index("frame")
    return f // (Y * Z * CORE), (f // (Z * CORE)) % Y, (f // CORE) % Z, f % CORE


def all_peer(k):
    f = lax.axis_index("frame")
    chan = lax.axis_index("chan")
    p = (f + k) % FRAME
    far = (p // (FRAME // 2) + f // (FRAME // 2)) % 2
    return p, {"frame": p, "chan": (chan + far) % 2}


def greet(peer):
    pl.semaphore_signal(
        pltpu.get_barrier_semaphore(), inc=1, device_id=peer, device_id_type=pl.DeviceIdType.MESH
    )


def part(ref, i, width):
    return ref.at[i, :, pl.ds(0, width)]


def all_copy(src, dst, sends, recvs, k, width):
    p, peer = all_peer(k)
    return pltpu.make_async_remote_copy(
        src_ref=part(src, p, width), dst_ref=part(dst, lax.axis_index("frame"), width),
        send_sem=sends.at[k], recv_sem=recvs.at[k],
        device_id=peer, device_id_type=pl.DeviceIdType.MESH,
    )


def wait_all(src, dst, sends, recvs, own_sem, width):
    f = lax.axis_index("frame")
    pltpu.make_async_copy(part(src, f, width), part(dst, f, width), own_sem).wait()

    def wait(k, _):
        all_copy(src, dst, sends, recvs, k, width).wait_recv()
        return 0

    lax.fori_loop(1, FRAME, wait, 0)


def drain_all(src, dst, sends, recvs, width):
    def drain(k, _):
        all_copy(src, dst, sends, recvs, k, width).wait_send()
        return 0

    lax.fori_loop(1, FRAME, drain, 0)


def dot(a, b):
    return jnp.dot(a, b, preferred_element_type=f32)


def dot_nt(a, b):
    return lax.dot_general(a, b, (((1,), (1,)), ((), ())), preferred_element_type=f32)


def dot_tn(a, b):
    return lax.dot_general(a, b, (((0,), (0,)), ((), ())), preferred_element_type=f32)


def alone(run):
    def once(i, _):
        run()
        return 0

    lax.fori_loop(0, lax.axis_index("chan") // 2 + 1, once, 0)


def iota(shape, dim):
    return lax.broadcasted_iota(jnp.int32, shape, dim)


def norm_terms(x):
    centered = x - jnp.mean(x, axis=-1, keepdims=True)
    rstd = lax.rsqrt(jnp.mean(centered * centered, axis=-1, keepdims=True) + EPS)
    return centered * rstd, rstd


def add_blocks(out, terms, count):
    def step(j, _):
        total = terms[0][j].astype(f32)
        for t in terms[1:]:
            total = total + t[j].astype(f32)
        out[j] = total.astype(out.dtype)
        return 0

    lax.fori_loop(0, count, step, 0)


def layer_kernel(
    clip, ids, gain, w_qkv_hbm, w_out_hbm, table_hbm, out, d_recv,
    x_v, leave, r, w_qkv, w_out, w_other, table,
    x_s, ids_s, n_s, qkv_s, o_s, oo_s, p_s, dy_s, do_s, ds_s, d_s, dn_s, dno_s, n_t, dy_t,
    nt_x, dyt_x, d_x, o_x, g, r1, l1, r2, l2, r3, l3, br1, bl1, br2, bl2, br3, bl3, bmr, bml, u, xr,
    load_sem, w_sem, w_send, w_recv, own_sem, all_send, all_recv, home_own, home_send, home_recv, on_send, on_recv,
    o_send, o_recv, dn_send, dn_recv,
    ox_sems, ntx_sems, dyx_sems, dx_sems, a_send, a_recv, b_send, b_recv, x_send, x_recv,
):
    xh, y, z, core = coordinates()
    chan = lax.axis_index("chan")
    tokens, width = x_v.shape
    cols = o_s.shape[0]
    n_heads = cols // HEAD_DIM
    half = tokens // 2
    scale = HEAD_DIM ** (-0.5)
    kept = (xh + chan + core) % 2
    here = y * (1 - core) + z * core
    there = z * (1 - core) + y * core

    def ring(first, step):
        dy = step if first else 0
        dz = 0 if first else step
        ny = (y + (1 - core) * dy + core * dz + Y) % Y
        nz = (z + core * dy + (1 - core) * dz + Z) % Z
        return {"frame": frame_index(xh, ny, nz, core)}

    sibling = {"frame": frame_index(xh, y, z, 1 - core)}
    across = {"frame": frame_index(1 - xh, y, z, core)}
    partner = {"chan": 1 - chan}

    def remote(src, dst, send, recv, peer):
        return pltpu.make_async_remote_copy(
            src_ref=src, dst_ref=dst, send_sem=send, recv_sem=recv,
            device_id=peer, device_id_type=pl.DeviceIdType.MESH,
        )

    loads = [
        pltpu.make_async_copy(clip, x_v, load_sem.at[0]),
        pltpu.make_async_copy(w_out_hbm, w_out, load_sem.at[1]),
        pltpu.make_async_copy(w_qkv_hbm, w_qkv, load_sem.at[2]),
        pltpu.make_async_copy(table_hbm, table, load_sem.at[3]),
    ]
    for c in loads:
        c.start()
    def greet_some(k, _):
        greet(all_peer(k)[1])
        return 0

    lax.fori_loop(1, FRAME, greet_some, 0)
    greet(partner)
    greet(across)

    loads[0].wait()
    gain_row = gain[...].astype(f32).reshape(1, width)
    id_row = jnp.concatenate([ids[0:1, :], ids[1:2, :]], axis=1).astype(f32)

    me = lax.axis_index("frame")

    def leaving(i, _):
        j = (me // 16 + i) % 4
        t = iota((128, tokens), 0) + j * 128
        source = (t % 2) * half + (t // 8) * 4 + t % 8 // 2
        pick = iota((128, tokens), 1) == source
        to = pl.ds(j * 16, 16)
        moved = dot(pick.astype(bf16), x_v[...])
        leave[to, :, :width] = moved.reshape(16, 8, width).astype(bf16)
        id_here = jnp.sum(jnp.where(pick, id_row, 0.0), axis=1, keepdims=True)
        high = jnp.floor(id_here * (1.0 / 32.0))
        lane = iota((128, 128), 1)
        pair = jnp.where(lane == 0, high, jnp.where(lane == 1, id_here - high * 32.0, 0.0))
        leave[to, :, width:] = pair.reshape(16, 8, 128).astype(bf16)

        def start(d, _):
            p = j * 16 + (me + d) % 16
            k = (p - me + FRAME) % FRAME

            @pl.when(k != 0)
            def _():
                all_copy(leave, r, all_send, all_recv, k, width + 128).start()

            @pl.when(k == 0)
            def _():
                pltpu.make_async_copy(
                    part(leave, me, width + 128), part(r, me, width + 128), own_sem
                ).start()

            return 0

        lax.fori_loop(0, 16, start, 0)
        return 0

    pl.semaphore_wait(pltpu.get_barrier_semaphore(), FRAME + 1)
    lax.fori_loop(0, 4, leaving, 0)
    loads[1].wait()

    rows_half = cols // 2
    own_rows = pl.ds(pl.multiple_of(core * rows_half, 16), rows_half)
    w_first = remote(w_out.at[own_rows], w_other.at[own_rows], w_send.at[0], w_recv.at[0], partner)
    w_first.start()
    wait_all(leave, r, all_send, all_recv, own_sem, width + 128)
    loads[2].wait()
    loads[3].wait()

    def rows(c):
        return pl.ds(pl.multiple_of(c * half, half), half)

    def swap_o(c):
        return remote(o_s.at[:, rows(c)], oo_s.at[:, rows(c)], o_send.at[c], o_recv.at[c], partner)

    def swap_dn(c):
        two = pl.ds(2 * c, 2)
        return remote(
            dn_s.at[two, 1 - kept], dno_s.at[two], dn_send.at[c], dn_recv.at[c], partner
        )

    half_rows = FRAME * PAD // 2
    theirs = pl.ds(pl.multiple_of((1 - core) * half_rows, half_rows), half_rows)
    ours = pl.ds(pl.multiple_of(core * half_rows, half_rows), half_rows)

    def swap_core(src, dst, sems, c):
        return remote(src, dst, sems.at[0, c], sems.at[1, c], sibling)

    def swap_ox(c):
        return swap_core(o_s.at[:, rows(c)], o_x.at[:, rows(c)], ox_sems, c)

    def swap_ntx(c):
        return swap_core(n_t.at[theirs, rows(c)], nt_x.at[:, rows(c)], ntx_sems, c)

    def swap_dyx(c):
        return swap_core(dy_t.at[theirs, rows(c)], dyt_x.at[:, rows(c)], dyx_sems, c)

    def swap_dx(c):
        return swap_core(d_s.at[:, rows(c)], d_x.at[:, rows(c)], dx_sems, c)

    def patch(c, pp):
        return pl.ds(pl.multiple_of(c * half + pp * 128, 128), 128)

    def forward(c, _):
        t = iota((half, tokens), 0)
        source = (t % 128 // 2) * 8 + 2 * (2 * c + t // 128) + t % 2
        pick = (iota((half, tokens), 1) == source).astype(bf16)
        moved = dot(pick, r[...].reshape(tokens, width + 128))
        x = moved[:, :width]
        x_s[rows(c), :] = x.astype(bf16)
        ids_s[rows(c), :] = moved[:, width:]
        xhat, _ = norm_terms(x)
        normed = (xhat * gain_row).astype(bf16)
        n_s[rows(c), :] = normed
        for i in range(3):
            qkv = dot_nt(w_qkv[i * cols : (i + 1) * cols, :], normed)
            for h in range(n_heads):
                qkv_s[i * n_heads + h, :, rows(c)] = qkv[
                    h * HEAD_DIM : (h + 1) * HEAD_DIM
                ].astype(bf16)
        alone(functools.partial(forward_heads, c))
        swap_o(c).start()
        swap_ox(c).start()
        return 0

    def forward_heads(c):
        for pp in range(2):
            at = patch(c, pp)
            for h in range(n_heads):
                scores = dot_tn(qkv_s[n_heads + h, :, at], qkv_s[h, :, at]) * scale
                expo = jnp.exp(scores - jnp.max(scores, axis=0, keepdims=True))
                probs = expo * (1.0 / jnp.sum(expo, axis=0, keepdims=True))
                p_s[(2 * c + pp) * n_heads + h] = probs
                o_s[h * HEAD_DIM : (h + 1) * HEAD_DIM, at] = dot(
                    qkv_s[2 * n_heads + h, :, at], probs.astype(bf16)
                ).astype(bf16)

    lax.fori_loop(0, 2, forward, 0)

    block = 8 * ROWS
    window = 384

    def columns(source, target, c):
        for k in range(width // block):
            start = min(k * block // 128, (width - window) // 128) * 128
            shape = (8 * PAD, window)
            at = iota(shape, 0)
            wanted = jnp.where(
                at % PAD < ROWS, k * block + (at // PAD) * ROWS + at % PAD - start, -1
            )
            pick = (iota(shape, 1) == wanted).astype(bf16)
            picked = dot_nt(pick, source[rows(c), start : start + window])
            for j in range(8):
                cj, zj = j % 2, j // 2
                a, b = (k % Y, zj) if cj == 0 else (zj, k % Y)
                to = (((cj * 4 + a) * 2 + k // Y) * 4 + b) * PAD
                target[to : to + PAD, rows(c)] = picked[j * PAD : (j + 1) * PAD].astype(bf16)

    def targets(c, _):
        hi_lo = ids_s[rows(c), :]
        wanted = hi_lo[:, 0:1] * 32.0 + hi_lo[:, 1:2]
        n_old = table.shape[0]
        pick = (iota((half, n_old), 1).astype(f32) == wanted).astype(bf16)
        x_v[rows(c), :] = dot(pick, table[...]).astype(bf16)
        alone(functools.partial(columns, n_s, n_t, c))
        swap_ntx(c).start()
        return 0

    w_first.wait_recv()
    w_second = remote(
        w_other.at[own_rows], w_other.at[own_rows], w_send.at[1], w_recv.at[1], sibling
    )
    w_second.start()
    lax.fori_loop(0, 2, targets, 0)
    w_second.wait_recv()

    def backward(c, _):
        swap_o(c).wait_recv()
        branch = dot_tn(o_s[:, rows(c)], w_out[...]) + dot_tn(oo_s[:, rows(c)], w_other[...])
        d_y = (x_s[rows(c), :].astype(f32) + branch - x_v[rows(c), :].astype(f32)).astype(bf16)
        dy_s[rows(c), :] = d_y
        alone(functools.partial(columns, dy_s, dy_t, c))
        swap_dyx(c).start()
        d_o = dot_nt(w_out[...], d_y)
        for h in range(n_heads):
            do_s[h] = d_o[h * HEAD_DIM : (h + 1) * HEAD_DIM].astype(bf16)
        alone(functools.partial(score_heads, c))
        alone(functools.partial(value_heads, c))
        swap_dx(c).start()
        dn = dot_tn(d_s[:, rows(c)], w_qkv[...])
        dn_s[pl.ds(2 * c, 2)] = dn.reshape(2, 2, 64, width).astype(bf16)
        swap_dn(c).start()
        return 0

    def score_heads(c):
        for pp in range(2):
            at = patch(c, pp)
            for h in range(n_heads):
                probs = p_s[(2 * c + pp) * n_heads + h]
                d_oh = do_s[h, :, pp * 128 : (pp + 1) * 128]
                dprobs = dot_tn(qkv_s[2 * n_heads + h, :, at], d_oh)
                rowsum = jnp.sum(dprobs * probs, axis=0, keepdims=True)
                ds = (probs * (dprobs - rowsum) * scale).astype(bf16)
                ds_s[pp * n_heads + h] = ds
                d_s[h * HEAD_DIM : (h + 1) * HEAD_DIM, at] = dot(
                    qkv_s[n_heads + h, :, at], ds
                ).astype(bf16)

    def value_heads(c):
        for pp in range(2):
            at = patch(c, pp)
            for h in range(n_heads):
                lo, hi = h * HEAD_DIM, (h + 1) * HEAD_DIM
                probs = p_s[(2 * c + pp) * n_heads + h].astype(bf16)
                d_oh = do_s[h, :, pp * 128 : (pp + 1) * 128]
                d_s[cols + lo : cols + hi, at] = dot_nt(
                    qkv_s[h, :, at], ds_s[pp * n_heads + h]
                ).astype(bf16)
                d_s[2 * cols + lo : 2 * cols + hi, at] = dot_nt(d_oh, probs).astype(bf16)

    lax.fori_loop(0, 2, backward, 0)

    def piece(a, h):
        return g.at[pl.ds(((here + a) % 4 * 2 + h) * 4, 4)]

    copies = []

    def plan(src, dst, k, peer, sends, recvs):
        c = remote(src, dst, sends.at[k], recvs.at[k], peer)
        copies.append(c)
        return c

    def send(*what):
        c = plan(*what)
        c.start()
        return c

    right, left = ring(True, 1), ring(True, -1)
    c1r = plan(piece(2, 0), r1, 0, right, a_send, a_recv)
    c1l = plan(piece(2, 1), l1, 1, left, a_send, a_recv)
    c2r = plan(piece(1, 1), r2, 2, right, a_send, a_recv)
    c2l = plan(piece(3, 0), l2, 3, left, a_send, a_recv)
    for c in range(2):
        swap_ntx(c).wait_recv()
        swap_ox(c).wait_recv()
        swap_dyx(c).wait_recv()
        swap_dx(c).wait_recv()

    def weight_grads(i, _):
        a = (here + jnp.where(i < 2, 2 - i, 5 - i - (i // 3) * 2)) % 4
        at = pl.ds(pl.multiple_of((core * 4 + a) * 8 * PAD, 8 * PAD), 8 * PAD)
        at_x = pl.ds(pl.multiple_of(a * 8 * PAD, 8 * PAD), 8 * PAD)
        to = pl.ds(a * 8, 8)
        part = dot_nt(n_t[at, :], d_s[...]) + dot_nt(nt_x[at_x, :], d_x[...])
        g[to, :, : 3 * cols] = part.reshape(8, PAD, 3 * cols).astype(bf16)
        part = dot_nt(dy_t[at, :], o_s[...]) + dot_nt(dyt_x[at_x, :], o_x[...])
        g[to, :, 3 * cols :] = part.reshape(8, PAD, cols).astype(bf16)

        @pl.when(i == 0)
        def _():
            c1r.start()
            c1l.start()

        @pl.when(i == 1)
        def _():
            c2r.start()

        @pl.when(i == 2)
        def _():
            c2l.start()

        return 0

    lax.fori_loop(0, 4, weight_grads, 0)

    drain_all(leave, r, all_send, all_recv, width + 128)

    def finish(p, _):
        @pl.when(p % 2 == 0)
        def _():
            swap_dn(p // 2).wait_recv()

        at = pl.ds(pl.multiple_of(p * 128 + kept * 64, 64), 64)
        dn = dn_s[p, kept].astype(f32) + dno_s[p].astype(f32)
        xhat, rstd = norm_terms(x_s[at, :].astype(f32))
        gs = dn * gain_row
        back = rstd * (
            gs
            - jnp.mean(gs, axis=-1, keepdims=True)
            - xhat * jnp.mean(gs * xhat, axis=-1, keepdims=True)
        )
        x_v[pl.ds(pl.multiple_of(p * 64, 64), 64), :] = (
            dy_s[at, :].astype(f32) + back
        ).astype(bf16)
        return 0

    lax.fori_loop(0, 4, finish, 0)

    def to_home(j, _):
        t = iota((128, half), 0) + j * 128
        source = (t % 8 // 2) * 64 + 2 * (t // 8) + t % 2
        pick = (iota((128, half), 1) == source).astype(bf16)
        leave[pl.ds(j * 16, 16), :, :width] = (
            dot(pick, x_v[pl.ds(0, half), :]).reshape(16, 8, width).astype(bf16)
        )
        return 0

    lax.fori_loop(0, 2, to_home, 0)

    f = lax.axis_index("frame")
    spots = FRAME // 2
    spot = f % spots
    own = core == chan

    def home_copy(k):
        q = (spot + k) % spots
        return remote(
            part(leave, q, width), d_recv.at[f], home_send.at[k], home_recv.at[f // 2],
            {"frame": kept * spots + q, "chan": core},
        )

    home_local = pltpu.make_async_copy(part(leave, spot, width), d_recv.at[f], home_own)

    def home_each(run, run_own):
        @pl.when(own)
        def _():
            run_own()

        @pl.when(jnp.logical_not(own))
        def _():
            run(home_copy(0))

        def step(k, _):
            run(home_copy(k))
            return 0

        lax.fori_loop(1, spots, step, 0)

    def pass_on(i):
        return remote(d_recv.at[i], d_recv.at[i], on_send.at[i // 2], on_recv.at[i // 2], partner)

    def landed(k, _):
        k = 2 * k + (core + chan) % 2
        for n in range(2):
            source = n * spots + (spot - k + spots) % spots
            local = jnp.logical_and(source == f, own)

            @pl.when(local)
            def _():
                home_local.wait()

            @pl.when(jnp.logical_not(local))
            def _(source=source):
                remote(
                    part(leave, 0, width), d_recv.at[source], home_send.at[0],
                    home_recv.at[source // 2], partner,
                ).wait_recv()

            pass_on(source).start()
        return 0

    def passed_on(run):
        def step(i, _):
            run(i)
            return 0

        lax.fori_loop(0, spots, step, 0)

    home_each(lambda c: c.start(), home_local.start)
    c1r.wait_recv()
    add_blocks(piece(1, 0), (piece(1, 0), r1), 4)
    c3r = send(piece(1, 0), r3, 4, right, a_send, a_recv)
    c1l.wait_recv()
    add_blocks(piece(3, 1), (piece(3, 1), l1), 4)
    c3l = send(piece(3, 1), l3, 5, left, a_send, a_recv)
    lax.fori_loop(0, 8, landed, 0)
    c2l.wait_recv()
    c3r.wait_recv()
    add_blocks(piece(0, 0), (piece(0, 0), r3, l2), 4)
    c2r.wait_recv()
    c3l.wait_recv()
    add_blocks(piece(0, 1), (piece(0, 1), r2, l3), 4)

    right, left = ring(False, 1), ring(False, -1)
    at = lambda h, d: g.at[(here * 2 + h) * 4 + (there + d) % 4]
    d1r = send(at(0, 2), br1, 0, right, b_send, b_recv)
    d1l = send(at(1, 2), bl1, 1, left, b_send, b_recv)
    d2r = send(at(1, 1), br2, 2, right, b_send, b_recv)
    d2l = send(at(0, 3), bl2, 3, left, b_send, b_recv)
    lax.fori_loop(8, spots // 2, landed, 0)
    d1r.wait_recv()
    bmr[...] = (at(0, 1)[...].astype(f32) + br1[...].astype(f32)).astype(bf16)
    d3r = send(bmr, br3, 4, right, b_send, b_recv)
    d1l.wait_recv()
    bml[...] = (at(1, 3)[...].astype(f32) + bl1[...].astype(f32)).astype(bf16)
    d3l = send(bml, bl3, 5, left, b_send, b_recv)
    d2l.wait_recv()
    d3r.wait_recv()
    u[0] = (at(0, 0)[...].astype(f32) + br3[...].astype(f32) + bl2[...].astype(f32)).astype(bf16)
    d2r.wait_recv()
    d3l.wait_recv()
    u[1] = (at(1, 0)[...].astype(f32) + br2[...].astype(f32) + bl3[...].astype(f32)).astype(bf16)

    e = remote(u.at[1 - xh], xr, x_send, x_recv, across)
    e.start()
    e.wait_recv()
    out[...] = u[xh].astype(f32) + xr[...].astype(f32)
    passed_on(lambda i: pass_on(2 * i + 1 - chan).wait_recv())

    e.wait_send()
    w_first.wait_send()
    w_second.wait_send()
    for c in copies:
        c.wait_send()
    for c in range(2):
        swap_o(c).wait_send()
        swap_dn(c).wait_send()
        swap_ox(c).wait_send()
        swap_ntx(c).wait_send()
        swap_dyx(c).wait_send()
        swap_dx(c).wait_send()
    home_each(lambda c: c.wait_send(), lambda: None)
    passed_on(lambda i: pass_on(2 * i + chan).wait_send())


def layer(clip, ids, gain, w_qkv, w_out, table):
    tokens, width = clip.shape
    cols = w_out.shape[0]
    n_heads = cols // HEAD_DIM
    each = tokens // FRAME
    vmem = pl.BlockSpec(memory_space=pltpu.VMEM)
    anywhere = pl.BlockSpec(memory_space=pl.ANY)
    wide = pltpu.VMEM((tokens, width), bf16)
    narrow = pltpu.VMEM((cols, tokens), bf16)
    piece = pltpu.VMEM((4, PAD, 4 * cols), bf16)
    block = pltpu.VMEM((PAD, 4 * cols), bf16)
    carry = pltpu.VMEM((FRAME, each, width + 128), bf16)
    dma = pltpu.SemaphoreType.DMA
    return pl.pallas_call(
        layer_kernel,
        out_shape=[
            jax.ShapeDtypeStruct((PAD, 4 * cols), f32),
            jax.ShapeDtypeStruct((FRAME, each, width), bf16),
        ],
        in_specs=[anywhere, vmem, vmem, anywhere, anywhere, anywhere],
        out_specs=[vmem, vmem],
        scratch_shapes=[
            wide,
            carry,
            carry,
            pltpu.VMEM((3 * cols, width), bf16),
            pltpu.VMEM((cols, width), bf16),
            pltpu.VMEM((cols, width), bf16),
            pltpu.VMEM(table.shape, bf16),
            wide,
            pltpu.VMEM((tokens, 128), f32),
            wide,
            pltpu.VMEM((3 * n_heads, HEAD_DIM, tokens), bf16),
            narrow,
            narrow,
            pltpu.VMEM((tokens // 128 * n_heads, 128, 128), f32),
            wide,
            pltpu.VMEM((n_heads, HEAD_DIM, tokens // 2), bf16),
            pltpu.VMEM((2 * n_heads, 128, 128), bf16),
            pltpu.VMEM((3 * cols, tokens), bf16),
            pltpu.VMEM((4, 2, 64, width), bf16),
            pltpu.VMEM((4, 64, width), bf16),
            pltpu.VMEM((FRAME * PAD, tokens), bf16),
            pltpu.VMEM((FRAME * PAD, tokens), bf16),
            pltpu.VMEM((FRAME * PAD // 2, tokens), bf16),
            pltpu.VMEM((FRAME * PAD // 2, tokens), bf16),
            pltpu.VMEM((3 * cols, tokens), bf16),
            narrow,
            pltpu.VMEM((FRAME // 2, PAD, 4 * cols), bf16),
        ]
        + [piece] * 6
        + [block] * 8
        + [pltpu.VMEM((2, PAD, 4 * cols), bf16), block]
        + [
            dma((4,)), dma, dma((2,)), dma((2,)),
            dma, dma((FRAME,)), dma((FRAME,)),
            dma, dma((FRAME // 2,)), dma((FRAME // 2,)), dma((FRAME // 2,)), dma((FRAME // 2,)),
            dma((2,)), dma((2,)), dma((2,)), dma((2,)),
            dma((2, 2)), dma((2, 2)), dma((2, 2)), dma((2, 2)), dma((6,)), dma((6,)), dma((6,)), dma((6,)), dma, dma,
        ],
        compiler_params=pltpu.CompilerParams(
            collective_id=0, has_side_effects=True, vmem_limit_bytes=VMEM_LIMIT
        ),
        name="layer",
    )(clip, ids, gain, w_qkv, w_out, table)


def settle_kernel(total, d_recv, d_qkv, d_out, d_clip):
    cols = d_out.shape[1]
    half, width = d_clip.shape[0] // 2, d_clip.shape[1]
    for i in range(3):
        d_qkv[i] = total[:ROWS, i * cols : (i + 1) * cols]
    d_out[...] = total[:ROWS, 3 * cols :]
    for h in range(2):
        t = iota((half, half), 0)
        source = (t % 128 // 4) * 8 + (t % 4) * 2 + t // 128
        pick = (iota((half, half), 1) == source).astype(bf16)
        landed = d_recv[h * (FRAME // 2) : (h + 1) * (FRAME // 2)].reshape(half, width)
        moved = dot(pick, landed).astype(bf16)
        d_clip[h * 128 : (h + 1) * 128, :] = moved[:128]
        d_clip[half + h * 128 : half + (h + 1) * 128, :] = moved[128:]


def settle(total, d_recv):
    cols = total.shape[1] // 4
    vmem = pl.BlockSpec(memory_space=pltpu.VMEM)
    return pl.pallas_call(
        settle_kernel,
        out_shape=[
            jax.ShapeDtypeStruct((3, ROWS, cols), f32),
            jax.ShapeDtypeStruct((ROWS, cols), f32),
            jax.ShapeDtypeStruct((d_recv.shape[0] * d_recv.shape[1], d_recv.shape[2]), bf16),
        ],
        in_specs=[vmem, vmem],
        out_specs=[vmem, vmem, vmem],
        compiler_params=pltpu.CompilerParams(vmem_limit_bytes=32 * 2**20),
        name="settle",
    )(total, d_recv)


def body(clip, gain, w_qkv, w_out, old_table, target_ids):
    frames_here, patches, width = clip.shape
    cols = w_qkv.shape[2]
    tokens = frames_here * patches

    total, d_recv = layer(
        clip.reshape(tokens, width),
        target_ids,
        gain,
        w_qkv.transpose(0, 2, 1).reshape(3 * cols, width),
        w_out,
        old_table,
    )
    d_qkv, d_out, d_clip = settle(total, d_recv)
    return d_clip.reshape(frames_here, patches, width), d_qkv, d_out.T


def solution(mesh):
    return jax.shard_map(
        body,
        mesh=mesh,
        in_specs=(
            P("frame", None, None),
            P(),
            P(None, None, "chan"),
            P("chan", None),
            P(),
            P("frame", None),
        ),
        out_specs=(P("frame", None, None), P(None, "frame", "chan"), P("chan", "frame")),
        check_vma=False,
    )
```

```python
import functools

import jax
import jax.numpy as jnp
from jax import lax
from jax.experimental import pallas as pl
from jax.experimental.pallas import tpu as pltpu
from jax.sharding import PartitionSpec as P

HEAD_DIM = 88
EPS = 1e-05
VMEM_LIMIT = 63 * 2**20
XH, Y, Z, CORE = 2, 4, 4, 2
FRAME = XH * Y * Z * CORE
ROWS = 22
PAD = 24

f32 = jnp.float32
bf16 = jnp.bfloat16


def frame_index(xh, y, z, core):
    return ((xh * Y + y) * Z + z) * CORE + core


def coordinates():
    f = lax.axis_index("frame")
    return f // (Y * Z * CORE), (f // (Z * CORE)) % Y, (f // CORE) % Z, f % CORE


def all_peer(k):
    f = lax.axis_index("frame")
    chan = lax.axis_index("chan")
    p = (f + k) % FRAME
    far = (p // (FRAME // 2) + f // (FRAME // 2)) % 2
    return p, {"frame": p, "chan": (chan + far) % 2}


def greet(peer):
    pl.semaphore_signal(
        pltpu.get_barrier_semaphore(), inc=1, device_id=peer, device_id_type=pl.DeviceIdType.MESH
    )


def part(ref, i, width):
    return ref.at[i, :, pl.ds(0, width)]


def all_copy(src, dst, sends, recvs, k, width):
    p, peer = all_peer(k)
    return pltpu.make_async_remote_copy(
        src_ref=part(src, p, width), dst_ref=part(dst, lax.axis_index("frame"), width),
        send_sem=sends.at[k], recv_sem=recvs.at[k],
        device_id=peer, device_id_type=pl.DeviceIdType.MESH,
    )


def wait_all(src, dst, sends, recvs, own_sem, width):
    f = lax.axis_index("frame")
    pltpu.make_async_copy(part(src, f, width), part(dst, f, width), own_sem).wait()

    def wait(k, _):
        all_copy(src, dst, sends, recvs, k, width).wait_recv()
        return 0

    lax.fori_loop(1, FRAME, wait, 0)


def drain_all(src, dst, sends, recvs, width):
    def drain(k, _):
        all_copy(src, dst, sends, recvs, k, width).wait_send()
        return 0

    lax.fori_loop(1, FRAME, drain, 0)


def dot(a, b):
    return jnp.dot(a, b, preferred_element_type=f32)


def dot_nt(a, b):
    return lax.dot_general(a, b, (((1,), (1,)), ((), ())), preferred_element_type=f32)


def dot_tn(a, b):
    return lax.dot_general(a, b, (((0,), (0,)), ((), ())), preferred_element_type=f32)


def alone(run):
    def once(i, _):
        run()
        return 0

    lax.fori_loop(0, lax.axis_index("chan") // 2 + 1, once, 0)


def iota(shape, dim):
    return lax.broadcasted_iota(jnp.int32, shape, dim)


def norm_terms(x):
    centered = x - jnp.mean(x, axis=-1, keepdims=True)
    rstd = lax.rsqrt(jnp.mean(centered * centered, axis=-1, keepdims=True) + EPS)
    return centered * rstd, rstd


def add_blocks(out, terms, count):
    def step(j, _):
        total = terms[0][j].astype(f32)
        for t in terms[1:]:
            total = total + t[j].astype(f32)
        out[j] = total.astype(out.dtype)
        return 0

    lax.fori_loop(0, count, step, 0)


def layer_kernel(
    clip, ids, gain, w_qkv_hbm, w_out_hbm, table_hbm, out, d_recv,
    x_v, leave, r, w_qkv, w_out, w_other, table,
    x_s, ids_s, n_s, qkv_s, o_s, oo_s, p_s, dy_s, do_s, ds_s, d_s, dn_s, dno_s, n_t, dy_t,
    nt_x, dyt_x, d_x, o_x, g, r1, l1, r2, l2, r3, l3, br1, bl1, br2, bl2, br3, bl3, bmr, bml, u, xr,
    load_sem, w_sem, w_send, w_recv, own_sem, all_send, all_recv, home_own, home_send, home_recv, on_send, on_recv,
    o_send, o_recv, dn_send, dn_recv,
    ox_sems, ntx_sems, dyx_sems, dx_sems, a_send, a_recv, b_send, b_recv, x_send, x_recv,
):
    xh, y, z, core = coordinates()
    chan = lax.axis_index("chan")
    tokens, width = x_v.shape
    cols = o_s.shape[0]
    n_heads = cols // HEAD_DIM
    half = tokens // 2
    scale = HEAD_DIM ** (-0.5)
    kept = (xh + chan + core) % 2
    here = y * (1 - core) + z * core
    there = z * (1 - core) + y * core

    def ring(first, step):
        dy = step if first else 0
        dz = 0 if first else step
        ny = (y + (1 - core) * dy + core * dz + Y) % Y
        nz = (z + core * dy + (1 - core) * dz + Z) % Z
        return {"frame": frame_index(xh, ny, nz, core)}

    sibling = {"frame": frame_index(xh, y, z, 1 - core)}
    across = {"frame": frame_index(1 - xh, y, z, core)}
    partner = {"chan": 1 - chan}

    def remote(src, dst, send, recv, peer):
        return pltpu.make_async_remote_copy(
            src_ref=src, dst_ref=dst, send_sem=send, recv_sem=recv,
            device_id=peer, device_id_type=pl.DeviceIdType.MESH,
        )

    loads = [
        pltpu.make_async_copy(clip, x_v, load_sem.at[0]),
        pltpu.make_async_copy(w_out_hbm, w_out, load_sem.at[1]),
        pltpu.make_async_copy(w_qkv_hbm, w_qkv, load_sem.at[2]),
        pltpu.make_async_copy(table_hbm, table, load_sem.at[3]),
    ]
    for c in loads:
        c.start()
    def greet_some(k, _):
        greet(all_peer(k)[1])
        return 0

    lax.fori_loop(1, FRAME, greet_some, 0)
    greet(partner)
    greet(across)

    loads[0].wait()
    gain_row = gain[...].astype(f32).reshape(1, width)
    id_row = jnp.concatenate([ids[0:1, :], ids[1:2, :]], axis=1).astype(f32)

    me = lax.axis_index("frame")

    def leaving(i, _):
        j = (me // 16 + i) % 4
        t = iota((128, tokens), 0) + j * 128
        source = (t % 2) * half + (t // 8) * 4 + t % 8 // 2
        pick = iota((128, tokens), 1) == source
        to = pl.ds(j * 16, 16)
        moved = dot(pick.astype(bf16), x_v[...])
        leave[to, :, :width] = moved.reshape(16, 8, width).astype(bf16)
        id_here = jnp.sum(jnp.where(pick, id_row, 0.0), axis=1, keepdims=True)
        high = jnp.floor(id_here * (1.0 / 32.0))
        lane = iota((128, 128), 1)
        pair = jnp.where(lane == 0, high, jnp.where(lane == 1, id_here - high * 32.0, 0.0))
        leave[to, :, width:] = pair.reshape(16, 8, 128).astype(bf16)

        def start(d, _):
            p = j * 16 + (me + d) % 16
            k = (p - me + FRAME) % FRAME

            @pl.when(k != 0)
            def _():
                all_copy(leave, r, all_send, all_recv, k, width + 128).start()

            @pl.when(k == 0)
            def _():
                pltpu.make_async_copy(
                    part(leave, me, width + 128), part(r, me, width + 128), own_sem
                ).start()

            return 0

        lax.fori_loop(0, 16, start, 0)
        return 0

    pl.semaphore_wait(pltpu.get_barrier_semaphore(), FRAME + 1)
    lax.fori_loop(0, 4, leaving, 0)
    loads[1].wait()

    rows_half = cols // 2
    own_rows = pl.ds(pl.multiple_of(core * rows_half, 16), rows_half)
    w_first = remote(w_out.at[own_rows], w_other.at[own_rows], w_send.at[0], w_recv.at[0], partner)
    w_first.start()
    wait_all(leave, r, all_send, all_recv, own_sem, width + 128)
    loads[2].wait()
    loads[3].wait()

    def rows(c):
        return pl.ds(pl.multiple_of(c * half, half), half)

    def swap_o(c):
        return remote(o_s.at[:, rows(c)], oo_s.at[:, rows(c)], o_send.at[c], o_recv.at[c], partner)

    def swap_dn(c):
        two = pl.ds(2 * c, 2)
        return remote(
            dn_s.at[two, 1 - kept], dno_s.at[two], dn_send.at[c], dn_recv.at[c], partner
        )

    half_rows = FRAME * PAD // 2
    theirs = pl.ds(pl.multiple_of((1 - core) * half_rows, half_rows), half_rows)
    ours = pl.ds(pl.multiple_of(core * half_rows, half_rows), half_rows)

    def swap_core(src, dst, sems, c):
        return remote(src, dst, sems.at[0, c], sems.at[1, c], sibling)

    def swap_ox(c):
        return swap_core(o_s.at[:, rows(c)], o_x.at[:, rows(c)], ox_sems, c)

    def swap_ntx(c):
        return swap_core(n_t.at[theirs, rows(c)], nt_x.at[:, rows(c)], ntx_sems, c)

    def swap_dyx(c):
        return swap_core(dy_t.at[theirs, rows(c)], dyt_x.at[:, rows(c)], dyx_sems, c)

    def swap_dx(c):
        return swap_core(d_s.at[:, rows(c)], d_x.at[:, rows(c)], dx_sems, c)

    def patch(c, pp):
        return pl.ds(pl.multiple_of(c * half + pp * 128, 128), 128)

    def forward(c, _):
        t = iota((half, tokens), 0)
        source = (t % 128 // 2) * 8 + 2 * (2 * c + t // 128) + t % 2
        pick = (iota((half, tokens), 1) == source).astype(bf16)
        moved = dot(pick, r[...].reshape(tokens, width + 128))
        x = moved[:, :width]
        x_s[rows(c), :] = x.astype(bf16)
        ids_s[rows(c), :] = moved[:, width:]
        xhat, _ = norm_terms(x)
        normed = (xhat * gain_row).astype(bf16)
        n_s[rows(c), :] = normed
        for i in range(3):
            qkv = dot_nt(w_qkv[i * cols : (i + 1) * cols, :], normed)
            for h in range(n_heads):
                qkv_s[i * n_heads + h, :, rows(c)] = qkv[
                    h * HEAD_DIM : (h + 1) * HEAD_DIM
                ].astype(bf16)
        alone(functools.partial(forward_heads, c))
        swap_o(c).start()
        swap_ox(c).start()
        return 0

    def forward_heads(c):
        for pp in range(2):
            at = patch(c, pp)
            for h in range(n_heads):
                scores = dot_tn(qkv_s[n_heads + h, :, at], qkv_s[h, :, at]) * scale
                expo = jnp.exp(scores - jnp.max(scores, axis=0, keepdims=True))
                probs = expo * (1.0 / jnp.sum(expo, axis=0, keepdims=True))
                p_s[(2 * c + pp) * n_heads + h] = probs
                o_s[h * HEAD_DIM : (h + 1) * HEAD_DIM, at] = dot(
                    qkv_s[2 * n_heads + h, :, at], probs.astype(bf16)
                ).astype(bf16)

    lax.fori_loop(0, 2, forward, 0)

    block = 8 * ROWS
    window = 384

    def columns(source, target, c):
        for k in range(width // block):
            start = min(k * block // 128, (width - window) // 128) * 128
            shape = (8 * PAD, window)
            at = iota(shape, 0)
            wanted = jnp.where(
                at % PAD < ROWS, k * block + (at // PAD) * ROWS + at % PAD - start, -1
            )
            pick = (iota(shape, 1) == wanted).astype(bf16)
            picked = dot_nt(pick, source[rows(c), start : start + window])
            for j in range(8):
                cj, zj = j % 2, j // 2
                a, b = (k % Y, zj) if cj == 0 else (zj, k % Y)
                to = (((cj * 4 + a) * 2 + k // Y) * 4 + b) * PAD
                target[to : to + PAD, rows(c)] = picked[j * PAD : (j + 1) * PAD].astype(bf16)

    def targets(c, _):
        hi_lo = ids_s[rows(c), :]
        wanted = hi_lo[:, 0:1] * 32.0 + hi_lo[:, 1:2]
        n_old = table.shape[0]
        pick = (iota((half, n_old), 1).astype(f32) == wanted).astype(bf16)
        x_v[rows(c), :] = dot(pick, table[...]).astype(bf16)
        alone(functools.partial(columns, n_s, n_t, c))
        swap_ntx(c).start()
        return 0

    w_first.wait_recv()
    w_second = remote(
        w_other.at[own_rows], w_other.at[own_rows], w_send.at[1], w_recv.at[1], sibling
    )
    w_second.start()
    lax.fori_loop(0, 2, targets, 0)
    w_second.wait_recv()

    drain_all(leave, r, all_send, all_recv, width + 128)

    def backward(c, _):
        swap_o(c).wait_recv()
        branch = dot_tn(o_s[:, rows(c)], w_out[...]) + dot_tn(oo_s[:, rows(c)], w_other[...])
        d_y = (x_s[rows(c), :].astype(f32) + branch - x_v[rows(c), :].astype(f32)).astype(bf16)
        dy_s[rows(c), :] = d_y
        d_o = dot_nt(w_out[...], d_y)
        for h in range(n_heads):
            do_s[h] = d_o[h * HEAD_DIM : (h + 1) * HEAD_DIM].astype(bf16)
        alone(functools.partial(score_heads, c))
        alone(functools.partial(value_heads, c))
        swap_dx(c).start()
        dn = dot_tn(d_s[:, rows(c)], w_qkv[...])
        dn_s[pl.ds(2 * c, 2)] = dn.reshape(2, 2, 64, width).astype(bf16)
        swap_dn(c).start()
        alone(functools.partial(columns, dy_s, dy_t, c))
        swap_dyx(c).start()
        return 0

    def score_heads(c):
        for pp in range(2):
            at = patch(c, pp)
            for h in range(n_heads):
                probs = p_s[(2 * c + pp) * n_heads + h]
                d_oh = do_s[h, :, pp * 128 : (pp + 1) * 128]
                dprobs = dot_tn(qkv_s[2 * n_heads + h, :, at], d_oh)
                rowsum = jnp.sum(dprobs * probs, axis=0, keepdims=True)
                ds = (probs * (dprobs - rowsum) * scale).astype(bf16)
                ds_s[pp * n_heads + h] = ds
                d_s[h * HEAD_DIM : (h + 1) * HEAD_DIM, at] = dot(
                    qkv_s[n_heads + h, :, at], ds
                ).astype(bf16)

    def value_heads(c):
        for pp in range(2):
            at = patch(c, pp)
            for h in range(n_heads):
                lo, hi = h * HEAD_DIM, (h + 1) * HEAD_DIM
                probs = p_s[(2 * c + pp) * n_heads + h].astype(bf16)
                d_oh = do_s[h, :, pp * 128 : (pp + 1) * 128]
                d_s[cols + lo : cols + hi, at] = dot_nt(
                    qkv_s[h, :, at], ds_s[pp * n_heads + h]
                ).astype(bf16)
                d_s[2 * cols + lo : 2 * cols + hi, at] = dot_nt(d_oh, probs).astype(bf16)

    lax.fori_loop(0, 2, backward, 0)

    def piece(a, h):
        return g.at[pl.ds(((here + a) % 4 * 2 + h) * 4, 4)]

    copies = []

    def plan(src, dst, k, peer, sends, recvs):
        c = remote(src, dst, sends.at[k], recvs.at[k], peer)
        copies.append(c)
        return c

    def send(*what):
        c = plan(*what)
        c.start()
        return c

    right, left = ring(True, 1), ring(True, -1)
    c1r = plan(piece(2, 0), r1, 0, right, a_send, a_recv)
    c1l = plan(piece(2, 1), l1, 1, left, a_send, a_recv)
    c2r = plan(piece(1, 1), r2, 2, right, a_send, a_recv)
    c2l = plan(piece(3, 0), l2, 3, left, a_send, a_recv)
    for c in range(2):
        swap_ntx(c).wait_recv()
        swap_ox(c).wait_recv()
        swap_dx(c).wait_recv()

    def weight_grads(i, _):
        a = (here + jnp.where(i < 2, 2 - i, 5 - i - (i // 3) * 2)) % 4
        at = pl.ds(pl.multiple_of((core * 4 + a) * 8 * PAD, 8 * PAD), 8 * PAD)
        at_x = pl.ds(pl.multiple_of(a * 8 * PAD, 8 * PAD), 8 * PAD)
        to = pl.ds(a * 8, 8)
        part = dot_nt(n_t[at, :], d_s[...]) + dot_nt(nt_x[at_x, :], d_x[...])
        g[to, :, : 3 * cols] = part.reshape(8, PAD, 3 * cols).astype(bf16)

        @pl.when(i == 0)
        def _():
            swap_dyx(0).wait_recv()
            swap_dyx(1).wait_recv()

        part = dot_nt(dy_t[at, :], o_s[...]) + dot_nt(dyt_x[at_x, :], o_x[...])
        g[to, :, 3 * cols :] = part.reshape(8, PAD, cols).astype(bf16)

        @pl.when(i == 0)
        def _():
            c1r.start()
            c1l.start()

        @pl.when(i == 1)
        def _():
            c2r.start()

        @pl.when(i == 2)
        def _():
            c2l.start()

        return 0

    lax.fori_loop(0, 4, weight_grads, 0)

    def finish(p, _):
        @pl.when(p % 2 == 0)
        def _():
            swap_dn(p // 2).wait_recv()

        at = pl.ds(pl.multiple_of(p * 128 + kept * 64, 64), 64)
        dn = dn_s[p, kept].astype(f32) + dno_s[p].astype(f32)
        xhat, rstd = norm_terms(x_s[at, :].astype(f32))
        gs = dn * gain_row
        back = rstd * (
            gs
            - jnp.mean(gs, axis=-1, keepdims=True)
            - xhat * jnp.mean(gs * xhat, axis=-1, keepdims=True)
        )
        x_v[pl.ds(pl.multiple_of(p * 64, 64), 64), :] = (
            dy_s[at, :].astype(f32) + back
        ).astype(bf16)
        return 0

    lax.fori_loop(0, 4, finish, 0)

    def to_home(j, _):
        t = iota((128, half), 0) + j * 128
        source = (t % 8 // 2) * 64 + 2 * (t // 8) + t % 2
        pick = (iota((128, half), 1) == source).astype(bf16)
        leave[pl.ds(j * 16, 16), :, :width] = (
            dot(pick, x_v[pl.ds(0, half), :]).reshape(16, 8, width).astype(bf16)
        )
        return 0

    lax.fori_loop(0, 2, to_home, 0)

    f = lax.axis_index("frame")
    spots = FRAME // 2
    spot = f % spots
    own = core == chan

    def home_copy(k):
        q = (spot + k) % spots
        return remote(
            part(leave, q, width), d_recv.at[f], home_send.at[k], home_recv.at[f // 2],
            {"frame": kept * spots + q, "chan": core},
        )

    home_local = pltpu.make_async_copy(part(leave, spot, width), d_recv.at[f], home_own)

    def home_each(run, run_own):
        @pl.when(own)
        def _():
            run_own()

        @pl.when(jnp.logical_not(own))
        def _():
            run(home_copy(0))

        def step(k, _):
            run(home_copy(k))
            return 0

        lax.fori_loop(1, spots, step, 0)

    def pass_on(i):
        return remote(d_recv.at[i], d_recv.at[i], on_send.at[i // 2], on_recv.at[i // 2], partner)

    def landed(k, _):
        k = 2 * k + (core + chan) % 2
        for n in range(2):
            source = n * spots + (spot - k + spots) % spots
            local = jnp.logical_and(source == f, own)

            @pl.when(local)
            def _():
                home_local.wait()

            @pl.when(jnp.logical_not(local))
            def _(source=source):
                remote(
                    part(leave, 0, width), d_recv.at[source], home_send.at[0],
                    home_recv.at[source // 2], partner,
                ).wait_recv()

            pass_on(source).start()
        return 0

    def passed_on(run):
        def step(i, _):
            run(i)
            return 0

        lax.fori_loop(0, spots, step, 0)

    home_each(lambda c: c.start(), home_local.start)
    c1r.wait_recv()
    add_blocks(piece(1, 0), (piece(1, 0), r1), 4)
    c3r = send(piece(1, 0), r3, 4, right, a_send, a_recv)
    c1l.wait_recv()
    add_blocks(piece(3, 1), (piece(3, 1), l1), 4)
    c3l = send(piece(3, 1), l3, 5, left, a_send, a_recv)
    lax.fori_loop(0, 12, landed, 0)
    c2l.wait_recv()
    c3r.wait_recv()
    add_blocks(piece(0, 0), (piece(0, 0), r3, l2), 4)
    c2r.wait_recv()
    c3l.wait_recv()
    add_blocks(piece(0, 1), (piece(0, 1), r2, l3), 4)

    right, left = ring(False, 1), ring(False, -1)
    at = lambda h, d: g.at[(here * 2 + h) * 4 + (there + d) % 4]
    d1r = send(at(0, 2), br1, 0, right, b_send, b_recv)
    d1l = send(at(1, 2), bl1, 1, left, b_send, b_recv)
    d2r = send(at(1, 1), br2, 2, right, b_send, b_recv)
    d2l = send(at(0, 3), bl2, 3, left, b_send, b_recv)
    lax.fori_loop(12, spots // 2, landed, 0)
    d1r.wait_recv()
    bmr[...] = (at(0, 1)[...].astype(f32) + br1[...].astype(f32)).astype(bf16)
    d3r = send(bmr, br3, 4, right, b_send, b_recv)
    d1l.wait_recv()
    bml[...] = (at(1, 3)[...].astype(f32) + bl1[...].astype(f32)).astype(bf16)
    d3l = send(bml, bl3, 5, left, b_send, b_recv)
    d2l.wait_recv()
    d3r.wait_recv()
    u[0] = (at(0, 0)[...].astype(f32) + br3[...].astype(f32) + bl2[...].astype(f32)).astype(bf16)
    d2r.wait_recv()
    d3l.wait_recv()
    u[1] = (at(1, 0)[...].astype(f32) + br2[...].astype(f32) + bl3[...].astype(f32)).astype(bf16)

    e = remote(u.at[1 - xh], xr, x_send, x_recv, across)
    e.start()
    e.wait_recv()
    out[...] = u[xh].astype(f32) + xr[...].astype(f32)
    passed_on(lambda i: pass_on(2 * i + 1 - chan).wait_recv())

    e.wait_send()
    w_first.wait_send()
    w_second.wait_send()
    for c in copies:
        c.wait_send()
    for c in range(2):
        swap_o(c).wait_send()
        swap_dn(c).wait_send()
        swap_ox(c).wait_send()
        swap_ntx(c).wait_send()
        swap_dyx(c).wait_send()
        swap_dx(c).wait_send()
    home_each(lambda c: c.wait_send(), lambda: None)
    passed_on(lambda i: pass_on(2 * i + chan).wait_send())


def layer(clip, ids, gain, w_qkv, w_out, table):
    tokens, width = clip.shape
    cols = w_out.shape[0]
    n_heads = cols // HEAD_DIM
    each = tokens // FRAME
    vmem = pl.BlockSpec(memory_space=pltpu.VMEM)
    anywhere = pl.BlockSpec(memory_space=pl.ANY)
    wide = pltpu.VMEM((tokens, width), bf16)
    narrow = pltpu.VMEM((cols, tokens), bf16)
    piece = pltpu.VMEM((4, PAD, 4 * cols), bf16)
    block = pltpu.VMEM((PAD, 4 * cols), bf16)
    carry = pltpu.VMEM((FRAME, each, width + 128), bf16)
    dma = pltpu.SemaphoreType.DMA
    return pl.pallas_call(
        layer_kernel,
        out_shape=[
            jax.ShapeDtypeStruct((PAD, 4 * cols), f32),
            jax.ShapeDtypeStruct((FRAME, each, width), bf16),
        ],
        in_specs=[anywhere, vmem, vmem, anywhere, anywhere, anywhere],
        out_specs=[vmem, vmem],
        scratch_shapes=[
            wide,
            carry,
            carry,
            pltpu.VMEM((3 * cols, width), bf16),
            pltpu.VMEM((cols, width), bf16),
            pltpu.VMEM((cols, width), bf16),
            pltpu.VMEM(table.shape, bf16),
            wide,
            pltpu.VMEM((tokens, 128), f32),
            wide,
            pltpu.VMEM((3 * n_heads, HEAD_DIM, tokens), bf16),
            narrow,
            narrow,
            pltpu.VMEM((tokens // 128 * n_heads, 128, 128), f32),
            wide,
            pltpu.VMEM((n_heads, HEAD_DIM, tokens // 2), bf16),
            pltpu.VMEM((2 * n_heads, 128, 128), bf16),
            pltpu.VMEM((3 * cols, tokens), bf16),
            pltpu.VMEM((4, 2, 64, width), bf16),
            pltpu.VMEM((4, 64, width), bf16),
            pltpu.VMEM((FRAME * PAD, tokens), bf16),
            pltpu.VMEM((FRAME * PAD, tokens), bf16),
            pltpu.VMEM((FRAME * PAD // 2, tokens), bf16),
            pltpu.VMEM((FRAME * PAD // 2, tokens), bf16),
            pltpu.VMEM((3 * cols, tokens), bf16),
            narrow,
            pltpu.VMEM((FRAME // 2, PAD, 4 * cols), bf16),
        ]
        + [piece] * 6
        + [block] * 8
        + [pltpu.VMEM((2, PAD, 4 * cols), bf16), block]
        + [
            dma((4,)), dma, dma((2,)), dma((2,)),
            dma, dma((FRAME,)), dma((FRAME,)),
            dma, dma((FRAME // 2,)), dma((FRAME // 2,)), dma((FRAME // 2,)), dma((FRAME // 2,)),
            dma((2,)), dma((2,)), dma((2,)), dma((2,)),
            dma((2, 2)), dma((2, 2)), dma((2, 2)), dma((2, 2)), dma((6,)), dma((6,)), dma((6,)), dma((6,)), dma, dma,
        ],
        compiler_params=pltpu.CompilerParams(
            collective_id=0, has_side_effects=True, vmem_limit_bytes=VMEM_LIMIT
        ),
        name="layer",
    )(clip, ids, gain, w_qkv, w_out, table)


def settle_kernel(total, d_recv, d_qkv, d_out, d_clip):
    cols = d_out.shape[1]
    width = d_clip.shape[2]
    half = 2 * d_clip.shape[1]

    @pl.when(pl.program_id(0) == 0)
    def _():
        for i in range(3):
            d_qkv[i] = total[:ROWS, i * cols : (i + 1) * cols]
        d_out[...] = total[:ROWS, 3 * cols :]

    t = iota((half, half), 0)
    source = (t % 128 // 4) * 8 + (t % 4) * 2 + t // 128
    pick = (iota((half, half), 1) == source).astype(bf16)
    moved = dot(pick, d_recv[...].reshape(half, width))
    d_clip[...] = moved.reshape(2, 128, width).astype(bf16)


def settle(total, d_recv):
    cols = total.shape[1] // 4
    sources, each, width = d_recv.shape
    return pl.pallas_call(
        settle_kernel,
        grid=(2,),
        out_shape=[
            jax.ShapeDtypeStruct((3, ROWS, cols), f32),
            jax.ShapeDtypeStruct((ROWS, cols), f32),
            jax.ShapeDtypeStruct((2, sources * each // 2, width), bf16),
        ],
        in_specs=[
            pl.BlockSpec((PAD, 4 * cols), lambda h: (0, 0)),
            pl.BlockSpec((sources // 2, each, width), lambda h: (h, 0, 0)),
        ],
        out_specs=[
            pl.BlockSpec((3, ROWS, cols), lambda h: (0, 0, 0)),
            pl.BlockSpec((ROWS, cols), lambda h: (0, 0)),
            pl.BlockSpec((2, sources * each // 4, width), lambda h: (0, h, 0)),
        ],
        compiler_params=pltpu.CompilerParams(vmem_limit_bytes=32 * 2**20),
        name="settle",
    )(total, d_recv)


def body(clip, gain, w_qkv, w_out, old_table, target_ids):
    frames_here, patches, width = clip.shape
    cols = w_qkv.shape[2]
    tokens = frames_here * patches

    total, d_recv = layer(
        clip.reshape(tokens, width),
        target_ids,
        gain,
        w_qkv.transpose(0, 2, 1).reshape(3 * cols, width),
        w_out,
        old_table,
    )
    d_qkv, d_out, d_clip = settle(total, d_recv)
    return d_clip, d_qkv, d_out.T


def solution(mesh):
    return jax.shard_map(
        body,
        mesh=mesh,
        in_specs=(
            P("frame", None, None),
            P(),
            P(None, None, "chan"),
            P("chan", None),
            P(),
            P("frame", None),
        ),
        out_specs=(P("frame", None, None), P(None, "frame", "chan"), P("chan", "frame")),
        check_vma=False,
    )
```
